32 devices in a mesh: wide: 8 (over y, x, core), narrow: 4 (over z).
Axes of the slice: x: 2, y: 2, z: 4, core: 2. Of those that a mesh axis runs over, the one named last changes fastest.
Arguments:
- tokens: bfloat16 [16, 1024, 2048], P('wide', 'narrow'), may hold values from -6 to 6
- active: int32 [16, 1024], P('wide'), may hold values from 0 to 1, as said below
- cotangent: bfloat16 [16, 1024, 2048], P('wide', 'narrow'), may hold values from -6 to 6
- gain_rows: float32 [2, 2048], P(None, ('wide', 'narrow')), may hold values from 0.5 to 1.5
- w_qkv: float32 [2048, 3072], P(('wide', 'narrow')), may hold values from -0.125 to 0.125
- w_out: float32 [2048, 2048], P(('wide', 'narrow')), may hold values from -0.75 to 0.75
- w_gateup: float32 [2048, 11264], P(('wide', 'narrow')), may hold values from -0.125 to 0.125
- w_down: float32 [5632, 2048], P(('wide', 'narrow')), may hold values from -0.078125 to 0.078125
- moment_gains: float32 [2, 2048], P(None, ('wide', 'narrow')), may hold values from -192 to 192
- moment_qkv: float32 [2048, 3072], P(('wide', 'narrow')), may hold values from -192 to 192
- moment_out: float32 [2048, 2048], P(('wide', 'narrow')), may hold values from -192 to 192
- moment_gateup: float32 [2048, 11264], P(('wide', 'narrow')), may hold values from -192 to 192
- moment_down: float32 [5632, 2048], P(('wide', 'narrow')), may hold values from -192 to 192
- average_gains: float32 [2, 2048], P(None, ('wide', 'narrow')), may hold values from 0.5 to 1.5
- average_qkv: float32 [2048, 3072], P(('wide', 'narrow')), may hold values from -0.125 to 0.125
- average_out: float32 [2048, 2048], P(('wide', 'narrow')), may hold values from -0.75 to 0.75
- average_gateup: float32 [2048, 11264], P(('wide', 'narrow')), may hold values from -0.125 to 0.125
- average_down: float32 [5632, 2048], P(('wide', 'narrow')), may hold values from -0.078125 to 0.078125
Outputs:
- layer_out: bfloat16 [16, 1024, 2048], P('wide', 'narrow')
- grad_tokens: bfloat16 [16, 1024, 2048], P('wide', 'narrow')
- grad_gains: float32 [2, 2048], P(None, ('wide', 'narrow'))
- grad_qkv: float32 [2048, 3072], P(('wide', 'narrow'))
- grad_out: float32 [2048, 2048], P(('wide', 'narrow'))
- grad_gateup: float32 [2048, 11264], P(('wide', 'narrow'))
- grad_down: float32 [5632, 2048], P(('wide', 'narrow'))
- new_gains: float32 [2, 2048], P(None, ('wide', 'narrow'))
- new_qkv: float32 [2048, 3072], P(('wide', 'narrow'))
- new_out: float32 [2048, 2048], P(('wide', 'narrow'))
- new_gateup: float32 [2048, 11264], P(('wide', 'narrow'))
- new_down: float32 [5632, 2048], P(('wide', 'narrow'))
- next_moment_gains: float32 [2, 2048], P(None, ('wide', 'narrow'))
- next_moment_qkv: float32 [2048, 3072], P(('wide', 'narrow'))
- next_moment_out: float32 [2048, 2048], P(('wide', 'narrow'))
- next_moment_gateup: float32 [2048, 11264], P(('wide', 'narrow'))
- next_moment_down: float32 [5632, 2048], P(('wide', 'narrow'))
- next_average_gains: float32 [2, 2048], P(None, ('wide', 'narrow'))
- next_average_qkv: float32 [2048, 3072], P(('wide', 'narrow'))
- next_average_out: float32 [2048, 2048], P(('wide', 'narrow'))
- next_average_gateup: float32 [2048, 11264], P(('wide', 'narrow'))
- next_average_down: float32 [5632, 2048], P(('wide', 'narrow'))
The draws below stay inside these ranges and needn't reach their ends.
Inputs may be any that keep to these rules, and one draw needn't show every extreme that they name: `active`: 1 marks a token that the layer processes, 0 one that keeps its input; each sequence has its own share of skipped tokens.
All inputs are finite; a program needn't handle non-finite values.
Results may differ from the reference program's by a relative error of at most 0.015.
Values may be sent and summed in bfloat16 or wider, within the bound.
A program may use at most 448 MiB of HBM per device.

```python
import jax
import jax.numpy as jnp
from jax import lax

D = 2048
HEADS = 16
KV_HEADS = 4
HEAD_DIM = 128
FF = 5632
LENGTH = 1024
SEQS = 16
QKV_COLS = 3072


def draw_active(key, part):
    key = jax.random.fold_in(key, 11)
    rate_key, token_key = jax.random.split(key)
    skip_rates = jax.random.randint(rate_key, (SEQS, 1), 300, 800)
    token_draws = jax.random.randint(token_key, (SEQS, LENGTH), 0, 1000)
    return (token_draws >= skip_rates).astype(jnp.int32)


def level_of(own_key, extent, cuts, low, high):
    def one(position, parts):
        steps = jax.random.uniform(jax.random.fold_in(jax.random.fold_in(own_key, 6), position), (parts,), jnp.float32, low / len(cuts), high / len(cuts))
        return jnp.repeat(jnp.exp(steps), extent[position] // parts).reshape((-1,) + (1,) * (len(extent) - position - 1))

    factor_of = one(*cuts[0])
    for cut in cuts[1:]:
        factor_of = factor_of * one(*cut)
    return factor_of


def noise(rng, extent, spread, limit, cuts=(), kind=jnp.bfloat16):
    gain = level_of(rng, extent, cuts, -0.22, 0.18) if cuts else 1.0
    values = jax.random.normal(rng, extent, jnp.float32) * spread * gain
    return jnp.minimum(jnp.maximum(values, -limit), limit).astype(kind)


def setup_inputs(seed: int = 0) -> dict:
    seeds = jax.random.split(jax.random.key(seed), 19)
    return {
        "tokens": noise(seeds[0], (SEQS, LENGTH, D), 1.0, 6.0, ((0, 8), (1, 4))),
        "active": draw_active(jax.random.fold_in(seeds[18], 71), 0),
        "cotangent": noise(seeds[2], (SEQS, LENGTH, D), 1.0, 6.0, ((0, 8), (1, 4))),
        "gain_rows": jnp.clip(1.0 + 0.1 * jax.random.normal(seeds[3], (2, D), jnp.float32), 0.5, 1.5),
        "w_qkv": noise(seeds[4], (D, QKV_COLS), D ** -0.5, 0.125, ((0, 32),), jnp.float32),
        "w_out": noise(seeds[5], (D, D), (D * 32 // LENGTH) ** -0.5, 0.75, ((0, 32),), jnp.float32),
        "w_gateup": noise(seeds[6], (D, 2 * FF), D ** -0.5, 0.125, ((0, 32),), jnp.float32),
        "w_down": noise(seeds[7], (FF, D), FF ** -0.5, 0.078125, ((0, 32),), jnp.float32),
        "moment_gains": noise(seeds[8], (2, D), ((SEQS * LENGTH) ** 0.5 / 4), 192.0, ((1, 32),), jnp.float32),
        "moment_qkv": noise(seeds[9], (D, QKV_COLS), ((SEQS * LENGTH) ** 0.5 / 4), 192.0, ((0, 32),), jnp.float32),
        "moment_out": noise(seeds[10], (D, D), ((SEQS * LENGTH) ** 0.5 / 4), 192.0, ((0, 32),), jnp.float32),
        "moment_gateup": noise(seeds[11], (D, 2 * FF), ((SEQS * LENGTH) ** 0.5 / 4), 192.0, ((0, 32),), jnp.float32),
        "moment_down": noise(seeds[12], (FF, D), ((SEQS * LENGTH) ** 0.5 / 4), 192.0, ((0, 32),), jnp.float32),
        "average_gains": jnp.clip(1.0 + 0.1 * jax.random.normal(seeds[13], (2, D), jnp.float32), 0.5, 1.5),
        "average_qkv": noise(seeds[14], (D, QKV_COLS), D ** -0.5, 0.125, ((0, 32),), jnp.float32),
        "average_out": noise(seeds[15], (D, D), (D * 32 // LENGTH) ** -0.5, 0.75, ((0, 32),), jnp.float32),
        "average_gateup": noise(seeds[16], (D, 2 * FF), D ** -0.5, 0.125, ((0, 32),), jnp.float32),
        "average_down": noise(seeds[17], (FF, D), FF ** -0.5, 0.078125, ((0, 32),), jnp.float32),
    }


@jax.custom_vjp
def low(v):
    return lax.optimization_barrier(v.astype(jnp.bfloat16)).astype(jnp.float32)

@jax.custom_vjp
def low_back(v):
    return v

def low_keep(v):
    return (low(v), None)

def low_pass(kept, grad):
    return (grad,)

def back_keep(v):
    return (v, None)

def back_low(kept, grad):
    return (low(grad),)
low.defvjp(low_keep, low_pass)
low_back.defvjp(back_keep, back_low)
EPSILON = 1e-05
MOMENTUM = 0.5
AVERAGING = 0.5
STEP_RATE = 0.0003
HIGHEST = lax.Precision.HIGHEST

def rotary_tables(positions):
    half_dim = HEAD_DIM // 2
    frequency = jnp.power(10000.0, -2.0 * jnp.arange(half_dim, dtype=jnp.float32) / HEAD_DIM)
    angles = positions[:, None] * frequency[None, :]
    return (jnp.cos(angles)[:, None, :], jnp.sin(angles)[:, None, :])

def rotate_heads(head_values, cosine_table, sine_table):
    half_dim = head_values.shape[-1] // 2
    first_half = head_values[..., :half_dim]
    second_half = head_values[..., half_dim:]
    return jnp.concatenate([first_half * cosine_table - second_half * sine_table, second_half * cosine_table + first_half * sine_table], axis=-1)

def rms_scale(values_in, gain_row):
    return values_in * lax.rsqrt(lax.optimization_barrier(jnp.mean(values_in * values_in, axis=-1, keepdims=True)) + EPSILON) * gain_row

def layer_forward(inputs, gain_rows, w_qkv, w_out, w_gateup, w_down, active_row):
    length = inputs.shape[0]
    kv_width = KV_HEADS * HEAD_DIM
    group_size = HEADS // KV_HEADS
    gains_low = low(gain_rows)
    qkv_low = low(w_qkv)
    out_low = low(w_out)
    gateup_low = low(w_gateup)
    down_low = low(w_down)
    normed = low(rms_scale(inputs, gains_low[0]))
    projected = low_back(jnp.dot(normed, qkv_low, precision=HIGHEST))
    cosine_table, sine_table = rotary_tables(jnp.arange(length, dtype=jnp.float32))
    queries = low(rotate_heads(projected[:, :D].reshape(length, HEADS, HEAD_DIM), cosine_table, sine_table))
    key_heads = low(rotate_heads(projected[:, D:D + kv_width].reshape(length, KV_HEADS, HEAD_DIM), cosine_table, sine_table))
    value_heads = low(projected[:, D + kv_width:].reshape(length, KV_HEADS, HEAD_DIM))
    grouped = queries.reshape(length, KV_HEADS, group_size, HEAD_DIM)
    raw_scores = low_back(jnp.einsum('qkgd,skd->kgqs', grouped, key_heads, precision=HIGHEST) * HEAD_DIM ** (-0.5))
    places = jnp.arange(length)
    allowed = (places[None, :] <= places[:, None]) & ((active_row[None, :] == 1) | (places[None, :] == places[:, None]))
    masked_scores = jnp.where(allowed, raw_scores, -1e+30)
    soft_probs = jax.nn.softmax(masked_scores, axis=-1)
    mixed_values = jnp.einsum('kgqs,skd->qkgd', low(soft_probs), value_heads, precision=HIGHEST)
    attended = low_back(low(mixed_values.reshape(length, D)))
    branch = low_back(jnp.dot(attended, out_low, precision=HIGHEST))
    live_rows = active_row.astype(jnp.float32)[:, None]
    middle = inputs + live_rows * branch
    normed_mid = low(rms_scale(middle, gains_low[1]))
    gate_up = low_back(jnp.dot(normed_mid, gateup_low, precision=HIGHEST))
    hidden = low(jax.nn.silu(gate_up[:, :FF]) * gate_up[:, FF:])
    down_proj = low_back(jnp.dot(hidden, down_low, precision=HIGHEST))
    return middle + live_rows * down_proj

def advance_state(weight, moment, average, gradient):
    moment_next = MOMENTUM * moment + gradient
    weight_next = weight - STEP_RATE * (gradient + MOMENTUM * moment_next)
    average_next = AVERAGING * average + (1.0 - AVERAGING) * weight_next
    return (weight_next, moment_next, average_next)

def reference(tokens, active, cotangent, gain_rows, w_qkv, w_out, w_gateup, w_down, moment_gains, moment_qkv, moment_out, moment_gateup, moment_down, average_gains, average_qkv, average_out, average_gateup, average_down):
    weights = (gain_rows, w_qkv, w_out, w_gateup, w_down)

    def one_sequence(carried, sequence_item):
        inputs, mask_row, upstream = sequence_item

        def closed(layer_in, *parameters):
            return layer_forward(layer_in, *parameters, mask_row)
        result, pullback = jax.vjp(closed, inputs.astype(jnp.float32), *weights)
        gradients = pullback(upstream.astype(jnp.float32))
        carried = tuple((total_grad + new_grad for total_grad, new_grad in zip(carried, gradients[1:])))
        return (carried, (result.astype(jnp.bfloat16), gradients[0].astype(jnp.bfloat16)))
    start_grads = tuple((jnp.zeros_like(weight) for weight in weights))
    summed, outputs_pair = lax.scan(one_sequence, start_grads, (tokens, active, cotangent))
    layer_out, grad_tokens = outputs_pair
    grad_gains, grad_qkv, grad_out, grad_gateup, grad_down = summed
    state_gains = advance_state(gain_rows, moment_gains, average_gains, grad_gains)
    state_qkv = advance_state(w_qkv, moment_qkv, average_qkv, grad_qkv)
    state_out = advance_state(w_out, moment_out, average_out, grad_out)
    state_gateup = advance_state(w_gateup, moment_gateup, average_gateup, grad_gateup)
    state_down = advance_state(w_down, moment_down, average_down, grad_down)
    return (layer_out, grad_tokens, grad_gains, grad_qkv, grad_out, grad_gateup, grad_down, state_gains[0], state_qkv[0], state_out[0], state_gateup[0], state_down[0], state_gains[1], state_qkv[1], state_out[1], state_gateup[1], state_down[1], state_gains[2], state_qkv[2], state_out[2], state_gateup[2], state_down[2])
```

```python
import functools

import jax
import jax.numpy as jnp
from jax import lax
from jax.experimental import pallas as pl
from jax.experimental.pallas import tpu as pltpu
from jax.sharding import PartitionSpec as P

HEADS = 16
KV_HEADS = 4
HEAD_DIM = 128
GROUP = HEADS // KV_HEADS
FF = 5632


EPSILON = 1e-05
MOMENTUM = 0.5
AVERAGING = 0.5
STEP_RATE = 0.0003

MESH = pl.DeviceIdType.MESH
MESH_AXES = ("wide", "narrow")
SCORE_SCALE = HEAD_DIM ** (-0.5)
LOG2_E = 1.4426950408889634
MASKED = -1e30


def dot_nt(a, b):
    return lax.dot_general(a, b, (((1,), (1,)), ((), ())), preferred_element_type=jnp.float32)


def dot_tn(a, b):
    return lax.dot_general(a, b, (((0,), (0,)), ((), ())), preferred_element_type=jnp.float32)


def fill_bias(key_code, query_code, query_base, bias):
    rows = query_code.shape[1]

    def chunk(r, carry):
        at = pl.ds(pl.multiple_of(r * rows, 128), rows)
        code = key_code[at, :]
        seen = (code <= query_code[...]) & (code >= query_base[...])
        bias[at, :] = jnp.where(seen, 0.0, MASKED)
        return carry

    lax.fori_loop(0, key_code.shape[0] // rows, chunk, 0)


def attend_kernel(q_ref, k_ref, v_ref, key_code, query_code, query_base, o_ref, total_ref, bias):
    rows = q_ref.shape[0]
    blocks = k_ref.shape[0] // rows

    @pl.when(pl.program_id(0) == 0)
    def _():
        fill_bias(key_code, query_code, query_base, bias)

    def chunk(r, carry):
        at = pl.ds(pl.multiple_of(r * rows, 128), rows)
        keys, values, hidden = k_ref[at, :], v_ref[at, :], bias[at, :]
        out = []
        for h in range(GROUP):
            peak, total, mixed = carry[h]
            query = q_ref[:, h * HEAD_DIM : (h + 1) * HEAD_DIM]
            scores = dot_nt(keys, query) * (SCORE_SCALE * LOG2_E) + hidden
            new_peak = jnp.maximum(peak, jnp.max(scores, axis=0, keepdims=True))
            weights = jnp.exp2(scores - new_peak)
            shrink = jnp.exp2(peak - new_peak)
            total = total * shrink + jnp.sum(weights, axis=0, keepdims=True)
            mixed = mixed * shrink + dot_tn(values, weights.astype(jnp.bfloat16))
            out.append((new_peak, total, mixed))
        return tuple(out)

    start = (
        jnp.full((1, rows), MASKED, jnp.float32),
        jnp.zeros((1, rows), jnp.float32),
        jnp.zeros((HEAD_DIM, rows), jnp.float32),
    )
    done = lax.fori_loop(0, blocks, chunk, (start,) * GROUP)
    for h, (peak, total, mixed) in enumerate(done):
        o_ref[:, h * HEAD_DIM : (h + 1) * HEAD_DIM] = (mixed / total).T.astype(jnp.bfloat16)
        total_ref[0, h : h + 1, :] = peak + jnp.log2(total)


def attend(query, kv, key_code, query_code, query_base):
    rows, width = query.shape
    length = kv.shape[0]
    whole = lambda g: (0, 0)
    return pl.pallas_call(
        attend_kernel,
        grid=(KV_HEADS,),
        in_specs=[
            pl.BlockSpec((rows, GROUP * HEAD_DIM), lambda g: (0, g)),
            pl.BlockSpec((length, HEAD_DIM), lambda g: (0, g)),
            pl.BlockSpec((length, HEAD_DIM), lambda g: (0, KV_HEADS + g)),
            pl.BlockSpec((length, 1), whole),
            pl.BlockSpec((1, rows), whole),
            pl.BlockSpec((1, rows), whole),
        ],
        out_specs=(
            pl.BlockSpec((rows, GROUP * HEAD_DIM), lambda g: (0, g)),
            pl.BlockSpec((1, GROUP, rows), lambda g: (g, 0, 0)),
        ),
        out_shape=(
            jax.ShapeDtypeStruct((rows, width), jnp.bfloat16),
            jax.ShapeDtypeStruct((KV_HEADS, GROUP, rows), jnp.float32),
        ),
        scratch_shapes=[pltpu.VMEM((length, rows), jnp.float32)],
        compiler_params=pltpu.CompilerParams(vmem_limit_bytes=48 * 1024 * 1024),
        cost_estimate=pl.CostEstimate(
            flops=4 * rows * length * width, bytes_accessed=8 * rows * width, transcendentals=HEADS * rows * length
        ),
        name="attend",
    )(query, kv, kv, key_code, query_code, query_base)


def attend_back_kernel(
    q_ref, k_ref, v_ref, do_ref, total_ref, inner_ref, key_code, query_code, query_base,
    dq_ref, dk_ref, dv_ref, bias, dk_sum, dv_sum, dq_sum,
):
    rows = q_ref.shape[0]
    blocks = k_ref.shape[0] // rows

    @pl.when(pl.program_id(0) == 0)
    def _():
        fill_bias(key_code, query_code, query_base, bias)

    for h in range(GROUP):
        lanes = slice(h * HEAD_DIM, (h + 1) * HEAD_DIM)
        query = q_ref[:, lanes]
        grad = do_ref[:, lanes]
        total = total_ref[0, h : h + 1, :]
        inner = inner_ref[0, h : h + 1, :]
        dq_sum[...] = jnp.zeros_like(dq_sum)

        def chunk(r, carry):
            at = pl.ds(pl.multiple_of(r * rows, 128), rows)
            keys = k_ref[at, :]
            scores = dot_nt(keys, query) * (SCORE_SCALE * LOG2_E) + bias[at, :]
            weights = jnp.exp2(scores - total)
            grad_weights = dot_nt(v_ref[at, :], grad)
            grad_scores = (weights * (grad_weights - inner)).astype(jnp.bfloat16)
            dv = jnp.dot(weights.astype(jnp.bfloat16), grad, preferred_element_type=jnp.float32)
            dk = jnp.dot(grad_scores, query, preferred_element_type=jnp.float32)
            if h == 0:
                dv_sum[at, :] = dv
                dk_sum[at, :] = dk
            elif h < GROUP - 1:
                dv_sum[at, :] += dv
                dk_sum[at, :] += dk
            else:
                dv_ref[at, :] = (dv_sum[at, :] + dv).astype(dv_ref.dtype)
                dk_ref[at, :] = ((dk_sum[at, :] + dk) * SCORE_SCALE).astype(dk_ref.dtype)
            dq_sum[...] += dot_tn(keys, grad_scores)
            return carry

        lax.fori_loop(0, blocks, chunk, 0)
        dq_ref[:, lanes] = dq_sum[...].T * SCORE_SCALE


def attend_back(query, kv, grad, total, inner, key_code, query_code, query_base):
    rows, width = query.shape
    length = kv.shape[0]
    whole = lambda g: (0, 0)
    heads = pl.BlockSpec((rows, GROUP * HEAD_DIM), lambda g: (0, g))
    kv_heads = pl.BlockSpec((length, HEAD_DIM), lambda g: (0, g))
    values = pl.BlockSpec((length, HEAD_DIM), lambda g: (0, KV_HEADS + g))
    per_head = pl.BlockSpec((1, GROUP, rows), lambda g: (g, 0, 0))
    return pl.pallas_call(
        attend_back_kernel,
        grid=(KV_HEADS,),
        in_specs=[
            heads, kv_heads, values, heads, per_head, per_head,
            pl.BlockSpec((length, 1), whole),
            pl.BlockSpec((1, rows), whole),
            pl.BlockSpec((1, rows), whole),
        ],
        out_specs=(heads, kv_heads, kv_heads),
        out_shape=(
            jax.ShapeDtypeStruct((rows, width), jnp.float32),
            jax.ShapeDtypeStruct((length, KV_HEADS * HEAD_DIM), jnp.float32),
            jax.ShapeDtypeStruct((length, KV_HEADS * HEAD_DIM), jnp.float32),
        ),
        scratch_shapes=[
            pltpu.VMEM((length, rows), jnp.float32),
            pltpu.VMEM((length, HEAD_DIM), jnp.float32),
            pltpu.VMEM((length, HEAD_DIM), jnp.float32),
            pltpu.VMEM((HEAD_DIM, rows), jnp.float32),
        ],
        compiler_params=pltpu.CompilerParams(vmem_limit_bytes=48 * 1024 * 1024),
        cost_estimate=pl.CostEstimate(
            flops=10 * rows * length * width, bytes_accessed=16 * rows * width, transcendentals=HEADS * rows * length
        ),
        name="attend_back",
    )(query, kv, kv, grad, total, inner, key_code, query_code, query_base)


def gather_kernel(n, qkv_ref, out_ref, ext_ref, trade_ref, qkv_all, out_line, ext_all, came, *sems):
    wide = lax.axis_index("wide")
    z = lax.axis_index("narrow")
    t, core = wide // 2, wide % 2
    send_sems, recv_sems, local_sems = sems
    t_x, t_y, t_d = t ^ 1, t ^ 2, t ^ 3

    def device(place, c=None, along=None):
        return (place * 2 + (core if c is None else c), z if along is None else along)

    by_x, by_y, by_d, sibling = device(t_x), device(t_y), device(t_d), device(t, 1 - core)

    barrier = pltpu.get_barrier_semaphore()
    for other in (by_x, by_y, by_d, sibling):
        pl.semaphore_signal(barrier, inc=1, device_id=other, device_id_type=MESH)

    @pl.when(z > 0)
    def _():
        pl.semaphore_signal(barrier, inc=1, device_id=device(t, along=z - 1), device_id_type=MESH)

    @pl.when(z < n - 1)
    def _():
        pl.semaphore_signal(barrier, inc=1, device_id=device(t, along=z + 1), device_id_type=MESH)

    peers = 4 + (z > 0).astype(jnp.int32) + (z < n - 1).astype(jnp.int32)
    pl.semaphore_wait(barrier, peers)

    count = [0]
    started = []

    def copy(src, dst, to):
        k = count[0]
        count[0] += 1
        return pltpu.make_async_remote_copy(
            src_ref=src, dst_ref=dst, send_sem=send_sems.at[k], recv_sem=recv_sems.at[k],
            device_id=to, device_id_type=MESH,
        )

    def go(moves, when=None):
        if when is None:
            for m in moves:
                m.start()
        else:
            @pl.when(when)
            def _():
                for m in moves:
                    m.start()
        started.append((moves, when))

    def arrive(moves, when=None):
        if when is None:
            for m in moves:
                m.wait_recv()
        else:
            @pl.when(when)
            def _():
                for m in moves:
                    m.wait_recv()

    local = []

    def place(src, dst):
        c = pltpu.make_async_copy(src, dst, local_sems.at[len(local)])
        c.start()
        local.append(c)

    place(qkv_ref, qkv_all.at[t, core, z])
    place(ext_ref, ext_all.at[t, core, z])
    place(out_ref, out_line.at[z])
    place(trade_ref.at[t], came.at[t])
    class Line:
        def __init__(self, view, own=None):
            self.view, self.own = view, own
            self.up, self.down = {}, {}

        def send(self, step):
            zz = z - (step - 1)
            block = self.view(jnp.maximum(zz, 0))
            first = self.own if step == 1 and self.own is not None else None
            up = copy(block if first is None else first, block, device(t, along=jnp.minimum(z + 1, n - 1)))
            self.up[step] = up
            go([up], (zz >= 0) & (z < n - 1))
            zz = z + (step - 1)
            block = self.view(jnp.minimum(zz, n - 1))
            down = copy(block if first is None else first, block, device(t, along=jnp.maximum(z - 1, 0)))
            self.down[step] = down
            go([down], (zz <= n - 1) & (z > 0))

        def take(self, step):
            arrive([self.up[step]], z - step >= 0)
            arrive([self.down[step]], z + step <= n - 1)

    def same(ref, to):
        return copy(ref, ref, to)

    qa, qb, qc = pl.ds(0, 1152), pl.ds(1152, 1152), pl.ds(2304, 768)
    lines = [
        Line(lambda zz, cols=cols: qkv_all.at[t, core, zz, :, cols], qkv_ref.at[:, cols])
        for cols in (qa, qb)
    ]
    line_ext = Line(lambda zz: ext_all.at[t, core, zz], ext_ref)
    line_out = Line(lambda zz: out_line.at[zz], out_ref)
    line_c = Line(lambda zz: qkv_all.at[:, core, zz, :, qc])

    c_x = copy(qkv_ref.at[:, qc], qkv_all.at[t, core, z, :, qc], by_x)
    trade = [copy(trade_ref.at[p], came.at[t], to) for p, to in ((t_x, by_x), (t_y, by_y), (t_d, by_d))]
    for line in lines + [line_ext]:
        line.send(1)
    go([c_x])
    for step in range(1, n):
        for line in lines + [line_ext]:
            line.take(step)
            if step < n - 1:
                line.send(step + 1)
        if step == 1:
            arrive([c_x])
            c_y = [
                copy(qkv_ref.at[:, qc], qkv_all.at[t, core, z, :, qc], by_y),
                same(qkv_all.at[t_x, core, z, :, qc], by_y),
            ]
            go(c_y)
            go(trade[:2])
        if step == 2:
            arrive(c_y)
            for c in local:
                c.wait()
            line_c.send(1)
            go(trade[2:])
    a_y = same(qkv_all.at[t, core, :, :, qa], by_y)
    b_x = same(qkv_all.at[t, core, :, :, qb], by_x)
    e_x = same(ext_all.at[t, core], by_x)
    go([a_y, b_x, e_x])
    own = [same(qkv_all.at[t, core, :, :, pl.ds(0, 2304)], sibling), same(ext_all.at[t, core], sibling)]
    go(own)
    line_c.take(1)
    line_c.send(2)
    arrive([a_y])
    a_x = [same(qkv_all.at[p, core, :, :, qa], by_x) for p in (t, t_y)]
    go(a_x)
    arrive([b_x])
    b_y = [same(qkv_all.at[p, core, :, :, qb], by_y) for p in (t, t_x)]
    go(b_y)
    arrive([e_x])
    e_y = [same(ext_all.at[p, core], by_y) for p in (t, t_x)]
    go(e_y)
    near = [
        same(qkv_all.at[t_y, core, :, :, qa], sibling),
        same(qkv_all.at[t_x, core, :, :, qb], sibling),
        same(ext_all.at[t_x, core], sibling),
    ]
    go(near)
    line_c.take(2)
    line_c.send(3)
    line_out.send(1)
    arrive(e_y)
    far_e = [same(ext_all.at[p, core], sibling) for p in (t_y, t_d)]
    go(far_e)
    line_c.take(3)
    c_all = same(qkv_all.at[:, core, :, :, qc], sibling)
    go([c_all])
    for step in range(1, n):
        line_out.take(step)
        if step < n - 1:
            line_out.send(step + 1)
    arrive(a_x)
    far_a = [same(qkv_all.at[p, core, :, :, qa], sibling) for p in (t_x, t_d)]
    go(far_a)
    arrive(b_y)
    far_b = [same(qkv_all.at[p, core, :, :, qb], sibling) for p in (t_y, t_d)]
    go(far_b)
    arrive(trade)
    arrive(own + near + far_e + [c_all] + far_a + far_b)
    for moves, when in started:
        if when is None:
            for m in moves:
                m.wait_send()
        else:
            @pl.when(when)
            def _(moves=moves):
                for m in moves:
                    m.wait_send()


COPIES = 80


def gather_first(qkv, out, ext, trade, planes, n):
    any_spec = pl.BlockSpec(memory_space=pl.ANY)
    rows = qkv.shape[0]
    low = jnp.bfloat16
    return pl.pallas_call(
        functools.partial(gather_kernel, n),
        out_shape=(
            jax.ShapeDtypeStruct((planes, 2, n, rows, qkv.shape[1]), low),
            jax.ShapeDtypeStruct((n, rows, out.shape[1]), low),
            jax.ShapeDtypeStruct((planes, 2, n) + ext.shape, low),
            jax.ShapeDtypeStruct(trade.shape, low),
        ),
        in_specs=[pl.BlockSpec(memory_space=pltpu.VMEM)] * 4,
        out_specs=(any_spec,) * 4,
        scratch_shapes=[
            pltpu.SemaphoreType.DMA((COPIES,)),
            pltpu.SemaphoreType.DMA((COPIES,)),
            pltpu.SemaphoreType.DMA((4,)),
        ],
        compiler_params=pltpu.CompilerParams(collective_id=0, has_side_effects=True),
        name="gather_first",
    )(qkv, out, ext, trade)


def rotary_tables(positions):
    half_dim = HEAD_DIM // 2
    frequency = jnp.power(10000.0, -2.0 * jnp.arange(half_dim, dtype=jnp.float32) / HEAD_DIM)
    angles = positions[:, None] * frequency[None, :]
    return (jnp.cos(angles)[:, None, :], jnp.sin(angles)[:, None, :])


def rotate_heads(values, cosine_table, sine_table):
    half_dim = HEAD_DIM // 2
    cosine, sine = cosine_table[:, 0], sine_table[:, 0]
    cosine = jnp.concatenate([cosine, cosine], axis=1)
    sine = jnp.concatenate([-sine, sine], axis=1)
    done = []
    for start in range(0, values.shape[1], HEAD_DIM):
        head = values[:, start : start + HEAD_DIM]
        done.append(head * cosine + jnp.roll(head, half_dim, axis=1) * sine)
    return jnp.concatenate(done, axis=1)


def norm_forward(values_in, gain_row):
    inverse = lax.rsqrt(jnp.mean(values_in * values_in, axis=-1, keepdims=True) + EPSILON)
    return (values_in * inverse * gain_row, inverse)


def norm_backward(values_in, inverse, gain_row, incoming):
    scaled_grad = incoming * gain_row
    return inverse * scaled_grad - values_in * inverse * inverse * inverse * jnp.mean(
        scaled_grad * values_in, axis=-1, keepdims=True
    )


def advance_state(weight, moment, average, gradient):
    moment_next = MOMENTUM * moment + gradient
    weight_next = weight - STEP_RATE * (gradient + MOMENTUM * moment_next)
    average_next = AVERAGING * average + (1.0 - AVERAGING) * weight_next
    return (weight_next, moment_next, average_next)


class Links:
    def __init__(self):
        self.wide = lax.axis_size("wide")
        self.n = lax.axis_size("narrow")
        self.planes = self.wide // 2
        self.wide_at = lax.axis_index("wide")
        self.z_at = lax.axis_index("narrow")
        self.t_at = self.wide_at // 2
        self.core_at = self.wide_at % 2
        self.bits = [1 << k for k in range(self.planes.bit_length() - 1)]
        per_chip = 2 * self.n
        self.same_chip = [[t * per_chip + j for j in range(per_chip)] for t in range(self.planes)]
        self.same_plane = [
            [t * per_chip + j for t in range(self.planes)] for j in range(per_chip)
        ]

    def swap(self, values, flip):
        pairs = [(i, i ^ (flip * self.n)) for i in range(self.wide * self.n)]
        return lax.ppermute(values, MESH_AXES, pairs)

    def shift(self, values, step):
        pairs = [
            (w * self.n + z, w * self.n + z + step)
            for w in range(self.wide)
            for z in range(self.n)
            if 0 <= z + step < self.n
        ]
        return lax.ppermute(values, MESH_AXES, pairs)

    def column_cuts(self, cols):
        lanes = cols // 128
        count = len(self.bits)
        edges = [128 * (lanes * k // count) for k in range(count + 1)]
        orders = [self.bits[k:] + self.bits[:k] for k in range(count)]
        return list(zip(edges[:-1], edges[1:], orders))

    def gather_planes(self, line):
        rows, cols = line.shape
        whole = jnp.zeros((self.wide, rows, cols), line.dtype)
        for low, high, order in self.column_cuts(cols):
            held = {0: line[:, low:high]}
            for bit in order:
                held.update({d | bit: self.swap(v, 2 * bit) for d, v in list(held.items())})
            for d, v in held.items():
                for flip, piece in ((2 * d, v), (2 * d + 1, self.swap(v, 1))):
                    whole = lax.dynamic_update_slice(whole, piece[None], (self.wide_at ^ flip, 0, low))
        return whole.reshape(self.wide * rows, cols)

    def scatter_core(self, term):
        mine = lax.dynamic_index_in_dim(term, self.core_at, 1, keepdims=False)
        other = lax.dynamic_index_in_dim(term, 1 - self.core_at, 1, keepdims=False)
        got = self.swap(other, 1)
        return (mine.astype(jnp.float32) + got.astype(jnp.float32)).astype(jnp.bfloat16)

    def scatter_rows(self, term):
        rows, cols = term.shape
        term = term.reshape(self.planes, 2, rows // self.wide, cols)
        term = self.scatter_core(term)
        parts = []
        for low, high, order in self.column_cuts(cols):
            part = term[:, :, low:high]
            left = sorted(self.bits, reverse=True)
            part = part.reshape((2,) * len(left) + part.shape[1:])
            for bit in order:
                axis = left.index(bit)
                my_bit = (self.t_at // bit) % 2
                mine = lax.dynamic_index_in_dim(part, my_bit, axis, keepdims=False)
                other = lax.dynamic_index_in_dim(part, 1 - my_bit, axis, keepdims=False)
                got = self.swap(other, 2 * bit)
                part = (mine.astype(jnp.float32) + got.astype(jnp.float32)).astype(jnp.bfloat16)
                left.remove(bit)
            parts.append(part)
        total = jnp.concatenate(parts, axis=1)
        return lax.psum_scatter(total, "narrow", scatter_dimension=0, tiled=True)

    def gather_tokens(self, rows):
        if self.planes != 4:
            every = lax.all_gather(
                rows, MESH_AXES, axis=0, tiled=False, axis_index_groups=self.same_plane
            )
            return [every[k] for k in range(self.planes)]
        half = rows.shape[0] // 2
        by_x = self.swap(rows, 2)
        by_y = self.swap(rows, 4)
        corner = [self.swap(by_y[:half], 2), self.swap(by_x[half:], 4)]
        return [rows, by_x, by_y, jnp.concatenate(corner)]

    def scatter_tokens(self, blocks):
        if self.planes != 4:
            every = jnp.concatenate([b.astype(jnp.bfloat16) for b in blocks])
            total = lax.psum_scatter(
                every, MESH_AXES, scatter_dimension=0, tiled=True, axis_index_groups=self.same_plane
            )
            return total.astype(jnp.float32)
        own, by_x, by_y, corner = blocks
        half = own.shape[0] // 2
        corner = corner.astype(jnp.bfloat16)
        top = self.swap(corner[:half], 2).astype(jnp.float32)
        bottom = self.swap(corner[half:], 4).astype(jnp.float32)
        by_y = jnp.concatenate([by_y[:half] + top, by_y[half:]]).astype(jnp.bfloat16)
        by_x = jnp.concatenate([by_x[:half], by_x[half:] + bottom]).astype(jnp.bfloat16)
        return (
            own
            + self.swap(by_x, 2).astype(jnp.float32)
            + self.swap(by_y, 4).astype(jnp.float32)
        )

    def trade_columns(self, pieces):
        came = jnp.zeros_like(pieces)
        for d in range(self.planes):
            piece = lax.dynamic_index_in_dim(pieces, self.t_at ^ d, 0)
            if d:
                piece = self.swap(piece, 2 * d)
            came = lax.dynamic_update_slice(came, piece, (self.t_at ^ d, 0, 0))
        return came

    def keys_before(self, own):
        blocks = [own]
        for _ in range(self.n - 1):
            blocks.append(self.shift(blocks[-1], 1))
        return blocks

    def keys_back(self, terms):
        got = None
        for r in range(self.n - 1, 0, -1):
            term = terms[r] if got is None else terms[r] + got
            got = self.shift(term.astype(jnp.bfloat16), -1).astype(jnp.float32)
        return terms[0] if got is None else terms[0] + got

    def gather_first(self, qkv, out, gains, count, trade):
        rows = qkv.shape[0]
        if self.planes == 4 and self.n > 1:
            digits = jnp.stack([count // 16, count % 16]).astype(jnp.bfloat16)
            ext = jnp.concatenate([gains.reshape(1, 2 * rows), jnp.zeros((15, 2 * rows), gains.dtype)])
            ext = lax.dynamic_update_slice(ext, digits[None], (1, 0))
            qkv_all, out_line, ext_all, came = gather_first(qkv, out, ext, trade, self.planes, self.n)
            ext_all = ext_all.reshape(self.wide * self.n, 16, 2 * rows)
            gain_full = ext_all[:, 0].reshape(-1, 2, rows).transpose(1, 0, 2).reshape(2, -1)
            digits = ext_all[:, 1, :2].astype(jnp.int32)
            most = jnp.max(digits[:, 0] * 16 + digits[:, 1])
            return (
                qkv_all.reshape(self.wide * self.n * rows, -1),
                out_line.reshape(self.n * rows, -1),
                gain_full,
                most,
                came,
            )
        return (
            lax.all_gather(qkv, MESH_AXES, axis=0, tiled=True),
            lax.all_gather(out, "narrow", axis=0, tiled=True),
            lax.all_gather(gains, MESH_AXES, axis=1, tiled=True),
            lax.pmax(count, MESH_AXES),
            self.trade_columns(trade),
        )


def dot32(a, b):
    return jnp.dot(a, b, preferred_element_type=jnp.float32)


def dot_low(a, b):
    return jnp.dot(a, b, preferred_element_type=jnp.float32).astype(jnp.bfloat16)


def pick_live(mask, cap):
    flat = mask.reshape(-1)
    rows = flat.shape[0]
    at = jnp.arange(rows, dtype=jnp.int32)
    rank = jnp.sum(jnp.where(at[None, :] <= at[:, None], flat[None, :], 0), axis=1) - 1
    slot = jnp.arange(cap, dtype=jnp.int32)
    chosen = (rank[None, :] == slot[:, None]) & (flat[None, :] == 1)
    return chosen, slot < jnp.sum(flat)


def layer(links, cap, given):
    (
        tokens,
        active,
        cotangent,
        gain_full,
        qkv_low,
        out_line,
        pieces,
        w_down,
    ) = given
    n, planes = links.n, links.planes
    seq_count, span_len, width = tokens.shape
    row_count = seq_count * span_len
    seq_len = n * span_len
    kv_width = KV_HEADS * HEAD_DIM
    ff_part = FF // planes
    shard_rows = pieces.shape[1]
    low = jnp.bfloat16

    gateup_low = lax.all_gather(
        pieces, MESH_AXES, axis=1, tiled=True, axis_index_groups=links.same_chip
    ).reshape(width, 2 * ff_part)
    down_low = lax.all_gather(
        w_down, MESH_AXES, axis=0, tiled=True, axis_index_groups=links.same_chip
    )
    out_low = links.gather_planes(out_line)

    def codes_of(block):
        mask = lax.dynamic_slice_in_dim(active, jnp.maximum(block, 0) * span_len, span_len, 1)
        chosen, live = pick_live(mask, cap)
        code = jnp.arange(seq_count, dtype=jnp.int32)[:, None] * seq_len + jnp.arange(span_len, dtype=jnp.int32)
        code = jnp.sum(jnp.where(chosen, code.reshape(1, -1), 0), axis=1) + block * span_len
        return chosen, live & (block >= 0), code

    chosen, live, own_code = codes_of(links.z_at)
    key_codes = []
    for r in range(n):
        _, there, code = codes_of(links.z_at - r)
        key_codes.append(jnp.where(there, code, seq_count * seq_len))
    key_code = jnp.concatenate(key_codes)[:, None]
    query_code = jnp.where(live, own_code, -1)[None]
    query_base = jnp.where(live, own_code // seq_len * seq_len, 0)[None]
    places = jnp.where(live, own_code % seq_len, 0).astype(jnp.float32)
    cosine_table, sine_table = rotary_tables(places)
    picker = chosen.astype(low)
    live_rows = live.astype(jnp.float32)[:, None]

    inputs = dot32(picker, tokens.reshape(row_count, width))
    down_grad = dot_low(picker, cotangent.reshape(row_count, width))
    upstream = down_grad.astype(jnp.float32)
    down_grad_blocks = links.gather_tokens(down_grad)

    normed, inverse_one = norm_forward(inputs, gain_full[0])
    normed_low = normed.astype(low)
    kv_part = dot32(normed_low, qkv_low[:, width:])
    kv_low = jnp.concatenate(
        [rotate_heads(kv_part[:, :kv_width], cosine_table, sine_table), kv_part[:, kv_width:]], axis=1
    ).astype(low)
    kv_all = jnp.concatenate(links.keys_before(kv_low))
    query_low = rotate_heads(dot32(normed_low, qkv_low[:, :width]), cosine_table, sine_table).astype(low)
    attended_low, totals = attend(query_low, kv_all, key_code, query_code, query_base)
    middle = inputs + live_rows * dot32(attended_low, out_low)
    normed_mid, inverse_two = norm_forward(middle, gain_full[1])
    blocks = links.gather_tokens(normed_mid.astype(low))

    down_terms, mid_terms, hidden_blocks, gateup_grad_blocks = [], [], [], []
    for block, down_grad_block in zip(blocks, down_grad_blocks):
        gate_part = dot32(block, gateup_low[:, :ff_part])
        upper_part = dot32(block, gateup_low[:, ff_part:])
        gate_sigmoid = jax.nn.sigmoid(gate_part)
        hidden = (gate_part * gate_sigmoid * upper_part).astype(low)
        grad_hidden = dot32(down_grad_block, down_low.T)
        grad_gate = grad_hidden * upper_part * gate_sigmoid * (1.0 + gate_part * (1.0 - gate_sigmoid))
        grad_upper = grad_hidden * gate_part * gate_sigmoid
        grad_gateup_low = jnp.concatenate([grad_gate, grad_upper], axis=1).astype(low)
        hidden_blocks.append(hidden)
        gateup_grad_blocks.append(grad_gateup_low)
        down_terms.append(dot32(hidden, down_low))
        mid_terms.append(dot32(grad_gateup_low, gateup_low.T))
    grad_normed_mid = links.scatter_tokens(mid_terms)

    term_down = dot_low(jnp.concatenate(hidden_blocks).T, jnp.concatenate(down_grad_blocks))
    term_gateup = dot_low(jnp.concatenate(blocks).T, jnp.concatenate(gateup_grad_blocks))
    down_half = links.scatter_core(term_down.reshape(1, 2, ff_part // 2, width))[0]
    gateup_half = links.scatter_core(term_gateup.reshape(planes, 2, n * shard_rows, 2 * ff_part))
    grad_down = lax.psum_scatter(down_half, "narrow", scatter_dimension=0, tiled=True)
    grad_pieces = lax.psum_scatter(gateup_half, "narrow", scatter_dimension=1, tiled=True)
    down_proj = links.scatter_tokens(down_terms)
    layer_out = (middle + down_proj).astype(low)

    grad_middle = upstream + norm_backward(middle, inverse_two, gain_full[1], grad_normed_mid)
    branch_grad_low = grad_middle.astype(low)
    branch_grad_low, down_half, gateup_half = lax.optimization_barrier(
        (branch_grad_low, down_half, gateup_half)
    )
    grad_attended_low = dot_low(branch_grad_low, out_low.T)
    grad_out = links.scatter_rows(dot_low(attended_low.T, branch_grad_low))
    inner = jnp.sum(
        (grad_attended_low.astype(jnp.float32) * attended_low.astype(jnp.float32)).reshape(
            cap, HEADS, HEAD_DIM
        ),
        axis=-1,
    )
    inner = inner.T.reshape(KV_HEADS, GROUP, cap)
    grad_query, key_term, value_term = attend_back(
        query_low, kv_all, grad_attended_low, totals, inner, key_code, query_code, query_base
    )
    kv_terms = [
        jnp.concatenate([key_term[r * cap : (r + 1) * cap], value_term[r * cap : (r + 1) * cap]], axis=1)
        for r in range(n)
    ]
    grad_kv = links.keys_back(kv_terms)
    grad_query_low = rotate_heads(grad_query, cosine_table, -sine_table).astype(low)
    grad_q_rows = links.scatter_rows(dot_low(normed_low.T, grad_query_low))
    grad_kv_low = jnp.concatenate(
        [rotate_heads(grad_kv[:, :kv_width], cosine_table, -sine_table), grad_kv[:, kv_width:]], axis=1
    ).astype(low)
    grad_kv_rows = links.scatter_rows(dot_low(normed_low.T, grad_kv_low))
    grad_normed = dot32(grad_query_low, qkv_low[:, :width].T) + dot32(grad_kv_low, qkv_low[:, width:].T)
    grad_tokens = (
        grad_middle + norm_backward(inputs, inverse_one, gain_full[0], grad_normed)
    ).astype(low)

    def spread(packed, skipped):
        back = lax.dot_general(
            picker, packed, (((0,), (0,)), ((), ())), preferred_element_type=jnp.float32
        ).astype(low)
        mask = lax.dynamic_slice_in_dim(active, links.z_at * span_len, span_len, 1)
        return jnp.where(mask[:, :, None] == 1, back.reshape(skipped.shape), skipped)

    layer_out, grad_tokens = spread(layer_out, tokens), spread(grad_tokens, cotangent)
    grad_pieces = links.trade_columns(grad_pieces).reshape(planes, shard_rows, 2, ff_part)
    grad_gateup = grad_pieces.transpose(1, 2, 0, 3).reshape(shard_rows, 2 * FF)
    grad_qkv = jnp.concatenate([grad_q_rows, grad_kv_rows], axis=1)
    return layer_out, grad_tokens, grad_qkv, grad_out, grad_gateup, grad_down


def on_device(
    tokens,
    active,
    cotangent,
    gain_rows,
    w_qkv,
    w_out,
    w_gateup,
    w_down,
    moment_gains,
    moment_qkv,
    moment_out,
    moment_gateup,
    moment_down,
    average_gains,
    average_qkv,
    average_out,
    average_gateup,
    average_down,
):
    links = Links()
    planes = links.planes
    seq_count, span_len, _ = tokens.shape
    row_count = seq_count * span_len
    ff_part = FF // planes
    low = jnp.bfloat16

    gains_low = gain_rows.astype(low)
    shard_rows = w_gateup.shape[0]
    gateup_shard = w_gateup.astype(low)
    pieces = gateup_shard.reshape(shard_rows, 2, planes, ff_part)
    pieces = pieces.transpose(2, 0, 1, 3).reshape(planes, shard_rows, 2 * ff_part)
    qkv_shard = w_qkv.astype(low)
    own_mask = lax.dynamic_slice_in_dim(active, links.z_at * span_len, span_len, 1)
    qkv_low, out_line, gain_full, most, pieces = links.gather_first(
        qkv_shard, w_out.astype(low), gains_low, jnp.sum(own_mask), pieces
    )
    gain_full = gain_full.astype(jnp.float32)
    given = (tokens, active, cotangent, gain_full, qkv_low, out_line, pieces, w_down.astype(low))
    few = -(-3 * row_count // 4 // 128) * 128
    if few < row_count:
        found = lax.cond(
            most <= few,
            lambda *g: layer(links, few, g),
            lambda *g: layer(links, row_count, g),
            *given,
        )
    else:
        found = layer(links, row_count, given)
    layer_out, grad_tokens, grad_qkv, grad_out, grad_gateup, grad_down = found
    grad_qkv, grad_out, grad_gateup, grad_down = (
        g.astype(jnp.float32) for g in (grad_qkv, grad_out, grad_gateup, grad_down)
    )

    def gain_grad(shard, gradient, row):
        return jnp.sum(shard.astype(jnp.float32) * gradient, axis=1) / gains_low[row].astype(jnp.float32)

    grad_gains = jnp.stack([gain_grad(qkv_shard, grad_qkv, 0), gain_grad(gateup_shard, grad_gateup, 1)])
    state_gains = advance_state(gain_rows, moment_gains, average_gains, grad_gains)
    state_qkv = advance_state(w_qkv, moment_qkv, average_qkv, grad_qkv)
    state_out = advance_state(w_out, moment_out, average_out, grad_out)
    state_gateup = advance_state(w_gateup, moment_gateup, average_gateup, grad_gateup)
    state_down = advance_state(w_down, moment_down, average_down, grad_down)
    return (
        layer_out,
        grad_tokens,
        grad_gains,
        grad_qkv,
        grad_out,
        grad_gateup,
        grad_down,
        state_gains[0],
        state_qkv[0],
        state_out[0],
        state_gateup[0],
        state_down[0],
        state_gains[1],
        state_qkv[1],
        state_out[1],
        state_gateup[1],
        state_down[1],
        state_gains[2],
        state_qkv[2],
        state_out[2],
        state_gateup[2],
        state_down[2],
    )


def solution(mesh):
    in_specs = (
        P("wide", "narrow", None),
        P("wide", None),
        P("wide", "narrow", None),
        P(None, ("wide", "narrow")),
        P(("wide", "narrow"), None),
        P(("wide", "narrow"), None),
        P(("wide", "narrow"), None),
        P(("wide", "narrow"), None),
        P(None, ("wide", "narrow")),
        P(("wide", "narrow"), None),
        P(("wide", "narrow"), None),
        P(("wide", "narrow"), None),
        P(("wide", "narrow"), None),
        P(None, ("wide", "narrow")),
        P(("wide", "narrow"), None),
        P(("wide", "narrow"), None),
        P(("wide", "narrow"), None),
        P(("wide", "narrow"), None),
    )
    out_specs = (
        P("wide", "narrow", None),
        P("wide", "narrow", None),
        P(None, ("wide", "narrow")),
        P(("wide", "narrow"), None),
        P(("wide", "narrow"), None),
        P(("wide", "narrow"), None),
        P(("wide", "narrow"), None),
        P(None, ("wide", "narrow")),
        P(("wide", "narrow"), None),
        P(("wide", "narrow"), None),
        P(("wide", "narrow"), None),
        P(("wide", "narrow"), None),
        P(None, ("wide", "narrow")),
        P(("wide", "narrow"), None),
        P(("wide", "narrow"), None),
        P(("wide", "narrow"), None),
        P(("wide", "narrow"), None),
        P(None, ("wide", "narrow")),
        P(("wide", "narrow"), None),
        P(("wide", "narrow"), None),
        P(("wide", "narrow"), None),
        P(("wide", "narrow"), None),
    )
    return jax.shard_map(
        on_device, mesh=mesh, in_specs=in_specs, out_specs=out_specs, check_vma=False
    )
```

```python
import functools

import jax
import jax.numpy as jnp
from jax import lax
from jax.experimental import pallas as pl
from jax.experimental.pallas import tpu as pltpu
from jax.sharding import PartitionSpec as P

HEADS = 16
KV_HEADS = 4
HEAD_DIM = 128
GROUP = HEADS // KV_HEADS
FF = 5632


EPSILON = 1e-05
MOMENTUM = 0.5
AVERAGING = 0.5
STEP_RATE = 0.0003

MESH = pl.DeviceIdType.MESH
MESH_AXES = ("wide", "narrow")
SCORE_SCALE = HEAD_DIM ** (-0.5)
LOG2_E = 1.4426950408889634
MASKED = -1e30


def dot_nt(a, b):
    return lax.dot_general(a, b, (((1,), (1,)), ((), ())), preferred_element_type=jnp.float32)


def dot_tn(a, b):
    return lax.dot_general(a, b, (((0,), (0,)), ((), ())), preferred_element_type=jnp.float32)


UNIT_GROUP = 256
WIDTH_GROUP = 256


def unit_groups(units):
    return [(low, min(low + UNIT_GROUP, units)) for low in range(0, units, UNIT_GROUP)]


def mlp_kernel(
    cap, counts, live_ref, rows_ref, grad_ref, gateup_hbm, down_hbm,
    hidden_ref, gateup_grad_ref, back_ref, gateup_ref, down_ref, gateup_sems, down_sems,
):
    step = pl.program_id(0)
    width = rows_ref.shape[1]
    units = down_ref.shape[0]
    full, rest = units // UNIT_GROUP, units % UNIT_GROUP
    live = live_ref[step]

    def span(low, size):
        return pl.ds(low if isinstance(low, int) else pl.multiple_of(low, size), size)

    def gateup_part(k, low, size):
        both = span(2 * low, 2 * size)
        return pltpu.make_async_copy(gateup_hbm.at[:, both], gateup_ref.at[:, both], gateup_sems.at[k])

    def down_part(k, low, size):
        one = span(low, size)
        return pltpu.make_async_copy(down_hbm.at[one, :], down_ref.at[one, :], down_sems.at[k])

    @pl.when(step == 0)
    def _():
        for k, (low, high) in enumerate(unit_groups(units)):
            gateup_part(k, low, high - low).start()
            down_part(k, low, high - low).start()

    def run(count):
        def units_step(k, low, size):
            @pl.when(step == 0)
            def _():
                gateup_part(k, low, size).wait()
                down_part(k, low, size).wait()

            both, one = span(2 * low, 2 * size), span(low, size)
            gate_up = jnp.dot(rows_ref[:count, :], gateup_ref[:, both], preferred_element_type=jnp.float32)
            gate, upper = gate_up[:, :size], gate_up[:, size:]
            grad_hidden = dot_nt(grad_ref[:count, :], down_ref[one, :])
            sigmoid = 1.0 / (1.0 + jnp.exp(-gate))
            silu = gate * sigmoid
            hidden_ref[:count, one] = (silu * upper).astype(jnp.bfloat16)
            grad_gate = grad_hidden * upper * (sigmoid + silu * (1.0 - sigmoid))
            grad_upper = grad_hidden * silu
            gateup_grad_ref[:count, both] = jnp.concatenate([grad_gate, grad_upper], axis=1).astype(jnp.bfloat16)

        lax.fori_loop(0, full, lambda k, c: (units_step(k, k * UNIT_GROUP, UNIT_GROUP), c)[1], 0)
        if rest:
            units_step(full, full * UNIT_GROUP, rest)

        def back_step(k, carry):
            at = span(k * WIDTH_GROUP, WIDTH_GROUP)
            back_ref[:count, at] = dot_nt(gateup_grad_ref[:count, :], gateup_ref[at, :]).astype(jnp.bfloat16)
            return carry

        lax.fori_loop(0, width // WIDTH_GROUP, back_step, 0)
        if count < cap:
            for ref in (hidden_ref, gateup_grad_ref, back_ref):
                ref[count:, :] = jnp.zeros((cap - count, ref.shape[1]), ref.dtype)

    for low, count in zip((None,) + counts[:-1], counts):
        chosen = live > (-1 if low is None else low)
        if count < cap:
            chosen &= live <= count

        @pl.when(chosen)
        def _(count=count):
            run(count)


def mlp_block(rows, grad, live, gateup, down, cap):
    blocks = rows.shape[0] // cap
    width = rows.shape[1]
    units = down.shape[0]
    if units % 128 or cap % 128:
        return mlp_plain(rows, grad, gateup, down)
    counts = (192, 256, 320, 384) if cap == 384 else tuple(range(256, cap, 256)) + (cap,)
    groups = len(unit_groups(units))
    low = jnp.bfloat16
    by_block = lambda cols: pl.BlockSpec((cap, cols), lambda b, live: (b, 0))
    return pl.pallas_call(
        functools.partial(mlp_kernel, cap, counts),
        grid_spec=pltpu.PrefetchScalarGridSpec(
            num_scalar_prefetch=1,
            grid=(blocks,),
            in_specs=[by_block(width), by_block(width)] + [pl.BlockSpec(memory_space=pl.ANY)] * 2,
            out_specs=(by_block(units), by_block(2 * units), by_block(width)),
            scratch_shapes=[
                pltpu.VMEM(gateup.shape, low),
                pltpu.VMEM(down.shape, low),
                pltpu.SemaphoreType.DMA((groups,)),
                pltpu.SemaphoreType.DMA((groups,)),
            ],
        ),
        out_shape=(
            jax.ShapeDtypeStruct((blocks * cap, units), low),
            jax.ShapeDtypeStruct((blocks * cap, 2 * units), low),
            jax.ShapeDtypeStruct((blocks * cap, width), low),
        ),
        compiler_params=pltpu.CompilerParams(vmem_limit_bytes=56 * 1024 * 1024),
        cost_estimate=pl.CostEstimate(
            flops=10 * blocks * cap * width * units,
            bytes_accessed=2 * (gateup.size + down.size) + 12 * blocks * cap * width,
            transcendentals=blocks * cap * units,
        ),
        name="mlp_block",
    )(live, rows, grad, gateup, down)


def mlp_plain(rows, grad, gateup, down):
    groups = unit_groups(down.shape[0])
    gate_up = jnp.dot(rows, gateup, preferred_element_type=jnp.float32)
    gate = jnp.concatenate([gate_up[:, 2 * low : low + high] for low, high in groups], axis=1)
    upper = jnp.concatenate([gate_up[:, low + high : 2 * high] for low, high in groups], axis=1)
    grad_hidden = jnp.dot(grad, down.T, preferred_element_type=jnp.float32)
    sigmoid = jax.nn.sigmoid(gate)
    silu = gate * sigmoid
    hidden = (silu * upper).astype(jnp.bfloat16)
    grad_gate = grad_hidden * upper * (sigmoid + silu * (1.0 - sigmoid))
    grad_upper = grad_hidden * silu
    gateup_grad = jnp.concatenate(
        [part[:, low:high] for low, high in groups for part in (grad_gate, grad_upper)], axis=1
    ).astype(jnp.bfloat16)
    back = jnp.dot(gateup_grad, gateup.T, preferred_element_type=jnp.float32).astype(jnp.bfloat16)
    return hidden, gateup_grad, back


class Place:
    def __init__(self, n):
        self.n = n
        self.wide = lax.axis_index("wide")
        self.z = lax.axis_index("narrow")
        self.t, self.core = self.wide // 2, self.wide % 2
        self.t_x, self.t_y, self.t_d = self.t ^ 1, self.t ^ 2, self.t ^ 3
        self.by_x = self.device(self.t_x)
        self.by_y = self.device(self.t_y)
        self.by_d = self.device(self.t_d)
        self.sibling = self.device(self.t, core=1 - self.core)
        self.above = self.device(self.t, z=jnp.minimum(self.z + 1, n - 1))
        self.below = self.device(self.t, z=jnp.maximum(self.z - 1, 0))

    def device(self, t, core=None, z=None):
        return (t * 2 + (self.core if core is None else core), self.z if z is None else z)

    def greet(self, others):
        barrier = pltpu.get_barrier_semaphore()
        for other in others:
            pl.semaphore_signal(barrier, inc=1, device_id=other, device_id_type=MESH)

        @pl.when(self.z > 0)
        def _():
            pl.semaphore_signal(barrier, inc=1, device_id=self.below, device_id_type=MESH)

        @pl.when(self.z < self.n - 1)
        def _():
            pl.semaphore_signal(barrier, inc=1, device_id=self.above, device_id_type=MESH)

        inner = (self.z > 0).astype(jnp.int32) + (self.z < self.n - 1).astype(jnp.int32)
        pl.semaphore_wait(barrier, len(others) + inner)


class Copies:
    def __init__(self, send_sems, recv_sems):
        self.send_sems, self.recv_sems = send_sems, recv_sems
        self.count = 0
        self.started = []

    def make(self, src, dst, to):
        k = self.count
        self.count += 1
        return pltpu.make_async_remote_copy(
            src_ref=src, dst_ref=dst, send_sem=self.send_sems.at[k], recv_sem=self.recv_sems.at[k],
            device_id=to, device_id_type=MESH,
        )

    def same(self, ref, to):
        return self.make(ref, ref, to)

    def each(self, moves, when, act):
        def run():
            for m in moves:
                act(m)

        if when is None:
            run()
        else:
            pl.when(when)(run)

    def go(self, moves, when=None):
        self.each(moves, when, lambda m: m.start())
        self.started.append((moves, when))

    def arrive(self, moves, when=None):
        self.each(moves, when, lambda m: m.wait_recv())

    def end(self):
        for moves, when in self.started:
            self.each(moves, when, lambda m: m.wait_send())


class LineGather:
    def __init__(self, place, copies, view, own):
        self.place, self.copies, self.view, self.own = place, copies, view, own
        self.up, self.down = {}, {}

    def send(self, step):
        p, last = self.place, self.place.n - 1
        block = self.view(jnp.maximum(p.z - (step - 1), 0))
        self.up[step] = self.copies.make(self.own if step == 1 else block, block, p.above)
        self.copies.go([self.up[step]], (p.z - (step - 1) >= 0) & (p.z < last))
        block = self.view(jnp.minimum(p.z + (step - 1), last))
        self.down[step] = self.copies.make(self.own if step == 1 else block, block, p.below)
        self.copies.go([self.down[step]], (p.z + (step - 1) <= last) & (p.z > 0))

    def take(self, step):
        p = self.place
        self.copies.arrive([self.up[step]], p.z - step >= 0)
        self.copies.arrive([self.down[step]], p.z + step <= p.n - 1)

    def hand_over(self, step):
        p, last = self.place, self.place.n - 1
        moves = []
        for at, there in ((p.z - step, p.z - step >= 0), (p.z + step, p.z + step <= last)):
            block = self.view(jnp.clip(at, 0, last))
            move = self.copies.same(block, p.sibling)
            self.copies.go([move], there)
            moves.append(([move], there))
        return moves


def gather_kernel(
    n, qkv_ref, out_ref, gateup_ref, down_ref, ext_ref, qkv_all, out_all, ext_all, came, down_all,
    qkv_low, out_low, trade_low, down_low, send_sems, recv_sems, local_sems,
):
    p = Place(n)
    c = Copies(send_sems, recv_sems)
    t, core, z = p.t, p.core, p.z
    low = jnp.bfloat16
    qkv_low[...] = qkv_ref[...].astype(low)
    p.greet([p.by_x, p.by_y, p.by_d, p.sibling])

    half = qkv_ref.shape[1] // 256 * 128
    qa, qb = slice(0, half), slice(half, qkv_ref.shape[1])
    lines = [
        LineGather(p, c, lambda zz, cols=cols: qkv_all.at[t, core, zz, :, cols], qkv_low.at[:, cols])
        for cols in (qa, qb)
    ]
    lines.append(LineGather(p, c, lambda zz: ext_all.at[t, core, zz], ext_ref))
    for line in lines:
        line.send(1)
    local = []

    def place(src, dst):
        move = pltpu.make_async_copy(src, dst, local_sems.at[len(local)])
        move.start()
        local.append(move)

    place(qkv_low, qkv_all.at[t, core, z])
    place(ext_ref, ext_all.at[t, core, z])
    units = trade_low.shape[2] // 2
    for k in range(trade_low.shape[0]):
        for first, last in unit_groups(units):
            for to, start in ((2 * first, k * units), (first + last, gateup_ref.shape[1] // 2 + k * units)):
                trade_low[k, :, to : to + last - first] = gateup_ref[:, start + first : start + last].astype(low)
    place(trade_low.at[t], came.at[t])
    trade = [
        c.make(trade_low.at[k], came.at[t], to) for k, to in ((p.t_x, p.by_x), (p.t_y, p.by_y), (p.t_d, p.by_d))
    ]
    c.go(trade)
    out_low[...] = out_ref[...].astype(low)
    down_low[...] = down_ref[...].astype(low)
    place(out_low, out_all.at[t, core, z])
    place(down_low, down_all.at[core, z])
    line_out = LineGather(p, c, lambda zz: out_all.at[t, core, zz], out_low)
    line_down = LineGather(p, c, lambda zz: down_all.at[core, zz], down_low)
    down_own = c.make(down_low, down_all.at[core, z], p.sibling)
    c.go([down_own])
    handed = [([down_own], None)]
    for step in range(1, n):
        for line in lines:
            line.take(step)
            if step < n - 1:
                line.send(step + 1)
    for move in local:
        move.wait()
    a_y = c.same(qkv_all.at[t, core, :, :, qa], p.by_y)
    b_x = c.same(qkv_all.at[t, core, :, :, qb], p.by_x)
    e_x = c.same(ext_all.at[t, core], p.by_x)
    c.go([a_y, b_x, e_x])
    line_down.send(1)
    line_out.send(1)
    own = [c.same(qkv_all.at[t, core], p.sibling), c.same(ext_all.at[t, core], p.sibling)]
    c.go(own)
    c.arrive([e_x])
    e_y = [c.same(ext_all.at[k, core], p.by_y) for k in (t, p.t_x)]
    c.go(e_y)
    c.arrive([a_y])
    a_x = [c.same(qkv_all.at[k, core, :, :, qa], p.by_x) for k in (t, p.t_y)]
    c.go(a_x)
    c.arrive([b_x])
    b_y = [c.same(qkv_all.at[k, core, :, :, qb], p.by_y) for k in (t, p.t_x)]
    c.go(b_y)
    near = [
        c.same(qkv_all.at[p.t_y, core, :, :, qa], p.sibling),
        c.same(qkv_all.at[p.t_x, core, :, :, qb], p.sibling),
        c.same(ext_all.at[p.t_x, core], p.sibling),
    ]
    c.go(near)
    c.arrive(e_y)
    far = [c.same(ext_all.at[k, core], p.sibling) for k in (p.t_y, p.t_d)]
    c.go(far)
    for step in range(1, n):
        for line in (line_down, line_out):
            line.take(step)
            if step < n - 1:
                line.send(step + 1)
        handed += line_down.hand_over(step)
        if step == max(n - 2, 1):
            c.arrive(a_x)
            c.arrive(b_y)
            last = [c.same(qkv_all.at[k, core, :, :, qa], p.sibling) for k in (p.t_x, p.t_d)]
            last += [c.same(qkv_all.at[k, core, :, :, qb], p.sibling) for k in (p.t_y, p.t_d)]
            c.go(last)
    c.arrive(trade + own + near + far + last)
    for moves, when in handed:
        c.arrive(moves, when)
    c.end()


def gather_first(qkv, out, gateup, down, ext, planes, n):
    any_spec = pl.BlockSpec(memory_space=pl.ANY)
    rows = qkv.shape[0]
    part = gateup.shape[1] // planes
    low = jnp.bfloat16
    copies = 64
    return pl.pallas_call(
        functools.partial(gather_kernel, n),
        out_shape=(
            jax.ShapeDtypeStruct((planes, 2, n, rows, qkv.shape[1]), low),
            jax.ShapeDtypeStruct((planes, 2, n, rows, out.shape[1]), low),
            jax.ShapeDtypeStruct((planes, 2, n) + ext.shape, low),
            jax.ShapeDtypeStruct((planes, rows, part), low),
            jax.ShapeDtypeStruct((2, n) + down.shape, low),
        ),
        in_specs=[pl.BlockSpec(memory_space=pltpu.VMEM)] * 5,
        out_specs=(any_spec,) * 5,
        scratch_shapes=[
            pltpu.VMEM(qkv.shape, low),
            pltpu.VMEM(out.shape, low),
            pltpu.VMEM((planes, rows, part), low),
            pltpu.VMEM(down.shape, low),
            pltpu.SemaphoreType.DMA((copies,)),
            pltpu.SemaphoreType.DMA((copies,)),
            pltpu.SemaphoreType.DMA((8,)),
        ],
        compiler_params=pltpu.CompilerParams(
            collective_id=0, has_side_effects=True, vmem_limit_bytes=32 * 1024 * 1024
        ),
        name="gather_first",
    )(qkv, out, gateup, down, ext)


def fill_bias(r, key_code, query_code, query_base, bias):
    rows = bias.shape[0]
    code = key_code[r * rows : (r + 1) * rows, :]
    seen = (code <= query_code[...]) & (code >= query_base[...])
    bias[...] = jnp.where(seen, 0.0, MASKED)


class PlaneGather:
    def __init__(self, place, copies, whole):
        self.p, self.c, self.whole = place, copies, whole
        cols = whole.shape[-1]
        self.a, self.b = slice(0, cols // 2), slice(cols // 2, cols)

    def block(self, t, cols=slice(None)):
        return self.whole.at[t, self.p.core, :, :, cols]

    def begin(self):
        p, c = self.p, self.c
        self.a_y, self.b_x = c.same(self.block(p.t, self.a), p.by_y), c.same(self.block(p.t, self.b), p.by_x)
        self.over = [c.same(self.block(p.t), p.sibling)]
        c.go([self.a_y, self.b_x] + self.over)

    def middle(self):
        p, c = self.p, self.c
        c.arrive([self.a_y, self.b_x])
        self.a_x = [c.same(self.block(k, self.a), p.by_x) for k in (p.t, p.t_y)]
        self.b_y = [c.same(self.block(k, self.b), p.by_y) for k in (p.t, p.t_x)]
        near = [c.same(self.block(p.t_y, self.a), p.sibling), c.same(self.block(p.t_x, self.b), p.sibling)]
        c.go(self.a_x + self.b_y + near)
        self.over += near

    def end(self):
        p, c = self.p, self.c
        c.arrive(self.a_x + self.b_y)
        far = [c.same(self.block(k, self.a), p.sibling) for k in (p.t_x, p.t_d)]
        far += [c.same(self.block(k, self.b), p.sibling) for k in (p.t_y, p.t_d)]
        c.go(far)
        c.arrive(self.over + far)


def attend_kernel(n, with_out, *refs):
    q_ref, kv_ref, key_code, query_code, query_base = refs[:5]
    o_ref, total_ref, kv_all = refs[5 + with_out : 8 + with_out]
    out_all = refs[8 + with_out] if with_out else None
    peak_now, total_now, mixed_now, bias, send_sems, recv_sems = refs[-6:]
    p = Place(n)
    c = Copies(send_sems, recv_sems)
    z = p.z
    rows = q_ref.shape[0]
    values_at = KV_HEADS * HEAD_DIM
    slot = lambda r: kv_all.at[r * rows : (r + 1) * rows, :]
    p.greet([p.by_x, p.by_y, p.sibling] if with_out else [])
    copies = [c.make(kv_ref if r == 0 else slot(r), slot(r + 1), p.above) for r in range(n - 1)]
    if copies:
        c.go([copies[0]], z < n - 1)
    if with_out:
        out_plane = PlaneGather(p, c, out_all)
        out_plane.begin()

    kv_all[:rows, :] = kv_ref[...]
    for r in range(1, n):
        @pl.when(z < r)
        def _(r=r):
            kv_all[r * rows : (r + 1) * rows, :] = jnp.zeros((rows, kv_all.shape[1]), kv_all.dtype)

    def block(r):
        fill_bias(r, key_code, query_code, query_base, bias)
        at = slice(r * rows, (r + 1) * rows)

        def group(g, carry):
            keys = kv_all[at, pl.ds(pl.multiple_of(g * HEAD_DIM, HEAD_DIM), HEAD_DIM)]
            values = kv_all[at, pl.ds(pl.multiple_of(values_at + g * HEAD_DIM, HEAD_DIM), HEAD_DIM)]
            hidden = bias[...]
            for h in range(GROUP):
                lanes = pl.ds(pl.multiple_of((g * GROUP + h) * HEAD_DIM, HEAD_DIM), HEAD_DIM)
                scores = dot_nt(keys, q_ref[:, lanes]) * (SCORE_SCALE * LOG2_E) + hidden
                peak = jnp.max(scores, axis=0, keepdims=True)
                if r:
                    before = peak_now[g, h : h + 1, :]
                    peak = jnp.maximum(peak, before)
                weights = jnp.exp2(scores - peak)
                total = jnp.sum(weights, axis=0, keepdims=True)
                mixed = dot_tn(values, weights.astype(jnp.bfloat16))
                if r:
                    shrink = jnp.exp2(before - peak)
                    total = total + total_now[g, h : h + 1, :] * shrink
                    mixed = mixed + mixed_now[g, h] * shrink
                peak_now[g, h : h + 1, :] = peak
                total_now[g, h : h + 1, :] = total
                mixed_now[g, h] = mixed
            return carry

        lax.fori_loop(0, KV_HEADS, group, 0)

    block(0)
    for r in range(1, n):
        c.arrive([copies[r - 1]], z >= r)
        if r < n - 1:
            c.go([copies[r]], (z >= r) & (z < n - 1))
        if with_out and r == 1:
            out_plane.middle()
        if with_out and r == n - 1:
            out_plane.end()

        @pl.when(z >= r)
        def _(r=r):
            block(r)

    def finish(g, carry):
        for h in range(GROUP):
            lanes = pl.ds(pl.multiple_of((g * GROUP + h) * HEAD_DIM, HEAD_DIM), HEAD_DIM)
            total = total_now[g, h : h + 1, :]
            o_ref[:, lanes] = (mixed_now[g, h] / total).T.astype(jnp.bfloat16)
            total_ref[g, h : h + 1, :] = peak_now[g, h : h + 1, :] + jnp.log2(total)
        return carry

    lax.fori_loop(0, KV_HEADS, finish, 0)
    c.end()


def attend(query, kv, key_code, query_code, query_base, n, collective_id, out_all=None):
    rows, width = query.shape
    in_vmem = pl.BlockSpec(memory_space=pltpu.VMEM)
    any_spec = pl.BlockSpec(memory_space=pl.ANY)
    outs = [] if out_all is None else [out_all]
    copies = n + 16
    return pl.pallas_call(
        functools.partial(attend_kernel, n, len(outs)),
        in_specs=[in_vmem] * 5 + [any_spec] * len(outs),
        out_specs=(in_vmem,) * 3 + (any_spec,) * len(outs),
        input_output_aliases={5: 3} if outs else {},
        out_shape=(
            jax.ShapeDtypeStruct((rows, width), jnp.bfloat16),
            jax.ShapeDtypeStruct((KV_HEADS, GROUP, rows), jnp.float32),
            jax.ShapeDtypeStruct((n * rows, kv.shape[1]), jnp.bfloat16),
        )
        + tuple(jax.ShapeDtypeStruct(o.shape, o.dtype) for o in outs),
        scratch_shapes=[
            pltpu.VMEM((KV_HEADS, GROUP, rows), jnp.float32),
            pltpu.VMEM((KV_HEADS, GROUP, rows), jnp.float32),
            pltpu.VMEM((KV_HEADS, GROUP, HEAD_DIM, rows), jnp.float32),
            pltpu.VMEM((rows, rows), jnp.float32),
            pltpu.SemaphoreType.DMA((copies,)),
            pltpu.SemaphoreType.DMA((copies,)),
        ],
        compiler_params=pltpu.CompilerParams(
            vmem_limit_bytes=48 * 1024 * 1024, collective_id=collective_id, has_side_effects=True
        ),
        cost_estimate=pl.CostEstimate(
            flops=4 * rows * n * rows * width, bytes_accessed=8 * rows * width, transcendentals=HEADS * rows * n * rows
        ),
        name="attend",
    )(query, kv, key_code, query_code, query_base, *outs)


def attend_back_kernel(
    n, q_ref, kv_all, do_ref, total_ref, inner_ref, key_code, query_code, query_base, dq_ref, dkv_ref,
    dq_now, dkv_now, bias, leaving, came, send_sems, recv_sems,
):
    p = Place(n)
    c = Copies(send_sems, recv_sems)
    z = p.z
    rows = q_ref.shape[0]
    values_at = KV_HEADS * HEAD_DIM
    p.greet([])
    copies = {r: c.make(leaving.at[r - 1], came.at[r - 1], p.below) for r in range(1, n)}
    dq_now[...] = jnp.zeros_like(dq_now)

    def block(r):
        fill_bias(r, key_code, query_code, query_base, bias)
        at = slice(r * rows, (r + 1) * rows)

        def group(g, carry):
            key_lanes = pl.ds(pl.multiple_of(g * HEAD_DIM, HEAD_DIM), HEAD_DIM)
            value_lanes = pl.ds(pl.multiple_of(values_at + g * HEAD_DIM, HEAD_DIM), HEAD_DIM)
            keys, values, hidden = kv_all[at, key_lanes], kv_all[at, value_lanes], bias[...]
            dk = dv = None
            for h in range(GROUP):
                lanes = pl.ds(pl.multiple_of((g * GROUP + h) * HEAD_DIM, HEAD_DIM), HEAD_DIM)
                query, grad = q_ref[:, lanes], do_ref[:, lanes]
                scores = dot_nt(keys, query) * (SCORE_SCALE * LOG2_E) + hidden
                weights = jnp.exp2(scores - total_ref[g, h : h + 1, :])
                grad_weights = dot_nt(values, grad)
                grad_scores = (weights * (grad_weights - inner_ref[g, h : h + 1, :])).astype(jnp.bfloat16)
                dv_term = jnp.dot(weights.astype(jnp.bfloat16), grad, preferred_element_type=jnp.float32)
                dk_term = jnp.dot(grad_scores, query, preferred_element_type=jnp.float32)
                dv = dv_term if dv is None else dv + dv_term
                dk = dk_term if dk is None else dk + dk_term
                dq_now[g, h] += dot_tn(keys, grad_scores)
            dkv_now[:, key_lanes] = dk * SCORE_SCALE
            dkv_now[:, value_lanes] = dv
            return carry

        lax.fori_loop(0, KV_HEADS, group, 0)

    for r in range(n - 1, -1, -1):
        @pl.when(z >= r)
        def _(r=r):
            block(r)
            if r < n - 1:
                @pl.when(z < n - 1)
                def _():
                    copies[r + 1].wait_recv()
                    dkv_now[...] += came[r].astype(jnp.float32)
            if r:
                leaving[r - 1] = dkv_now[...].astype(jnp.bfloat16)
                copies[r].start()
            else:
                dkv_ref[...] = dkv_now[...]

    def finish(g, carry):
        for h in range(GROUP):
            lanes = pl.ds(pl.multiple_of((g * GROUP + h) * HEAD_DIM, HEAD_DIM), HEAD_DIM)
            dq_ref[:, lanes] = dq_now[g, h].T * SCORE_SCALE
        return carry

    lax.fori_loop(0, KV_HEADS, finish, 0)
    for r in range(1, n):
        @pl.when(z >= r)
        def _(r=r):
            copies[r].wait_send()


def attend_back(query, kv_all, grad, total, inner, key_code, query_code, query_base, n, collective_id):
    rows, width = query.shape
    kv_cols = kv_all.shape[1]
    in_vmem = pl.BlockSpec(memory_space=pltpu.VMEM)
    slots = max(n - 1, 1)
    return pl.pallas_call(
        functools.partial(attend_back_kernel, n),
        in_specs=[in_vmem] * 8,
        out_specs=(in_vmem,) * 2,
        out_shape=(
            jax.ShapeDtypeStruct((rows, width), jnp.float32),
            jax.ShapeDtypeStruct((rows, kv_cols), jnp.float32),
        ),
        scratch_shapes=[
            pltpu.VMEM((KV_HEADS, GROUP, HEAD_DIM, rows), jnp.float32),
            pltpu.VMEM((rows, kv_cols), jnp.float32),
            pltpu.VMEM((rows, rows), jnp.float32),
            pltpu.VMEM((slots, rows, kv_cols), jnp.bfloat16),
            pltpu.VMEM((slots, rows, kv_cols), jnp.bfloat16),
            pltpu.SemaphoreType.DMA((n,)),
            pltpu.SemaphoreType.DMA((n,)),
        ],
        compiler_params=pltpu.CompilerParams(
            vmem_limit_bytes=56 * 1024 * 1024, collective_id=collective_id, has_side_effects=True
        ),
        cost_estimate=pl.CostEstimate(
            flops=10 * rows * n * rows * width, bytes_accessed=16 * rows * width, transcendentals=HEADS * rows * n * rows
        ),
        name="attend_back",
    )(query, kv_all, grad, total, inner, key_code, query_code, query_base)


def rotary_tables(positions):
    half_dim = HEAD_DIM // 2
    frequency = jnp.power(10000.0, -2.0 * jnp.arange(half_dim, dtype=jnp.float32) / HEAD_DIM)
    angles = positions[:, None] * frequency[None, :]
    return (jnp.cos(angles)[:, None, :], jnp.sin(angles)[:, None, :])


def rotate_heads(values, cosine_table, sine_table):
    half_dim = HEAD_DIM // 2
    cosine, sine = cosine_table[:, 0], sine_table[:, 0]
    cosine = jnp.concatenate([cosine, cosine], axis=1)
    sine = jnp.concatenate([-sine, sine], axis=1)
    done = []
    for start in range(0, values.shape[1], HEAD_DIM):
        head = values[:, start : start + HEAD_DIM]
        done.append(head * cosine + jnp.roll(head, half_dim, axis=1) * sine)
    return jnp.concatenate(done, axis=1)


def norm_forward(values_in, gain_row):
    inverse = lax.rsqrt(jnp.mean(values_in * values_in, axis=-1, keepdims=True) + EPSILON)
    return (values_in * inverse * gain_row, inverse)


def norm_backward(values_in, inverse, gain_row, incoming):
    scaled_grad = incoming * gain_row
    return inverse * scaled_grad - values_in * inverse * inverse * inverse * jnp.mean(
        scaled_grad * values_in, axis=-1, keepdims=True
    )


def advance_state(weight, moment, average, gradient):
    moment_next = MOMENTUM * moment + gradient
    weight_next = weight - STEP_RATE * (gradient + MOMENTUM * moment_next)
    average_next = AVERAGING * average + (1.0 - AVERAGING) * weight_next
    return (weight_next, moment_next, average_next)


class Links:
    def __init__(self):
        self.wide = lax.axis_size("wide")
        self.n = lax.axis_size("narrow")
        self.planes = self.wide // 2
        self.wide_at = lax.axis_index("wide")
        self.z_at = lax.axis_index("narrow")
        self.t_at = self.wide_at // 2
        self.core_at = self.wide_at % 2
        self.bits = [1 << k for k in range(self.planes.bit_length() - 1)]
        per_chip = 2 * self.n
        self.same_chip = [[t * per_chip + j for j in range(per_chip)] for t in range(self.planes)]
        self.same_plane = [
            [t * per_chip + j for t in range(self.planes)] for j in range(per_chip)
        ]

    def swap(self, values, flip):
        pairs = [(i, i ^ (flip * self.n)) for i in range(self.wide * self.n)]
        return lax.ppermute(values, MESH_AXES, pairs)

    def column_cuts(self, cols):
        lanes = cols // 128
        count = len(self.bits)
        edges = [128 * (lanes * k // count) for k in range(count + 1)]
        orders = [self.bits[k:] + self.bits[:k] for k in range(count)]
        return list(zip(edges[:-1], edges[1:], orders))

    def scatter_core(self, term):
        mine = lax.dynamic_index_in_dim(term, self.core_at, 1, keepdims=False)
        other = lax.dynamic_index_in_dim(term, 1 - self.core_at, 1, keepdims=False)
        got = self.swap(other, 1)
        return (mine.astype(jnp.float32) + got.astype(jnp.float32)).astype(jnp.bfloat16)

    def scatter_rows(self, term):
        rows, cols = term.shape
        term = term.reshape(self.planes, 2, rows // self.wide, cols)
        term = self.scatter_core(term)
        parts = []
        for low, high, order in self.column_cuts(cols):
            part = term[:, :, low:high]
            left = sorted(self.bits, reverse=True)
            part = part.reshape((2,) * len(left) + part.shape[1:])
            for bit in order:
                axis = left.index(bit)
                my_bit = (self.t_at // bit) % 2
                mine = lax.dynamic_index_in_dim(part, my_bit, axis, keepdims=False)
                other = lax.dynamic_index_in_dim(part, 1 - my_bit, axis, keepdims=False)
                got = self.swap(other, 2 * bit)
                part = (mine.astype(jnp.float32) + got.astype(jnp.float32)).astype(jnp.bfloat16)
                left.remove(bit)
            parts.append(part)
        total = jnp.concatenate(parts, axis=1)
        return lax.psum_scatter(total, "narrow", scatter_dimension=0, tiled=True)

    def gather_tokens(self, rows):
        if self.planes != 4:
            every = lax.all_gather(
                rows, MESH_AXES, axis=0, tiled=False, axis_index_groups=self.same_plane
            )
            return [every[k] for k in range(self.planes)]
        half = rows.shape[0] // 2
        by_x = self.swap(rows, 2)
        by_y = self.swap(rows, 4)
        corner = [self.swap(by_y[:half], 2), self.swap(by_x[half:], 4)]
        return [rows, by_x, by_y, jnp.concatenate(corner)]

    def scatter_tokens(self, blocks):
        if self.planes != 4:
            every = jnp.concatenate([b.astype(jnp.bfloat16) for b in blocks])
            total = lax.psum_scatter(
                every, MESH_AXES, scatter_dimension=0, tiled=True, axis_index_groups=self.same_plane
            )
            return total.astype(jnp.float32)
        own, by_x, by_y, corner = blocks
        half = own.shape[0] // 2
        top = self.swap(corner[:half], 2).astype(jnp.float32)
        bottom = self.swap(corner[half:], 4).astype(jnp.float32)
        by_y = jnp.concatenate([by_y[:half] + top, by_y[half:]]).astype(jnp.bfloat16)
        by_x = jnp.concatenate([by_x[:half], by_x[half:] + bottom]).astype(jnp.bfloat16)
        return (
            own.astype(jnp.float32)
            + self.swap(by_x, 2).astype(jnp.float32)
            + self.swap(by_y, 4).astype(jnp.float32)
        )

    def plane_counts(self, counts, cap):
        if self.planes != 4:
            return jnp.full((self.planes,), cap, jnp.int32)
        at = [((self.t_at ^ d) * 2 + self.core_at) * self.n + self.z_at for d in range(4)]
        return counts[jnp.stack(at)]

    def trade_columns(self, pieces):
        came = jnp.zeros_like(pieces)
        for d in range(self.planes):
            piece = lax.dynamic_index_in_dim(pieces, self.t_at ^ d, 0)
            if d:
                piece = self.swap(piece, 2 * d)
            came = lax.dynamic_update_slice(came, piece, (self.t_at ^ d, 0, 0))
        return came

    def gather_first(self, qkv, out, gateup, down, gains, count):
        rows = qkv.shape[0]
        low = jnp.bfloat16
        if self.planes == 4 and self.n > 1:
            digits = jnp.stack([count // 16, count % 16]).astype(low)
            ext = jnp.concatenate([gains.reshape(1, 2 * rows), jnp.zeros((15, 2 * rows), gains.dtype)])
            ext = lax.dynamic_update_slice(ext, digits[None], (1, 0))
            qkv_all, out_all, ext_all, came, down_all = gather_first(
                qkv, out, gateup, down, ext, self.planes, self.n
            )
            ext_all = ext_all.reshape(self.wide * self.n, 16, 2 * rows)
            gain_full = ext_all[:, 0].reshape(-1, 2, rows).transpose(1, 0, 2).reshape(2, -1)
            digits = ext_all[:, 1, :2].astype(jnp.int32)
            return (
                qkv_all.reshape(self.wide * self.n * rows, -1),
                out_all,
                came,
                down_all.reshape(-1, down.shape[1]),
                gain_full,
                digits[:, 0] * 16 + digits[:, 1],
            )
        return (
            lax.all_gather(qkv.astype(low), MESH_AXES, axis=0, tiled=True),
            lax.all_gather(out.astype(low), MESH_AXES, axis=0, tiled=True),
            self.trade_columns(split_columns(gateup.astype(low), self.planes)),
            lax.all_gather(
                down.astype(low), MESH_AXES, axis=0, tiled=True, axis_index_groups=self.same_chip
            ),
            lax.all_gather(gains, MESH_AXES, axis=1, tiled=True),
            lax.all_gather(count, MESH_AXES),
        )


def dot32(a, b):
    return jnp.dot(a, b, preferred_element_type=jnp.float32)


def dot_low(a, b):
    return jnp.dot(a, b, preferred_element_type=jnp.float32).astype(jnp.bfloat16)


def together(arrays):
    return arrays[0] if len(arrays) == 1 else jnp.concatenate(arrays)


def split_columns(shard, planes):
    units = FF // planes
    found = []
    for t in range(planes):
        for low, high in unit_groups(units):
            for start in (t * units, FF + t * units):
                found.append(shard[:, start + low : start + high])
    return jnp.concatenate(found, axis=1).reshape(shard.shape[0], planes, 2 * units).transpose(1, 0, 2)


def join_columns(pieces):
    planes, _, cols = pieces.shape
    gates, uppers = [], []
    for t in range(planes):
        for low, high in unit_groups(cols // 2):
            gates.append(pieces[t, :, 2 * low : low + high])
            uppers.append(pieces[t, :, low + high : 2 * high])
    return jnp.concatenate(gates + uppers, axis=1)


def pick_live(mask, cap):
    flat = mask.reshape(-1)
    rows = flat.shape[0]
    at = jnp.arange(rows, dtype=jnp.int32)
    rank = jnp.sum(jnp.where(at[None, :] <= at[:, None], flat[None, :], 0), axis=1) - 1
    slot = jnp.arange(cap, dtype=jnp.int32)
    chosen = (rank[None, :] == slot[:, None]) & (flat[None, :] == 1)
    return chosen, slot < jnp.sum(flat)


def layer(links, cap, given):
    (
        tokens,
        active,
        cotangent,
        gain_full,
        counts,
        qkv_low,
        out_all,
        pieces,
        down_low,
    ) = given
    n, planes = links.n, links.planes
    seq_count, span_len, width = tokens.shape
    row_count = seq_count * span_len
    seq_len = n * span_len
    kv_width = KV_HEADS * HEAD_DIM
    ff_part = FF // planes
    shard_rows = pieces.shape[1]
    low = jnp.bfloat16


    def codes_of(block):
        mask = lax.dynamic_slice_in_dim(active, jnp.maximum(block, 0) * span_len, span_len, 1)
        chosen, live = pick_live(mask, cap)
        code = jnp.arange(seq_count, dtype=jnp.int32)[:, None] * seq_len + jnp.arange(span_len, dtype=jnp.int32)
        code = jnp.sum(jnp.where(chosen, code.reshape(1, -1), 0), axis=1) + block * span_len
        return chosen, live & (block >= 0), code

    chosen, live, own_code = codes_of(links.z_at)
    key_codes = []
    for r in range(n):
        _, there, code = codes_of(links.z_at - r)
        key_codes.append(jnp.where(there, code, seq_count * seq_len))
    key_code = jnp.concatenate(key_codes)[:, None]
    query_code = jnp.where(live, own_code, -1)[None]
    query_base = jnp.where(live, own_code // seq_len * seq_len, 0)[None]
    places = jnp.where(live, own_code % seq_len, 0).astype(jnp.float32)
    cosine_table, sine_table = rotary_tables(places)
    picker = chosen.astype(low)
    live_rows = live.astype(jnp.float32)[:, None]

    inputs = dot32(picker, tokens.reshape(row_count, width))
    down_grad = dot_low(picker, cotangent.reshape(row_count, width))
    upstream = down_grad.astype(jnp.float32)
    down_grad_blocks = links.gather_tokens(down_grad)

    normed, inverse_one = norm_forward(inputs, gain_full[0])
    normed_low = normed.astype(low)
    kv_part = dot32(normed_low, qkv_low[:, width:])
    kv_low = jnp.concatenate(
        [rotate_heads(kv_part[:, :kv_width], cosine_table, sine_table), kv_part[:, kv_width:]], axis=1
    ).astype(low)
    query_low = rotate_heads(dot32(normed_low, qkv_low[:, :width]), cosine_table, sine_table).astype(low)
    ids = 1 if cap < row_count else 3
    codes = (key_code, query_code, query_base)
    if out_all.ndim == 2:
        out_low = out_all
        attended_low, totals, kv_all = attend(query_low, kv_low, *codes, n, ids)
    else:
        attended_low, totals, kv_all, out_all = attend(query_low, kv_low, *codes, n, ids, out_all)
        out_low = out_all.reshape(width, width)
    pieces, attended_low = lax.optimization_barrier((pieces, attended_low))
    gateup_low = lax.all_gather(
        pieces, MESH_AXES, axis=1, tiled=True, axis_index_groups=links.same_chip
    ).reshape(width, 2 * ff_part)
    middle = inputs + live_rows * dot32(attended_low, out_low)
    normed_mid, inverse_two = norm_forward(middle, gain_full[1])
    blocks = links.gather_tokens(normed_mid.astype(low))
    lives = links.plane_counts(counts, cap)

    parts = [[k] for k in range(planes)] if planes != 4 else [[0], [1, 2], [3]]
    hidden_blocks, gateup_grad_blocks, mid_terms = [], [], [None] * planes
    row_parts, grad_parts = [], []
    for part in parts:
        rows = together([blocks[k] for k in part])
        grads = together([down_grad_blocks[k] for k in part])
        row_parts.append(rows)
        grad_parts.append(grads)
        hidden, gateup_grad, back = mlp_block(rows, grads, lives[jnp.array(part)], gateup_low, down_low, cap)
        hidden_blocks.append(hidden)
        gateup_grad_blocks.append(gateup_grad)
        for i, k in enumerate(part):
            mid_terms[k] = back[i * cap : (i + 1) * cap]
    grad_normed_mid = links.scatter_tokens(mid_terms)
    hidden_all = jnp.concatenate(hidden_blocks)

    term_down = dot_low(hidden_all.T, jnp.concatenate(grad_parts))
    term_gateup = dot_low(jnp.concatenate(row_parts).T, jnp.concatenate(gateup_grad_blocks))
    down_half = links.scatter_core(term_down.reshape(1, 2, ff_part // 2, width))[0]
    gateup_half = links.scatter_core(term_gateup.reshape(planes, 2, n * shard_rows, 2 * ff_part))
    grad_down = lax.psum_scatter(down_half, "narrow", scatter_dimension=0, tiled=True)
    grad_pieces = lax.psum_scatter(gateup_half, "narrow", scatter_dimension=1, tiled=True)
    down_terms = dot_low(hidden_all, down_low)
    order = [k for part in parts for k in part]
    down_terms = {k: down_terms[i * cap : (i + 1) * cap] for i, k in enumerate(order)}
    down_proj = links.scatter_tokens([down_terms[k] for k in range(planes)])
    layer_out = (middle + down_proj).astype(low)

    grad_middle = upstream + norm_backward(middle, inverse_two, gain_full[1], grad_normed_mid)
    branch_grad_low = grad_middle.astype(low)
    branch_grad_low, down_half, gateup_half = lax.optimization_barrier(
        (branch_grad_low, down_half, gateup_half)
    )
    grad_attended_low = dot_low(branch_grad_low, out_low.T)
    grad_out = links.scatter_rows(dot_low(attended_low.T, branch_grad_low))
    inner = jnp.sum(
        (grad_attended_low.astype(jnp.float32) * attended_low.astype(jnp.float32)).reshape(
            cap, HEADS, HEAD_DIM
        ),
        axis=-1,
    )
    inner = inner.T.reshape(KV_HEADS, GROUP, cap)
    grad_query, grad_kv = attend_back(
        query_low, kv_all, grad_attended_low, totals, inner, *codes, n, ids + 1
    )
    grad_query_low = rotate_heads(grad_query, cosine_table, -sine_table).astype(low)
    grad_q_rows = links.scatter_rows(dot_low(normed_low.T, grad_query_low))
    grad_kv_low = jnp.concatenate(
        [rotate_heads(grad_kv[:, :kv_width], cosine_table, -sine_table), grad_kv[:, kv_width:]], axis=1
    ).astype(low)
    grad_kv_rows = links.scatter_rows(dot_low(normed_low.T, grad_kv_low))
    grad_normed = dot32(grad_query_low, qkv_low[:, :width].T) + dot32(grad_kv_low, qkv_low[:, width:].T)
    grad_tokens = (
        grad_middle + norm_backward(inputs, inverse_one, gain_full[0], grad_normed)
    ).astype(low)

    def spread(packed, skipped):
        back = lax.dot_general(
            picker, packed, (((0,), (0,)), ((), ())), preferred_element_type=jnp.float32
        ).astype(low)
        mask = lax.dynamic_slice_in_dim(active, links.z_at * span_len, span_len, 1)
        return jnp.where(mask[:, :, None] == 1, back.reshape(skipped.shape), skipped)

    layer_out, grad_tokens = spread(layer_out, tokens), spread(grad_tokens, cotangent)
    grad_gateup = join_columns(links.trade_columns(grad_pieces))
    grad_qkv = jnp.concatenate([grad_q_rows, grad_kv_rows], axis=1)
    return layer_out, grad_tokens, grad_qkv, grad_out, grad_gateup, grad_down


def on_device(
    tokens,
    active,
    cotangent,
    gain_rows,
    w_qkv,
    w_out,
    w_gateup,
    w_down,
    moment_gains,
    moment_qkv,
    moment_out,
    moment_gateup,
    moment_down,
    average_gains,
    average_qkv,
    average_out,
    average_gateup,
    average_down,
):
    links = Links()
    seq_count, span_len, _ = tokens.shape
    row_count = seq_count * span_len
    low = jnp.bfloat16

    gains_low = gain_rows.astype(low)
    own_mask = lax.dynamic_slice_in_dim(active, links.z_at * span_len, span_len, 1)
    qkv_low, out_all, pieces, down_low, gain_full, counts = links.gather_first(
        w_qkv, w_out, w_gateup, w_down, gains_low, jnp.sum(own_mask)
    )
    gain_full = gain_full.astype(jnp.float32)
    given = (tokens, active, cotangent, gain_full, counts, qkv_low, out_all, pieces, down_low)
    few = -(-3 * row_count // 4 // 128) * 128
    if few < row_count:
        found = lax.cond(
            jnp.max(counts) <= few,
            lambda *g: layer(links, few, g),
            lambda *g: layer(links, row_count, g),
            *given,
        )
    else:
        found = layer(links, row_count, given)
    layer_out, grad_tokens, grad_qkv, grad_out, grad_gateup, grad_down = found
    grad_qkv, grad_out, grad_gateup, grad_down = (
        g.astype(jnp.float32) for g in (grad_qkv, grad_out, grad_gateup, grad_down)
    )

    def gain_grad(shard, gradient, row):
        return jnp.sum(shard.astype(low).astype(jnp.float32) * gradient, axis=1) / gains_low[row].astype(jnp.float32)

    grad_gains = jnp.stack([gain_grad(w_qkv, grad_qkv, 0), gain_grad(w_gateup, grad_gateup, 1)])
    state_gains = advance_state(gain_rows, moment_gains, average_gains, grad_gains)
    state_qkv = advance_state(w_qkv, moment_qkv, average_qkv, grad_qkv)
    state_out = advance_state(w_out, moment_out, average_out, grad_out)
    state_gateup = advance_state(w_gateup, moment_gateup, average_gateup, grad_gateup)
    state_down = advance_state(w_down, moment_down, average_down, grad_down)
    return (
        layer_out,
        grad_tokens,
        grad_gains,
        grad_qkv,
        grad_out,
        grad_gateup,
        grad_down,
        state_gains[0],
        state_qkv[0],
        state_out[0],
        state_gateup[0],
        state_down[0],
        state_gains[1],
        state_qkv[1],
        state_out[1],
        state_gateup[1],
        state_down[1],
        state_gains[2],
        state_qkv[2],
        state_out[2],
        state_gateup[2],
        state_down[2],
    )


def solution(mesh):
    in_specs = (
        P("wide", "narrow", None),
        P("wide", None),
        P("wide", "narrow", None),
        P(None, ("wide", "narrow")),
        P(("wide", "narrow"), None),
        P(("wide", "narrow"), None),
        P(("wide", "narrow"), None),
        P(("wide", "narrow"), None),
        P(None, ("wide", "narrow")),
        P(("wide", "narrow"), None),
        P(("wide", "narrow"), None),
        P(("wide", "narrow"), None),
        P(("wide", "narrow"), None),
        P(None, ("wide", "narrow")),
        P(("wide", "narrow"), None),
        P(("wide", "narrow"), None),
        P(("wide", "narrow"), None),
        P(("wide", "narrow"), None),
    )
    out_specs = (
        P("wide", "narrow", None),
        P("wide", "narrow", None),
        P(None, ("wide", "narrow")),
        P(("wide", "narrow"), None),
        P(("wide", "narrow"), None),
        P(("wide", "narrow"), None),
        P(("wide", "narrow"), None),
        P(None, ("wide", "narrow")),
        P(("wide", "narrow"), None),
        P(("wide", "narrow"), None),
        P(("wide", "narrow"), None),
        P(("wide", "narrow"), None),
        P(None, ("wide", "narrow")),
        P(("wide", "narrow"), None),
        P(("wide", "narrow"), None),
        P(("wide", "narrow"), None),
        P(("wide", "narrow"), None),
        P(None, ("wide", "narrow")),
        P(("wide", "narrow"), None),
        P(("wide", "narrow"), None),
        P(("wide", "narrow"), None),
        P(("wide", "narrow"), None),
    )
    return jax.shard_map(
        on_device, mesh=mesh, in_specs=in_specs, out_specs=out_specs, check_vma=False
    )
```

```python
import functools

import jax
import jax.numpy as jnp
from jax import lax
from jax.experimental import pallas as pl
from jax.experimental.pallas import tpu as pltpu
from jax.sharding import PartitionSpec as P

HEADS = 16
KV_HEADS = 4
HEAD_DIM = 128
GROUP = HEADS // KV_HEADS
FF = 5632


EPSILON = 1e-05
MOMENTUM = 0.5
AVERAGING = 0.5
STEP_RATE = 0.0003

MESH = pl.DeviceIdType.MESH
MESH_AXES = ("wide", "narrow")
SCORE_SCALE = HEAD_DIM ** (-0.5)
LOG2_E = 1.4426950408889634
MASKED = -1e30


def dot_nt(a, b):
    return lax.dot_general(a, b, (((1,), (1,)), ((), ())), preferred_element_type=jnp.float32)


def dot_tn(a, b):
    return lax.dot_general(a, b, (((0,), (0,)), ((), ())), preferred_element_type=jnp.float32)


UNIT_GROUP = 256
WIDTH_GROUP = 256


def unit_groups(units):
    return [(low, min(low + UNIT_GROUP, units)) for low in range(0, units, UNIT_GROUP)]


def mlp_kernel(
    cap, counts, live_ref, rows_ref, grad_ref, gateup_first, gateup_last, down_hbm,
    hidden_ref, gateup_grad_ref, back_ref, gateup_ref, down_ref, gateup_sems, down_sems,
):
    step = pl.program_id(0)
    width = rows_ref.shape[1]
    units = down_ref.shape[0]
    full, rest = units // UNIT_GROUP, units % UNIT_GROUP
    live = live_ref[step]

    def span(low, size):
        return pl.ds(low if isinstance(low, int) else pl.multiple_of(low, size), size)

    def gateup_part(k, low, size, to=None):
        both = span(2 * low, 2 * size)
        into = both if to is None else span(2 * to, 2 * size)
        first = gateup_first.shape[1]
        held = gateup_first.at[:, both] if 2 * low < first else gateup_last.at[:, span(2 * low - first, 2 * size)]
        return pltpu.make_async_copy(held, gateup_ref.at[:, into], gateup_sems.at[k])

    def down_part(k, low, size):
        one = span(low, size)
        return pltpu.make_async_copy(down_hbm.at[one, :], down_ref.at[one, :], down_sems.at[k])

    @pl.when(step == 0)
    def _():
        for k, (low, high) in enumerate(unit_groups(units)):
            gateup_part(k, low, high - low).start()
            down_part(k, low, high - low).start()

    def run(count):
        def units_step(k, low, size):
            @pl.when(step == 0)
            def _():
                gateup_part(k, 0 if size == UNIT_GROUP else low, size, low).wait()
                down_part(k, low, size).wait()

            both, one = span(2 * low, 2 * size), span(low, size)
            gate_up = jnp.dot(rows_ref[:count, :], gateup_ref[:, both], preferred_element_type=jnp.float32)
            gate, upper = gate_up[:, :size], gate_up[:, size:]
            grad_hidden = dot_nt(grad_ref[:count, :], down_ref[one, :])
            sigmoid = 1.0 / (1.0 + jnp.exp(-gate))
            silu = gate * sigmoid
            hidden_ref[:count, one] = (silu * upper).astype(jnp.bfloat16)
            grad_gate = grad_hidden * upper * (sigmoid + silu * (1.0 - sigmoid))
            grad_upper = grad_hidden * silu
            gateup_grad_ref[:count, both] = jnp.concatenate([grad_gate, grad_upper], axis=1).astype(jnp.bfloat16)

        lax.fori_loop(0, full, lambda k, c: (units_step(k, k * UNIT_GROUP, UNIT_GROUP), c)[1], 0)
        if rest:
            units_step(full, full * UNIT_GROUP, rest)

        def back_step(k, carry):
            at = span(k * WIDTH_GROUP, WIDTH_GROUP)
            back_ref[:count, at] = dot_nt(gateup_grad_ref[:count, :], gateup_ref[at, :]).astype(jnp.bfloat16)
            return carry

        lax.fori_loop(0, width // WIDTH_GROUP, back_step, 0)
        if count < cap:
            for ref in (hidden_ref, gateup_grad_ref, back_ref):
                ref[count:, :] = jnp.zeros((cap - count, ref.shape[1]), ref.dtype)

    for low, count in zip((None,) + counts[:-1], counts):
        chosen = live > (-1 if low is None else low)
        if count < cap:
            chosen &= live <= count

        @pl.when(chosen)
        def _(count=count):
            run(count)


def mlp_block(rows, grad, live, gateup_first, gateup_last, down, cap):
    blocks = rows.shape[0] // cap
    width = rows.shape[1]
    units = down.shape[0]
    if units % 128 or cap % 128:
        return mlp_plain(rows, grad, jnp.concatenate([gateup_first, gateup_last], axis=1), down)
    gateup_cols = gateup_first.shape[1] + gateup_last.shape[1]
    counts = (192, 256, 320, 384) if cap == 384 else tuple(range(256, cap, 256)) + (cap,)
    groups = len(unit_groups(units))
    low = jnp.bfloat16
    by_block = lambda cols: pl.BlockSpec((cap, cols), lambda b, live: (b, 0))
    return pl.pallas_call(
        functools.partial(mlp_kernel, cap, counts),
        grid_spec=pltpu.PrefetchScalarGridSpec(
            num_scalar_prefetch=1,
            grid=(blocks,),
            in_specs=[by_block(width), by_block(width)] + [pl.BlockSpec(memory_space=pl.ANY)] * 3,
            out_specs=(by_block(units), by_block(2 * units), by_block(width)),
            scratch_shapes=[
                pltpu.VMEM((width, gateup_cols), low),
                pltpu.VMEM(down.shape, low),
                pltpu.SemaphoreType.DMA((groups,)),
                pltpu.SemaphoreType.DMA((groups,)),
            ],
        ),
        out_shape=(
            jax.ShapeDtypeStruct((blocks * cap, units), low),
            jax.ShapeDtypeStruct((blocks * cap, 2 * units), low),
            jax.ShapeDtypeStruct((blocks * cap, width), low),
        ),
        compiler_params=pltpu.CompilerParams(vmem_limit_bytes=56 * 1024 * 1024),
        cost_estimate=pl.CostEstimate(
            flops=10 * blocks * cap * width * units,
            bytes_accessed=2 * (width * gateup_cols + down.size) + 12 * blocks * cap * width,
            transcendentals=blocks * cap * units,
        ),
        name="mlp_block",
    )(live, rows, grad, gateup_first, gateup_last, down)


def mlp_plain(rows, grad, gateup, down):
    groups = unit_groups(down.shape[0])
    gate_up = jnp.dot(rows, gateup, preferred_element_type=jnp.float32)
    gate = jnp.concatenate([gate_up[:, 2 * low : low + high] for low, high in groups], axis=1)
    upper = jnp.concatenate([gate_up[:, low + high : 2 * high] for low, high in groups], axis=1)
    grad_hidden = jnp.dot(grad, down.T, preferred_element_type=jnp.float32)
    sigmoid = jax.nn.sigmoid(gate)
    silu = gate * sigmoid
    hidden = (silu * upper).astype(jnp.bfloat16)
    grad_gate = grad_hidden * upper * (sigmoid + silu * (1.0 - sigmoid))
    grad_upper = grad_hidden * silu
    gateup_grad = jnp.concatenate(
        [part[:, low:high] for low, high in groups for part in (grad_gate, grad_upper)], axis=1
    ).astype(jnp.bfloat16)
    back = jnp.dot(gateup_grad, gateup.T, preferred_element_type=jnp.float32).astype(jnp.bfloat16)
    return hidden, gateup_grad, back


class Place:
    def __init__(self, n):
        self.n = n
        self.wide = lax.axis_index("wide")
        self.z = lax.axis_index("narrow")
        self.t, self.core = self.wide // 2, self.wide % 2
        self.t_x, self.t_y, self.t_d = self.t ^ 1, self.t ^ 2, self.t ^ 3
        self.by_x = self.device(self.t_x)
        self.by_y = self.device(self.t_y)
        self.by_d = self.device(self.t_d)
        self.sibling = self.device(self.t, core=1 - self.core)
        self.above = self.device(self.t, z=jnp.minimum(self.z + 1, n - 1))
        self.below = self.device(self.t, z=jnp.maximum(self.z - 1, 0))

    def device(self, t, core=None, z=None):
        return (t * 2 + (self.core if core is None else core), self.z if z is None else z)

    def greet(self, others):
        barrier = pltpu.get_barrier_semaphore()
        for other in others:
            pl.semaphore_signal(barrier, inc=1, device_id=other, device_id_type=MESH)

        @pl.when(self.z > 0)
        def _():
            pl.semaphore_signal(barrier, inc=1, device_id=self.below, device_id_type=MESH)

        @pl.when(self.z < self.n - 1)
        def _():
            pl.semaphore_signal(barrier, inc=1, device_id=self.above, device_id_type=MESH)

        inner = (self.z > 0).astype(jnp.int32) + (self.z < self.n - 1).astype(jnp.int32)
        pl.semaphore_wait(barrier, len(others) + inner)


class Copies:
    def __init__(self, send_sems, recv_sems):
        self.send_sems, self.recv_sems = send_sems, recv_sems
        self.count = 0
        self.started = []

    def make(self, src, dst, to):
        k = self.count
        self.count += 1
        return pltpu.make_async_remote_copy(
            src_ref=src, dst_ref=dst, send_sem=self.send_sems.at[k], recv_sem=self.recv_sems.at[k],
            device_id=to, device_id_type=MESH,
        )

    def same(self, ref, to):
        return self.make(ref, ref, to)

    def each(self, moves, when, act):
        def run():
            for m in moves:
                act(m)

        if when is None:
            run()
        else:
            pl.when(when)(run)

    def go(self, moves, when=None):
        self.each(moves, when, lambda m: m.start())
        self.started.append((moves, when))

    def arrive(self, moves, when=None):
        self.each(moves, when, lambda m: m.wait_recv())

    def end(self):
        for moves, when in self.started:
            self.each(moves, when, lambda m: m.wait_send())


class LineGather:
    def __init__(self, place, copies, view, own):
        self.place, self.copies, self.view, self.own = place, copies, view, own
        self.up, self.down = {}, {}

    def send(self, step):
        p, last = self.place, self.place.n - 1
        block = self.view(jnp.maximum(p.z - (step - 1), 0))
        self.up[step] = self.copies.make(self.own if step == 1 else block, block, p.above)
        self.copies.go([self.up[step]], (p.z - (step - 1) >= 0) & (p.z < last))
        block = self.view(jnp.minimum(p.z + (step - 1), last))
        self.down[step] = self.copies.make(self.own if step == 1 else block, block, p.below)
        self.copies.go([self.down[step]], (p.z + (step - 1) <= last) & (p.z > 0))

    def take(self, step):
        p = self.place
        self.copies.arrive([self.up[step]], p.z - step >= 0)
        self.copies.arrive([self.down[step]], p.z + step <= p.n - 1)

    def hand_over(self, step):
        p, last = self.place, self.place.n - 1
        moves = []
        for at, there in ((p.z - step, p.z - step >= 0), (p.z + step, p.z + step <= last)):
            block = self.view(jnp.clip(at, 0, last))
            move = self.copies.same(block, p.sibling)
            self.copies.go([move], there)
            moves.append(([move], there))
        return moves


def gather_kernel(
    n, qkv_ref, out_ref, gateup_ref, down_ref, ext_ref, qkv_all, out_all, ext_all, came, down_all,
    qkv_low, out_low, trade_low, down_low, send_sems, recv_sems, local_sems,
):
    p = Place(n)
    c = Copies(send_sems, recv_sems)
    t, core, z = p.t, p.core, p.z
    low = jnp.bfloat16
    qkv_low[...] = qkv_ref[...].astype(low)
    p.greet([p.by_x, p.by_y, p.by_d, p.sibling])

    half = qkv_ref.shape[1] // 256 * 128
    qa, qb = slice(0, half), slice(half, qkv_ref.shape[1])
    lines = [
        LineGather(p, c, lambda zz, cols=cols: qkv_all.at[t, core, zz, :, cols], qkv_low.at[:, cols])
        for cols in (qa, qb)
    ]
    lines.append(LineGather(p, c, lambda zz: ext_all.at[t, core, zz], ext_ref))
    for line in lines:
        line.send(1)
    local = []

    def place(src, dst):
        move = pltpu.make_async_copy(src, dst, local_sems.at[len(local)])
        move.start()
        local.append(move)

    place(qkv_low, qkv_all.at[t, core, z])
    place(ext_ref, ext_all.at[t, core, z])
    units = trade_low.shape[2] // 2
    for k in range(trade_low.shape[0]):
        for first, last in unit_groups(units):
            for to, start in ((2 * first, k * units), (first + last, gateup_ref.shape[1] // 2 + k * units)):
                trade_low[k, :, to : to + last - first] = gateup_ref[:, start + first : start + last].astype(low)
    place(trade_low.at[t], came.at[t])
    trade = [
        c.make(trade_low.at[k], came.at[t], to) for k, to in ((p.t_x, p.by_x), (p.t_y, p.by_y), (p.t_d, p.by_d))
    ]
    c.go(trade)
    out_low[...] = out_ref[...].astype(low)
    down_low[...] = down_ref[...].astype(low)
    place(out_low, out_all.at[t, core, z])
    place(down_low, down_all.at[core, z])
    line_out = LineGather(p, c, lambda zz: out_all.at[t, core, zz], out_low)
    line_down = LineGather(p, c, lambda zz: down_all.at[core, zz], down_low)
    down_own = c.make(down_low, down_all.at[core, z], p.sibling)
    c.go([down_own])
    handed = [([down_own], None)]
    for step in range(1, n):
        for line in lines:
            line.take(step)
            if step < n - 1:
                line.send(step + 1)
    for move in local:
        move.wait()
    a_y = c.same(qkv_all.at[t, core, :, :, qa], p.by_y)
    b_x = c.same(qkv_all.at[t, core, :, :, qb], p.by_x)
    e_x = c.same(ext_all.at[t, core], p.by_x)
    c.go([a_y, b_x, e_x])
    line_down.send(1)
    line_out.send(1)
    own = [c.same(qkv_all.at[t, core], p.sibling), c.same(ext_all.at[t, core], p.sibling)]
    c.go(own)
    c.arrive([e_x])
    e_y = [c.same(ext_all.at[k, core], p.by_y) for k in (t, p.t_x)]
    c.go(e_y)
    c.arrive([a_y])
    a_x = [c.same(qkv_all.at[k, core, :, :, qa], p.by_x) for k in (t, p.t_y)]
    c.go(a_x)
    c.arrive([b_x])
    b_y = [c.same(qkv_all.at[k, core, :, :, qb], p.by_y) for k in (t, p.t_x)]
    c.go(b_y)
    near = [
        c.same(qkv_all.at[p.t_y, core, :, :, qa], p.sibling),
        c.same(qkv_all.at[p.t_x, core, :, :, qb], p.sibling),
        c.same(ext_all.at[p.t_x, core], p.sibling),
    ]
    c.go(near)
    c.arrive(e_y)
    far = [c.same(ext_all.at[k, core], p.sibling) for k in (p.t_y, p.t_d)]
    c.go(far)
    for step in range(1, n):
        for line in (line_down, line_out):
            line.take(step)
            if step < n - 1:
                line.send(step + 1)
        handed += line_down.hand_over(step)
        if step == max(n - 2, 1):
            c.arrive(a_x)
            c.arrive(b_y)
            last = [c.same(qkv_all.at[k, core, :, :, qa], p.sibling) for k in (p.t_x, p.t_d)]
            last += [c.same(qkv_all.at[k, core, :, :, qb], p.sibling) for k in (p.t_y, p.t_d)]
            c.go(last)
    c.arrive(trade + own + near + far + last)
    for moves, when in handed:
        c.arrive(moves, when)
    c.end()


def gather_first(qkv, out, gateup, down, ext, planes, n):
    any_spec = pl.BlockSpec(memory_space=pl.ANY)
    rows = qkv.shape[0]
    part = gateup.shape[1] // planes
    low = jnp.bfloat16
    copies = 64
    return pl.pallas_call(
        functools.partial(gather_kernel, n),
        out_shape=(
            jax.ShapeDtypeStruct((planes, 2, n, rows, qkv.shape[1]), low),
            jax.ShapeDtypeStruct((planes, 2, n, rows, out.shape[1]), low),
            jax.ShapeDtypeStruct((planes, 2, n) + ext.shape, low),
            jax.ShapeDtypeStruct((planes, rows, part), low),
            jax.ShapeDtypeStruct((2, n) + down.shape, low),
        ),
        in_specs=[pl.BlockSpec(memory_space=pltpu.VMEM)] * 5,
        out_specs=(any_spec,) * 5,
        scratch_shapes=[
            pltpu.VMEM(qkv.shape, low),
            pltpu.VMEM(out.shape, low),
            pltpu.VMEM((planes, rows, part), low),
            pltpu.VMEM(down.shape, low),
            pltpu.SemaphoreType.DMA((copies,)),
            pltpu.SemaphoreType.DMA((copies,)),
            pltpu.SemaphoreType.DMA((8,)),
        ],
        compiler_params=pltpu.CompilerParams(
            collective_id=0, has_side_effects=True, vmem_limit_bytes=32 * 1024 * 1024
        ),
        name="gather_first",
    )(qkv, out, gateup, down, ext)


class PlaneScatter:
    def __init__(self, place, copies, left, right, parts, turned, leaving, came, total, first, second):
        self.p, self.c, self.left, self.right, self.parts = place, copies, left, right, parts
        self.turned, self.leaving, self.came, self.total = turned, leaving, came, total
        self.first, self.second = first, second
        self.moves = {}

    def turn(self):
        rows = self.turned.shape[1]

        def one(k, carry):
            self.turned[k] = self.left[:, pl.ds(pl.multiple_of(k * rows, rows), rows)].T
            return carry

        lax.fori_loop(0, self.turned.shape[0], one, 0)

    def at(self, part):
        low, high, _ = self.parts[part]
        return slice(low, high)

    def begin(self, part):
        p, cols = self.p, self.at(part)
        right = self.right[:, cols]

        def terms(into, core):
            def one(t, carry):
                term = jnp.dot(self.turned[t * 2 + core], right, preferred_element_type=jnp.float32)
                into[t, :, cols] = term.astype(jnp.bfloat16)
                return carry

            lax.fori_loop(0, into.shape[0], one, 0)

        terms(self.leaving, 1 - p.core)
        self.moves[part, 0] = [self.c.make(self.leaving.at[:, :, cols], self.came.at[:, :, cols], p.sibling)]
        self.c.go(self.moves[part, 0])
        terms(self.total, p.core)

    def add(self, t, cols, came):
        both = self.total[t, :, cols].astype(jnp.float32) + came.astype(jnp.float32)
        self.total[t, :, cols] = both.astype(jnp.bfloat16)

    def across_first(self, part):
        p, c, cols = self.p, self.c, self.at(part)
        c.arrive(self.moves[part, 0])

        def one(t, carry):
            self.add(t, cols, self.came[t, :, cols])
            return carry

        lax.fori_loop(0, self.total.shape[0], one, 0)
        near, to = (p.t_x, p.by_x) if self.parts[part][2] else (p.t_y, p.by_y)
        self.moves[part, 1] = [
            c.make(self.total.at[t, :, cols], self.first.at[k, :, cols], to) for k, t in enumerate((near, p.t_d))
        ]
        c.go(self.moves[part, 1])

    def across_second(self, part):
        p, c, cols = self.p, self.c, self.at(part)
        c.arrive(self.moves[part, 1])
        near, to = (p.t_y, p.by_y) if self.parts[part][2] else (p.t_x, p.by_x)
        self.add(near, cols, self.first[1, :, cols])
        self.moves[part, 2] = [c.make(self.total.at[near, :, cols], self.second.at[:, cols], to)]
        c.go(self.moves[part, 2])
        self.add(p.t, cols, self.first[0, :, cols])

    def end(self, part):
        cols = self.at(part)
        self.c.arrive(self.moves[part, 2])
        self.add(self.p.t, cols, self.second[:, cols])


class LineScatter:
    def __init__(self, place, copies, read, cols, up_leaving, up_came, down_leaving, down_came):
        self.p, self.c, self.read, self.cols = place, copies, read, cols
        self.ways = ((up_leaving, up_came, place.above), (down_leaving, down_came, place.below))
        self.rows = up_came.shape[1]
        self.moves = []

    def block(self, d):
        at = pl.ds(pl.multiple_of(jnp.clip(d, 0, self.p.n - 1) * self.rows, self.rows), self.rows)
        return self.read(at, self.cols).astype(jnp.float32)

    def step(self, s):
        p, c, n, cols = self.p, self.c, self.p.n, self.cols
        self.take()
        self.moves = []
        for way, (leaving, came, to) in enumerate(self.ways):
            behind = p.z if way == 0 else n - 1 - p.z
            block = n - s + p.z if way == 0 else p.z - (n - s)
            sends = (behind <= s - 1) & (behind < n - 1)

            @pl.when(sends & (behind == 0) if s > 1 else sends)
            def _():
                leaving[s - 1, :, cols] = self.block(block).astype(jnp.bfloat16)

            if s > 1:
                @pl.when(sends & (behind > 0))
                def _():
                    both = self.block(block) + came[s - 2, :, cols].astype(jnp.float32)
                    leaving[s - 1, :, cols] = both.astype(jnp.bfloat16)

            move = c.make(leaving.at[s - 1, :, cols], came.at[s - 1, :, cols], to)
            c.go([move], sends)
            self.moves.append((move, (behind >= 1) & (behind <= s)))

    def take(self):
        for move, when in self.moves:
            self.c.arrive([move], when)

    def end(self, out_ref):
        p, n, cols = self.p, self.p.n, self.cols
        self.take()
        up_came, down_came = self.ways[0][1], self.ways[1][1]
        own = self.block(p.z)

        @pl.when(p.z == 0)
        def _():
            out_ref[:, cols] = own + down_came[n - 2, :, cols].astype(jnp.float32)

        @pl.when(p.z == n - 1)
        def _():
            out_ref[:, cols] = own + up_came[n - 2, :, cols].astype(jnp.float32)

        @pl.when((p.z > 0) & (p.z < n - 1))
        def _():
            out_ref[:, cols] = own + (
                up_came[n - 2, :, cols].astype(jnp.float32) + down_came[n - 2, :, cols].astype(jnp.float32)
            )


def plane_parts(cols, count):
    edges = [cols // 128 * k // count * 128 for k in range(count + 1)]
    return [(low, high, k % 2 == 0) for k, (low, high) in enumerate(zip(edges[:-1], edges[1:]))]


def plane_scratch(rows, width, cols, planes):
    low = jnp.bfloat16
    line = width // planes // 2
    return [
        pltpu.VMEM((planes * 2, line, rows), low),
        pltpu.VMEM((planes, line, cols), low),
        pltpu.VMEM((planes, line, cols), low),
        pltpu.VMEM((planes, line, cols), low),
        pltpu.VMEM((2, line, cols), low),
        pltpu.VMEM((line, cols), low),
    ]


def qkv_back_kernel(
    n, parts, normed_ref, grad_ref, weights_hbm, pieces_ref, out_sum, sum_ref, back_ref, gateup_ref, out_ref, weights,
    traded, turned, leaving, came, total, first, second, up_leaving, up_came, down_leaving, down_came, out_up_leaving,
    out_up_came, out_down_leaving, out_down_came, send_sems, recv_sems, load_sem,
):
    p = Place(n)
    c = Copies(send_sems, recv_sems)
    held = weights.shape[0]

    def load(k):
        return pltpu.make_async_copy(weights_hbm.at[k * held : (k + 1) * held], weights, load_sem)

    load(0).start()
    p.greet([p.by_x, p.by_y, p.by_d, p.sibling])
    trade = [
        c.make(pieces_ref.at[k], traded.at[p.t], to) for k, to in ((p.t_x, p.by_x), (p.t_y, p.by_y), (p.t_d, p.by_d))
    ]
    c.go(trade)
    traded[p.t] = pieces_ref[p.t]
    out_line = LineScatter(
        p, c, lambda at, cols: out_sum[at, cols], slice(None), out_up_leaving, out_up_came, out_down_leaving, out_down_came
    )
    out_line.step(1)
    scatter = PlaneScatter(p, c, normed_ref, grad_ref, parts, turned, leaving, came, total, first, second)
    every = range(len(parts))
    scatter.turn()
    for k in every:
        scatter.begin(k)
    chunk = 2 * HEAD_DIM

    def back(half):
        load(half).wait()

        def one(k, carry):
            at = pl.ds(pl.multiple_of(k * chunk, chunk), chunk)
            to = pl.ds(pl.multiple_of(half * held + k * chunk, chunk), chunk)
            back_ref[:, to] = dot_nt(grad_ref[...], weights[at, :])
            return carry

        lax.fori_loop(0, held // chunk, one, 0)

    for k in every:
        scatter.across_first(k)
    if n > 2:
        out_line.step(2)
    back(0)
    load(1).start()
    c.arrive(trade)
    units = traded.shape[2] // 2
    for k in range(traded.shape[0]):
        for low, high in unit_groups(units):
            for at, start in ((2 * low, k * units), (low + high, gateup_ref.shape[1] // 2 + k * units)):
                columns = traded[k, :, at : at + high - low]
                gateup_ref[:, start + low : start + high] = columns.astype(jnp.float32)
    for s in range(3, n):
        out_line.step(s)
    for k in every:
        scatter.across_second(k)
    back(1)
    lines = [
        LineScatter(
            p, c, lambda at, cols: total[p.t, at, cols], scatter.at(k), up_leaving, up_came, down_leaving, down_came
        )
        for k in every
    ]
    for k in every:
        scatter.end(k)
        lines[k].step(1)
    for s in range(2, n):
        for line in lines:
            line.step(s)
    out_line.end(out_ref)
    for line in lines:
        line.end(sum_ref)
    c.end()


def qkv_back(normed, grad, weights, pieces, out_sum, planes, n, collective_id):
    rows, width = normed.shape
    cols = grad.shape[1]
    parts = plane_parts(cols, 4)
    in_vmem = pl.BlockSpec(memory_space=pltpu.VMEM)
    low = jnp.bfloat16
    line = pltpu.VMEM((n - 1, width // planes // 2 // n, cols), low)
    out_line = pltpu.VMEM((n - 1, out_sum.shape[0] // n, out_sum.shape[1]), low)
    copies = len(parts) * (4 + 2 * n) + 2 * n + 4
    return pl.pallas_call(
        functools.partial(qkv_back_kernel, n, parts),
        in_specs=[in_vmem, in_vmem, pl.BlockSpec(memory_space=pl.ANY), in_vmem, in_vmem],
        out_specs=(in_vmem,) * 4,
        out_shape=(
            jax.ShapeDtypeStruct((width // planes // 2 // n, cols), jnp.float32),
            jax.ShapeDtypeStruct((rows, width), jnp.float32),
            jax.ShapeDtypeStruct((pieces.shape[1], planes * pieces.shape[2]), jnp.float32),
            jax.ShapeDtypeStruct((out_sum.shape[0] // n, out_sum.shape[1]), jnp.float32),
        ),
        scratch_shapes=[pltpu.VMEM((weights.shape[0] // 2, cols), low), pltpu.VMEM(pieces.shape, low)]
        + plane_scratch(rows, width, cols, planes)
        + [line] * 4
        + [out_line] * 4
        + [pltpu.SemaphoreType.DMA((copies,)), pltpu.SemaphoreType.DMA((copies,)), pltpu.SemaphoreType.DMA],
        compiler_params=pltpu.CompilerParams(
            vmem_limit_bytes=60 * 1024 * 1024, collective_id=collective_id, has_side_effects=True
        ),
        cost_estimate=pl.CostEstimate(
            flops=48 * rows * width * cols, bytes_accessed=2 * weights.size + 8 * rows * width, transcendentals=0
        ),
        name="qkv_back",
    )(normed, grad, weights, pieces, out_sum)


def fill_bias(r, key_code, query_code, query_base, bias):
    rows = bias.shape[0]
    code = key_code[r * rows : (r + 1) * rows, :]
    seen = (code <= query_code[...]) & (code >= query_base[...])
    bias[...] = jnp.where(seen, 0.0, MASKED)


class PlaneGather:
    def __init__(self, place, copies, whole):
        self.p, self.c, self.whole = place, copies, whole
        cols = whole.shape[-1]
        self.a, self.b = slice(0, cols // 2), slice(cols // 2, cols)

    def block(self, t, cols=slice(None)):
        return self.whole.at[t, self.p.core, :, :, cols]

    def begin(self):
        p, c = self.p, self.c
        self.a_y, self.b_x = c.same(self.block(p.t, self.a), p.by_y), c.same(self.block(p.t, self.b), p.by_x)
        self.over = [c.same(self.block(p.t), p.sibling)]
        c.go([self.a_y, self.b_x] + self.over)

    def middle(self):
        p, c = self.p, self.c
        c.arrive([self.a_y, self.b_x])
        self.a_x = [c.same(self.block(k, self.a), p.by_x) for k in (p.t, p.t_y)]
        self.b_y = [c.same(self.block(k, self.b), p.by_y) for k in (p.t, p.t_x)]
        near = [c.same(self.block(p.t_y, self.a), p.sibling), c.same(self.block(p.t_x, self.b), p.sibling)]
        c.go(self.a_x + self.b_y + near)
        self.over += near

    def end(self):
        p, c = self.p, self.c
        c.arrive(self.a_x + self.b_y)
        far = [c.same(self.block(k, self.a), p.sibling) for k in (p.t_x, p.t_d)]
        far += [c.same(self.block(k, self.b), p.sibling) for k in (p.t_y, p.t_d)]
        c.go(far)
        c.arrive(self.over + far)


def attend_kernel(n, with_out, *refs):
    inputs_ref, gain_ref, cosine, sine, weights_hbm, key_code, query_code, query_base = refs[:8]
    refs = refs[8:]
    if with_out:
        (own_grad, _), refs = refs[:2], refs[2:]
    (normed_ref, inverse_ref, q_ref, o_ref, total_ref, kv_all), refs = refs[:6], refs[6:]
    if with_out:
        (out_all, grad_x, grad_y, grad_d), refs = refs[:4], refs[4:]
    weights, peak_now, total_now, mixed_now, bias, send_sems, recv_sems, load_sems = refs
    p = Place(n)
    c = Copies(send_sems, recv_sems)
    z = p.z
    rows, width = q_ref.shape
    values_at = KV_HEADS * HEAD_DIM
    pair = 2 * HEAD_DIM
    slot = lambda r: kv_all.at[r * rows : (r + 1) * rows, :]
    loads = [
        pltpu.make_async_copy(weights_hbm.at[:, cols], weights.at[:, cols], load_sems.at[k])
        for k, cols in enumerate((slice(width, weights.shape[1]), slice(0, width)))
    ]
    for load in loads:
        load.start()
    p.greet([p.by_x, p.by_y, p.sibling] if with_out else [])
    if with_out:
        half = rows // 2
        near = [c.make(own_grad, grad_x, p.by_x), c.make(own_grad, grad_y, p.by_y)]
        out_plane = PlaneGather(p, c, out_all)
        out_plane.begin()
        c.go(near)
    inputs = inputs_ref[...]
    inverse = lax.rsqrt(jnp.mean(inputs * inputs, axis=1, keepdims=True) + EPSILON)
    inverse_ref[...] = inverse
    normed_ref[...] = (inputs * inverse * gain_ref[...]).astype(jnp.bfloat16)

    def project(low, into, to, turned):
        at = pl.ds(pl.multiple_of(low, pair), pair)
        both = jnp.dot(normed_ref[...], weights[:, at], preferred_element_type=jnp.float32)
        for k in range(2):
            head = both[:, k * HEAD_DIM : (k + 1) * HEAD_DIM]
            if turned:
                head = head * cosine[...] + pltpu.roll(head, HEAD_DIM // 2, 1) * sine[...]
            lanes = pl.ds(pl.multiple_of(to + k * HEAD_DIM, HEAD_DIM), HEAD_DIM)
            into[:rows, lanes] = head.astype(jnp.bfloat16)

    def project_all(start, count, into, to, turned):
        def one(k, carry):
            project(start + k * pair, into, to + k * pair, turned)
            return carry

        lax.fori_loop(0, count // pair, one, 0)

    loads[0].wait()
    project_all(width, values_at, kv_all, 0, True)
    project_all(width + values_at, values_at, kv_all, values_at, False)
    copies = [c.make(slot(r), slot(r + 1), p.above) for r in range(n - 1)]
    if copies:
        c.go([copies[0]], z < n - 1)
    for r in range(1, n):
        @pl.when(z < r)
        def _(r=r):
            kv_all[r * rows : (r + 1) * rows, :] = jnp.zeros((rows, kv_all.shape[1]), kv_all.dtype)

    loads[1].wait()
    project_all(0, width, q_ref, 0, True)

    def block(r):
        fill_bias(r, key_code, query_code, query_base, bias)
        at = slice(r * rows, (r + 1) * rows)

        def group(g, carry):
            keys = kv_all[at, pl.ds(pl.multiple_of(g * HEAD_DIM, HEAD_DIM), HEAD_DIM)]
            values = kv_all[at, pl.ds(pl.multiple_of(values_at + g * HEAD_DIM, HEAD_DIM), HEAD_DIM)]
            hidden = bias[...]
            for h in range(GROUP):
                lanes = pl.ds(pl.multiple_of((g * GROUP + h) * HEAD_DIM, HEAD_DIM), HEAD_DIM)
                scores = dot_nt(keys, q_ref[:, lanes]) * (SCORE_SCALE * LOG2_E) + hidden
                peak = jnp.max(scores, axis=0, keepdims=True)
                if r:
                    before = peak_now[g, h : h + 1, :]
                    peak = jnp.maximum(peak, before)
                weights = jnp.exp2(scores - peak)
                total = jnp.sum(weights, axis=0, keepdims=True)
                mixed = dot_tn(values, weights.astype(jnp.bfloat16))
                if r:
                    shrink = jnp.exp2(before - peak)
                    total = total + total_now[g, h : h + 1, :] * shrink
                    mixed = mixed + mixed_now[g, h] * shrink
                peak_now[g, h : h + 1, :] = peak
                total_now[g, h : h + 1, :] = total
                mixed_now[g, h] = mixed
            return carry

        lax.fori_loop(0, KV_HEADS, group, 0)

    block(0)
    for r in range(1, n):
        c.arrive([copies[r - 1]], z >= r)
        if r < n - 1:
            c.go([copies[r]], (z >= r) & (z < n - 1))
        if with_out and r == 1:
            out_plane.middle()
        if with_out and r == max(n - 2, 1):
            c.arrive(near)
            corners = [
                c.make(grad_y.at[:half], grad_d.at[:half], p.by_x),
                c.make(grad_x.at[half:], grad_d.at[half:], p.by_y),
            ]
            c.go(corners)
        if with_out and r == n - 1:
            out_plane.end()

        @pl.when(z >= r)
        def _(r=r):
            block(r)

    def finish(g, carry):
        for h in range(GROUP):
            lanes = pl.ds(pl.multiple_of((g * GROUP + h) * HEAD_DIM, HEAD_DIM), HEAD_DIM)
            total = total_now[g, h : h + 1, :]
            o_ref[:, lanes] = (mixed_now[g, h] / total).T.astype(jnp.bfloat16)
            total_ref[g, h : h + 1, :] = peak_now[g, h : h + 1, :] + jnp.log2(total)
        return carry

    lax.fori_loop(0, KV_HEADS, finish, 0)
    if with_out:
        c.arrive(corners)
    c.end()


def attend(
    inputs, gain, cosine, sine, weights, key_code, query_code, query_base, n, collective_id, down_grad=None, out_all=None
):
    rows, width = inputs.shape
    kv_cols = weights.shape[1] - width
    low = jnp.bfloat16
    in_vmem = pl.BlockSpec(memory_space=pltpu.VMEM)
    any_spec = pl.BlockSpec(memory_space=pl.ANY)
    given = [] if out_all is None else [down_grad, out_all]
    more = [] if out_all is None else [out_all] + [down_grad] * 3
    copies = n + 24
    return pl.pallas_call(
        functools.partial(attend_kernel, n, out_all is not None),
        in_specs=[in_vmem] * 4 + [any_spec] + [in_vmem] * 3 + [any_spec] * len(given),
        out_specs=(in_vmem,) * 6 + (any_spec,) * len(more),
        input_output_aliases={9: 6} if given else {},
        out_shape=(
            jax.ShapeDtypeStruct((rows, width), low),
            jax.ShapeDtypeStruct((rows, 1), jnp.float32),
            jax.ShapeDtypeStruct((rows, width), low),
            jax.ShapeDtypeStruct((rows, width), low),
            jax.ShapeDtypeStruct((KV_HEADS, GROUP, rows), jnp.float32),
            jax.ShapeDtypeStruct((n * rows, kv_cols), low),
        )
        + tuple(jax.ShapeDtypeStruct(o.shape, o.dtype) for o in more),
        scratch_shapes=[
            pltpu.VMEM(weights.shape, low),
            pltpu.VMEM((KV_HEADS, GROUP, rows), jnp.float32),
            pltpu.VMEM((KV_HEADS, GROUP, rows), jnp.float32),
            pltpu.VMEM((KV_HEADS, GROUP, HEAD_DIM, rows), jnp.float32),
            pltpu.VMEM((rows, rows), jnp.float32),
            pltpu.SemaphoreType.DMA((copies,)),
            pltpu.SemaphoreType.DMA((copies,)),
            pltpu.SemaphoreType.DMA((2,)),
        ],
        compiler_params=pltpu.CompilerParams(
            vmem_limit_bytes=52 * 1024 * 1024, collective_id=collective_id, has_side_effects=True
        ),
        cost_estimate=pl.CostEstimate(
            flops=64 * rows * n * rows * width, bytes_accessed=8 * rows * width, transcendentals=HEADS * rows * n * rows
        ),
        name="attend",
    )(inputs, gain, cosine, sine, weights, key_code, query_code, query_base, *given)


def attend_back_kernel(n, parts, *refs):
    q_ref, kv_all, do_ref, total_ref, mixed_ref, key_code, query_code, query_base, cosine, sine = refs[:10]
    refs = refs[10:]
    if parts:
        branch_ref, refs = refs[0], refs[1:]
    grad_ref, refs = refs[0], refs[1:]
    if parts:
        out_sum, refs = refs[0], refs[1:]
    dq_now, dkv_now, bias, inner_now, leaving, came, send_sems, recv_sems = refs[:8]
    p = Place(n)
    c = Copies(send_sems, recv_sems)
    z = p.z
    rows = q_ref.shape[0]
    values_at = KV_HEADS * HEAD_DIM
    p.greet([p.by_x, p.by_y, p.sibling] if parts else [])
    every = range(len(parts))
    if parts:
        scatter = PlaneScatter(p, c, mixed_ref, branch_ref, parts, *refs[8:])
    copies = {r: c.make(leaving.at[r - 1], came.at[r - 1], p.below) for r in range(1, n)}
    dq_now[...] = jnp.zeros_like(dq_now)
    q_cols = HEADS * HEAD_DIM

    def turned_back(head):
        return head * cosine[...] - pltpu.roll(head, HEAD_DIM // 2, 1) * sine[...]

    def put(low, head):
        grad_ref[:, low : low + HEAD_DIM] = head.astype(jnp.bfloat16)

    def block(r):
        fill_bias(r, key_code, query_code, query_base, bias)
        at = slice(r * rows, (r + 1) * rows)

        def group(g, carry):
            key_lanes = pl.ds(pl.multiple_of(g * HEAD_DIM, HEAD_DIM), HEAD_DIM)
            value_lanes = pl.ds(pl.multiple_of(values_at + g * HEAD_DIM, HEAD_DIM), HEAD_DIM)
            keys, values, hidden = kv_all[at, key_lanes], kv_all[at, value_lanes], bias[...]
            dk = dv = None
            for h in range(GROUP):
                lanes = pl.ds(pl.multiple_of((g * GROUP + h) * HEAD_DIM, HEAD_DIM), HEAD_DIM)
                query, grad = q_ref[:, lanes], do_ref[:, lanes]
                scores = dot_nt(keys, query) * (SCORE_SCALE * LOG2_E) + hidden
                weights = jnp.exp2(scores - total_ref[g, h : h + 1, :])
                grad_weights = dot_nt(values, grad)
                grad_scores = (weights * (grad_weights - inner_now[g, h : h + 1, :])).astype(jnp.bfloat16)
                dv_term = jnp.dot(weights.astype(jnp.bfloat16), grad, preferred_element_type=jnp.float32)
                dk_term = jnp.dot(grad_scores, query, preferred_element_type=jnp.float32)
                dv = dv_term if dv is None else dv + dv_term
                dk = dk_term if dk is None else dk + dk_term
                dq_now[g, h] += dot_tn(keys, grad_scores)
            dkv_now[:, key_lanes] = dk * SCORE_SCALE
            dkv_now[:, value_lanes] = dv
            return carry

        lax.fori_loop(0, KV_HEADS, group, 0)

    def inner_of(g, carry):
        for h in range(GROUP):
            lanes = pl.ds(pl.multiple_of((g * GROUP + h) * HEAD_DIM, HEAD_DIM), HEAD_DIM)
            both = do_ref[:, lanes].astype(jnp.float32) * mixed_ref[:, lanes].astype(jnp.float32)
            inner_now[g, h : h + 1, :] = jnp.sum(both.T, axis=0, keepdims=True)
        return carry

    lax.fori_loop(0, KV_HEADS, inner_of, 0)
    for r in range(n - 1, -1, -1):
        @pl.when(z >= r)
        def _(r=r):
            block(r)
            if r < n - 1:
                @pl.when(z < n - 1)
                def _():
                    copies[r + 1].wait_recv()
                    dkv_now[...] += came[r].astype(jnp.float32)
            if r:
                leaving[r - 1] = dkv_now[...].astype(jnp.bfloat16)
                copies[r].start()
            else:
                for g in range(KV_HEADS):
                    put(q_cols + g * HEAD_DIM, turned_back(dkv_now[:, g * HEAD_DIM : (g + 1) * HEAD_DIM]))
                grad_ref[:, q_cols + values_at :] = dkv_now[:, values_at:].astype(jnp.bfloat16)

        if parts and r == n - 1:
            scatter.turn()
            for k in every:
                scatter.begin(k)
        if parts and r == max(n - 2, 0):
            for k in every:
                scatter.across_first(k)
        if parts and r == max(n - 3, 0):
            for k in every:
                scatter.across_second(k)
    if parts:
        for k in every:
            scatter.end(k)
        out_sum[...] = scatter.total[p.t]

    def finish(g, carry):
        for h in range(GROUP):
            lanes = pl.ds(pl.multiple_of((g * GROUP + h) * HEAD_DIM, HEAD_DIM), HEAD_DIM)
            grad_ref[:, lanes] = turned_back(dq_now[g, h].T * SCORE_SCALE).astype(jnp.bfloat16)
        return carry

    lax.fori_loop(0, KV_HEADS, finish, 0)
    for r in range(1, n):
        @pl.when(z >= r)
        def _(r=r):
            copies[r].wait_send()
    c.end()


def attend_back(
    query, kv_all, grad, total, mixed, key_code, query_code, query_base, cosine, sine, n, collective_id, branch_grad=None,
    planes=0,
):
    rows, width = query.shape
    kv_cols = kv_all.shape[1]
    in_vmem = pl.BlockSpec(memory_space=pltpu.VMEM)
    slots = max(n - 1, 1)
    more, parts, shapes, scratch = (), [], (), []
    if branch_grad is not None:
        more, parts = (branch_grad,), plane_parts(width, 2)
        shapes = (jax.ShapeDtypeStruct((width // planes // 2, width), jnp.bfloat16),)
        scratch = plane_scratch(rows, width, width, planes)
    copies = n + 4 * len(parts)
    return pl.pallas_call(
        functools.partial(attend_back_kernel, n, parts),
        in_specs=[in_vmem] * (10 + len(more)),
        out_specs=(in_vmem,) * (1 + len(shapes)),
        out_shape=(jax.ShapeDtypeStruct((rows, width + kv_cols), jnp.bfloat16),) + shapes,
        scratch_shapes=[
            pltpu.VMEM((KV_HEADS, GROUP, HEAD_DIM, rows), jnp.float32),
            pltpu.VMEM((rows, kv_cols), jnp.float32),
            pltpu.VMEM((rows, rows), jnp.float32),
            pltpu.VMEM((KV_HEADS, GROUP, rows), jnp.float32),
            pltpu.VMEM((slots, rows, kv_cols), jnp.bfloat16),
            pltpu.VMEM((slots, rows, kv_cols), jnp.bfloat16),
            pltpu.SemaphoreType.DMA((copies,)),
            pltpu.SemaphoreType.DMA((copies,)),
        ]
        + scratch,
        compiler_params=pltpu.CompilerParams(
            vmem_limit_bytes=60 * 1024 * 1024, collective_id=collective_id, has_side_effects=True
        ),
        cost_estimate=pl.CostEstimate(
            flops=72 * rows * n * rows * width, bytes_accessed=16 * rows * width, transcendentals=HEADS * rows * n * rows
        ),
        name="attend_back",
    )(query, kv_all, grad, total, mixed, key_code, query_code, query_base, cosine, sine, *more)


def rotary_tables(positions):
    half_dim = HEAD_DIM // 2
    frequency = jnp.power(10000.0, -2.0 * jnp.arange(half_dim, dtype=jnp.float32) / HEAD_DIM)
    angles = positions[:, None] * frequency[None, :]
    return (jnp.cos(angles), jnp.sin(angles))


def norm_forward(values_in, gain_row):
    inverse = lax.rsqrt(jnp.mean(values_in * values_in, axis=-1, keepdims=True) + EPSILON)
    return (values_in * inverse * gain_row, inverse)


def norm_backward(values_in, inverse, gain_row, incoming):
    scaled_grad = incoming * gain_row
    return inverse * scaled_grad - values_in * inverse * inverse * inverse * jnp.mean(
        scaled_grad * values_in, axis=-1, keepdims=True
    )


def advance_state(weight, moment, average, gradient):
    moment_next = MOMENTUM * moment + gradient
    weight_next = weight - STEP_RATE * (gradient + MOMENTUM * moment_next)
    average_next = AVERAGING * average + (1.0 - AVERAGING) * weight_next
    return (weight_next, moment_next, average_next)


class Links:
    def __init__(self):
        self.wide = lax.axis_size("wide")
        self.n = lax.axis_size("narrow")
        self.planes = self.wide // 2
        self.wide_at = lax.axis_index("wide")
        self.z_at = lax.axis_index("narrow")
        self.t_at = self.wide_at // 2
        self.core_at = self.wide_at % 2
        self.bits = [1 << k for k in range(self.planes.bit_length() - 1)]
        per_chip = 2 * self.n
        self.same_chip = [[t * per_chip + j for j in range(per_chip)] for t in range(self.planes)]
        self.same_plane = [
            [t * per_chip + j for t in range(self.planes)] for j in range(per_chip)
        ]

    def swap(self, values, flip):
        pairs = [(i, i ^ (flip * self.n)) for i in range(self.wide * self.n)]
        return lax.ppermute(values, MESH_AXES, pairs)

    def column_cuts(self, cols):
        lanes = cols // 128
        count = len(self.bits)
        edges = [128 * (lanes * k // count) for k in range(count + 1)]
        orders = [self.bits[k:] + self.bits[:k] for k in range(count)]
        return list(zip(edges[:-1], edges[1:], orders))

    def scatter_core(self, term):
        mine = lax.dynamic_index_in_dim(term, self.core_at, 1, keepdims=False)
        other = lax.dynamic_index_in_dim(term, 1 - self.core_at, 1, keepdims=False)
        got = self.swap(other, 1)
        return (mine.astype(jnp.float32) + got.astype(jnp.float32)).astype(jnp.bfloat16)

    def scatter_rows(self, term):
        rows, cols = term.shape
        term = term.reshape(self.planes, 2, rows // self.wide, cols)
        term = self.scatter_core(term)
        parts = []
        for low, high, order in self.column_cuts(cols):
            part = term[:, :, low:high]
            left = sorted(self.bits, reverse=True)
            part = part.reshape((2,) * len(left) + part.shape[1:])
            for bit in order:
                axis = left.index(bit)
                my_bit = (self.t_at // bit) % 2
                mine = lax.dynamic_index_in_dim(part, my_bit, axis, keepdims=False)
                other = lax.dynamic_index_in_dim(part, 1 - my_bit, axis, keepdims=False)
                got = self.swap(other, 2 * bit)
                part = (mine.astype(jnp.float32) + got.astype(jnp.float32)).astype(jnp.bfloat16)
                left.remove(bit)
            parts.append(part)
        total = jnp.concatenate(parts, axis=1)
        return lax.psum_scatter(total, "narrow", scatter_dimension=0, tiled=True)

    def gather_tokens(self, rows):
        if self.planes != 4:
            every = lax.all_gather(
                rows, MESH_AXES, axis=0, tiled=False, axis_index_groups=self.same_plane
            )
            return [every[k] for k in range(self.planes)]
        half = rows.shape[0] // 2
        by_x = self.swap(rows, 2)
        by_y = self.swap(rows, 4)
        corner = [self.swap(by_y[:half], 2), self.swap(by_x[half:], 4)]
        return [rows, by_x, by_y, jnp.concatenate(corner)]

    def scatter_far(self, blocks):
        if self.planes != 4:
            return jnp.concatenate([b.astype(jnp.bfloat16) for b in blocks]), None, None
        own, by_x, by_y, corner = blocks
        half = own.shape[0] // 2
        top = self.swap(corner[:half], 2).astype(jnp.float32)
        bottom = self.swap(corner[half:], 4).astype(jnp.float32)
        by_y = jnp.concatenate([by_y[:half] + top, by_y[half:]]).astype(jnp.bfloat16)
        by_x = jnp.concatenate([by_x[:half], by_x[half:] + bottom]).astype(jnp.bfloat16)
        return own, by_x, by_y

    def scatter_near(self, own, by_x, by_y):
        if self.planes != 4:
            total = lax.psum_scatter(
                own, MESH_AXES, scatter_dimension=0, tiled=True, axis_index_groups=self.same_plane
            )
            return total, None, None
        return own, self.swap(by_x, 2), self.swap(by_y, 4)

    def scatter_sum(self, own, came_x, came_y):
        if came_x is None:
            return own.astype(jnp.float32)
        return own.astype(jnp.float32) + came_x.astype(jnp.float32) + came_y.astype(jnp.float32)

    def gather_chip(self, pieces):
        every = lax.all_gather(pieces, MESH_AXES, axis=1, tiled=True, axis_index_groups=self.same_chip)
        return every.reshape(-1, every.shape[-1])

    def plane_counts(self, counts, cap):
        if self.planes != 4:
            return jnp.full((self.planes,), cap, jnp.int32)
        at = [((self.t_at ^ d) * 2 + self.core_at) * self.n + self.z_at for d in range(4)]
        return counts[jnp.stack(at)]

    def trade_columns(self, pieces):
        came = jnp.zeros_like(pieces)
        for d in range(self.planes):
            piece = lax.dynamic_index_in_dim(pieces, self.t_at ^ d, 0)
            if d:
                piece = self.swap(piece, 2 * d)
            came = lax.dynamic_update_slice(came, piece, (self.t_at ^ d, 0, 0))
        return came

    def gather_first(self, qkv, out, gateup, down, gains, count):
        rows = qkv.shape[0]
        low = jnp.bfloat16
        if self.planes == 4 and self.n > 1:
            digits = jnp.stack([count // 16, count % 16]).astype(low)
            ext = jnp.concatenate([gains.reshape(1, 2 * rows), jnp.zeros((15, 2 * rows), gains.dtype)])
            ext = lax.dynamic_update_slice(ext, digits[None], (1, 0))
            qkv_all, out_all, ext_all, came, down_all = gather_first(
                qkv, out, gateup, down, ext, self.planes, self.n
            )
            ext_all = ext_all.reshape(self.wide * self.n, 16, 2 * rows)
            gain_full = ext_all[:, 0].reshape(-1, 2, rows).transpose(1, 0, 2).reshape(2, -1)
            digits = ext_all[:, 1, :2].astype(jnp.int32)
            return (
                qkv_all.reshape(self.wide * self.n * rows, -1),
                out_all,
                came,
                down_all.reshape(-1, down.shape[1]),
                gain_full,
                digits[:, 0] * 16 + digits[:, 1],
            )
        return (
            lax.all_gather(qkv.astype(low), MESH_AXES, axis=0, tiled=True),
            lax.all_gather(out.astype(low), MESH_AXES, axis=0, tiled=True),
            self.trade_columns(split_columns(gateup.astype(low), self.planes)),
            lax.all_gather(
                down.astype(low), MESH_AXES, axis=0, tiled=True, axis_index_groups=self.same_chip
            ),
            lax.all_gather(gains, MESH_AXES, axis=1, tiled=True),
            lax.all_gather(count, MESH_AXES),
        )


def dot32(a, b):
    return jnp.dot(a, b, preferred_element_type=jnp.float32)


def dot_low(a, b):
    return jnp.dot(a, b, preferred_element_type=jnp.float32).astype(jnp.bfloat16)


def together(arrays):
    return arrays[0] if len(arrays) == 1 else jnp.concatenate(arrays)


def split_columns(shard, planes):
    units = FF // planes
    found = []
    for t in range(planes):
        for low, high in unit_groups(units):
            for start in (t * units, FF + t * units):
                found.append(shard[:, start + low : start + high])
    return jnp.concatenate(found, axis=1).reshape(shard.shape[0], planes, 2 * units).transpose(1, 0, 2)


def join_columns(pieces):
    planes, _, cols = pieces.shape
    gates, uppers = [], []
    for t in range(planes):
        for low, high in unit_groups(cols // 2):
            gates.append(pieces[t, :, 2 * low : low + high])
            uppers.append(pieces[t, :, low + high : 2 * high])
    return jnp.concatenate(gates + uppers, axis=1)


def pick_live(mask, cap):
    flat = mask.reshape(-1)
    rows = flat.shape[0]
    at = jnp.arange(rows, dtype=jnp.int32)
    rank = jnp.sum(jnp.where(at[None, :] <= at[:, None], flat[None, :], 0), axis=1) - 1
    slot = jnp.arange(cap, dtype=jnp.int32)
    chosen = (rank[None, :] == slot[:, None]) & (flat[None, :] == 1)
    return chosen, slot < jnp.sum(flat)


def layer(links, cap, given):
    (
        tokens,
        active,
        cotangent,
        gain_full,
        counts,
        qkv_low,
        out_all,
        pieces,
        down_low,
    ) = given
    n, planes = links.n, links.planes
    seq_count, span_len, width = tokens.shape
    row_count = seq_count * span_len
    seq_len = n * span_len
    kv_width = KV_HEADS * HEAD_DIM
    ff_part = FF // planes
    shard_rows = pieces.shape[1]
    low = jnp.bfloat16


    first_cols = 2 * UNIT_GROUP * max(ff_part // UNIT_GROUP * 2 // 5, 1)
    gateup_first = links.gather_chip(pieces[:, :, :first_cols])

    def codes_of(block):
        mask = lax.dynamic_slice_in_dim(active, jnp.maximum(block, 0) * span_len, span_len, 1)
        chosen, live = pick_live(mask, cap)
        code = jnp.arange(seq_count, dtype=jnp.int32)[:, None] * seq_len + jnp.arange(span_len, dtype=jnp.int32)
        code = jnp.sum(jnp.where(chosen, code.reshape(1, -1), 0), axis=1) + block * span_len
        return chosen, live & (block >= 0), code

    chosen, live, own_code = codes_of(links.z_at)
    key_codes = []
    for r in range(n):
        _, there, code = codes_of(links.z_at - r)
        key_codes.append(jnp.where(there, code, seq_count * seq_len))
    key_code = jnp.concatenate(key_codes)[:, None]
    query_code = jnp.where(live, own_code, -1)[None]
    query_base = jnp.where(live, own_code // seq_len * seq_len, 0)[None]
    places = jnp.where(live, own_code % seq_len, 0).astype(jnp.float32)
    cosine_table, sine_table = rotary_tables(places)
    picker = chosen.astype(low)
    live_rows = live.astype(jnp.float32)[:, None]

    inputs = dot32(picker, tokens.reshape(row_count, width))
    down_grad = dot_low(picker, cotangent.reshape(row_count, width))
    upstream = down_grad.astype(jnp.float32)

    cosine = jnp.concatenate([cosine_table, cosine_table], axis=1)
    sine = jnp.concatenate([-sine_table, sine_table], axis=1)
    ids = 1 if cap < row_count else 3
    codes = (key_code, query_code, query_base)
    first = (inputs, gain_full[:1], cosine, sine, qkv_low, *codes, n, ids)
    if out_all.ndim == 2:
        out_low = out_all
        normed_low, inverse_one, query_low, attended_low, totals, kv_all = attend(*first)
        down_grad_blocks = links.gather_tokens(down_grad)
    else:
        normed_low, inverse_one, query_low, attended_low, totals, kv_all, out_all, *others = attend(
            *first, down_grad, out_all
        )
        down_grad_blocks = [down_grad, *others]
        out_low = out_all.reshape(width, width)
    pieces_last, attended_low = lax.optimization_barrier((pieces[:, :, first_cols:], attended_low))
    gateup_last = links.gather_chip(pieces_last)
    middle = inputs + live_rows * dot32(attended_low, out_low)
    normed_mid, inverse_two = norm_forward(middle, gain_full[1])
    blocks = links.gather_tokens(normed_mid.astype(low))
    lives = links.plane_counts(counts, cap)

    parts = [[k] for k in range(planes)] if planes != 4 else [[0], [1, 2], [3]]
    hidden_blocks, gateup_grad_blocks, mid_terms = [], [], [None] * planes
    row_parts, grad_parts = [], []
    for part in parts:
        rows = together([blocks[k] for k in part])
        grads = together([down_grad_blocks[k] for k in part])
        row_parts.append(rows)
        grad_parts.append(grads)
        hidden, gateup_grad, back = mlp_block(
            rows, grads, lives[jnp.array(part)], gateup_first, gateup_last, down_low, cap
        )
        hidden_blocks.append(hidden)
        gateup_grad_blocks.append(gateup_grad)
        for i, k in enumerate(part):
            mid_terms[k] = back[i * cap : (i + 1) * cap]
    mid_far = links.scatter_far(mid_terms)
    hidden_all, rows_all = jnp.concatenate(hidden_blocks), jnp.concatenate(row_parts)
    grads_all, gateup_grad_all = jnp.concatenate(grad_parts), jnp.concatenate(gateup_grad_blocks)
    mid_far, hidden_all, gateup_grad_all = lax.optimization_barrier((mid_far, hidden_all, gateup_grad_all))
    mid_near = links.scatter_near(*mid_far)
    term_down = dot_low(hidden_all.T, grads_all)
    down_half = links.scatter_core(term_down.reshape(1, 2, ff_part // 2, width))[0]
    grad_down = lax.psum_scatter(down_half, "narrow", scatter_dimension=0, tiled=True)
    term_gateup = dot_low(rows_all.T, gateup_grad_all)
    gateup_half = links.scatter_core(term_gateup.reshape(planes, 2, n * shard_rows, 2 * ff_part))
    gateup_half, grad_down = lax.optimization_barrier((gateup_half, grad_down))
    grad_pieces = lax.psum_scatter(gateup_half, "narrow", scatter_dimension=1, tiled=True)
    down_terms = dot_low(hidden_all, down_low)
    down_terms, mid_near = lax.optimization_barrier((down_terms, mid_near))
    grad_normed_mid = links.scatter_sum(*mid_near)
    order = [k for part in parts for k in part]
    down_terms = {k: down_terms[i * cap : (i + 1) * cap] for i, k in enumerate(order)}
    down_far = links.scatter_far([down_terms[k] for k in range(planes)])

    grad_middle = upstream + norm_backward(middle, inverse_two, gain_full[1], grad_normed_mid)
    branch_grad_low = grad_middle.astype(low)
    branch_grad_low, gateup_half = lax.optimization_barrier((branch_grad_low, gateup_half))
    grad_attended_low = dot_low(branch_grad_low, out_low.T)
    grad_attended_low, down_far = lax.optimization_barrier((grad_attended_low, down_far))
    down_near = links.scatter_near(*down_far)
    back = (query_low, kv_all, grad_attended_low, totals, attended_low, *codes, cosine, sine, n, ids + 1)
    if planes == 4 and n > 1:
        grad_projected_low, out_sum = attend_back(*back, branch_grad_low, planes)
        down_near, grad_projected_low = lax.optimization_barrier((down_near, grad_projected_low))
        grad_qkv, grad_normed, grad_gateup, grad_out = qkv_back(
            normed_low, grad_projected_low, qkv_low, grad_pieces, out_sum, planes, n, ids + 4
        )
    else:
        grad_projected_low = attend_back(*back)[0]
        grad_out = links.scatter_rows(dot_low(attended_low.T, branch_grad_low))
        grad_qkv = links.scatter_rows(dot_low(normed_low.T, grad_projected_low)).astype(jnp.float32)
        grad_normed = dot32(grad_projected_low, qkv_low.T)
        grad_gateup = join_columns(links.trade_columns(grad_pieces)).astype(jnp.float32)
    grad_tokens = (
        grad_middle + norm_backward(inputs, inverse_one, gain_full[0], grad_normed)
    ).astype(low)

    layer_out = (middle + links.scatter_sum(*down_near)).astype(low)

    def spread(packed, skipped):
        back = lax.dot_general(
            picker, packed, (((0,), (0,)), ((), ())), preferred_element_type=jnp.float32
        ).astype(low)
        mask = lax.dynamic_slice_in_dim(active, links.z_at * span_len, span_len, 1)
        return jnp.where(mask[:, :, None] == 1, back.reshape(skipped.shape), skipped)

    layer_out, grad_tokens = spread(layer_out, tokens), spread(grad_tokens, cotangent)
    return layer_out, grad_tokens, grad_qkv, grad_out, grad_gateup, grad_down


def on_device(
    tokens,
    active,
    cotangent,
    gain_rows,
    w_qkv,
    w_out,
    w_gateup,
    w_down,
    moment_gains,
    moment_qkv,
    moment_out,
    moment_gateup,
    moment_down,
    average_gains,
    average_qkv,
    average_out,
    average_gateup,
    average_down,
):
    links = Links()
    seq_count, span_len, _ = tokens.shape
    row_count = seq_count * span_len
    low = jnp.bfloat16

    gains_low = gain_rows.astype(low)
    own_mask = lax.dynamic_slice_in_dim(active, links.z_at * span_len, span_len, 1)
    qkv_low, out_all, pieces, down_low, gain_full, counts = links.gather_first(
        w_qkv, w_out, w_gateup, w_down, gains_low, jnp.sum(own_mask)
    )
    gain_full = gain_full.astype(jnp.float32)
    given = (tokens, active, cotangent, gain_full, counts, qkv_low, out_all, pieces, down_low)
    few = -(-3 * row_count // 4 // 128) * 128
    if few < row_count:
        found = lax.cond(
            jnp.max(counts) <= few,
            lambda *g: layer(links, few, g),
            lambda *g: layer(links, row_count, g),
            *given,
        )
    else:
        found = layer(links, row_count, given)
    layer_out, grad_tokens, grad_qkv, grad_out, grad_gateup, grad_down = found
    grad_qkv, grad_out, grad_gateup, grad_down = (
        g.astype(jnp.float32) for g in (grad_qkv, grad_out, grad_gateup, grad_down)
    )

    def gain_grad(shard, gradient, row):
        return jnp.sum(shard.astype(low).astype(jnp.float32) * gradient, axis=1) / gains_low[row].astype(jnp.float32)

    grad_gains = jnp.stack([gain_grad(w_qkv, grad_qkv, 0), gain_grad(w_gateup, grad_gateup, 1)])
    state_gains = advance_state(gain_rows, moment_gains, average_gains, grad_gains)
    state_qkv = advance_state(w_qkv, moment_qkv, average_qkv, grad_qkv)
    state_out = advance_state(w_out, moment_out, average_out, grad_out)
    state_gateup = advance_state(w_gateup, moment_gateup, average_gateup, grad_gateup)
    state_down = advance_state(w_down, moment_down, average_down, grad_down)
    return (
        layer_out,
        grad_tokens,
        grad_gains,
        grad_qkv,
        grad_out,
        grad_gateup,
        grad_down,
        state_gains[0],
        state_qkv[0],
        state_out[0],
        state_gateup[0],
        state_down[0],
        state_gains[1],
        state_qkv[1],
        state_out[1],
        state_gateup[1],
        state_down[1],
        state_gains[2],
        state_qkv[2],
        state_out[2],
        state_gateup[2],
        state_down[2],
    )


def solution(mesh):
    in_specs = (
        P("wide", "narrow", None),
        P("wide", None),
        P("wide", "narrow", None),
        P(None, ("wide", "narrow")),
        P(("wide", "narrow"), None),
        P(("wide", "narrow"), None),
        P(("wide", "narrow"), None),
        P(("wide", "narrow"), None),
        P(None, ("wide", "narrow")),
        P(("wide", "narrow"), None),
        P(("wide", "narrow"), None),
        P(("wide", "narrow"), None),
        P(("wide", "narrow"), None),
        P(None, ("wide", "narrow")),
        P(("wide", "narrow"), None),
        P(("wide", "narrow"), None),
        P(("wide", "narrow"), None),
        P(("wide", "narrow"), None),
    )
    out_specs = (
        P("wide", "narrow", None),
        P("wide", "narrow", None),
        P(None, ("wide", "narrow")),
        P(("wide", "narrow"), None),
        P(("wide", "narrow"), None),
        P(("wide", "narrow"), None),
        P(("wide", "narrow"), None),
        P(None, ("wide", "narrow")),
        P(("wide", "narrow"), None),
        P(("wide", "narrow"), None),
        P(("wide", "narrow"), None),
        P(("wide", "narrow"), None),
        P(None, ("wide", "narrow")),
        P(("wide", "narrow"), None),
        P(("wide", "narrow"), None),
        P(("wide", "narrow"), None),
        P(("wide", "narrow"), None),
        P(None, ("wide", "narrow")),
        P(("wide", "narrow"), None),
        P(("wide", "narrow"), None),
        P(("wide", "narrow"), None),
        P(("wide", "narrow"), None),
    )
    return jax.shard_map(
        on_device, mesh=mesh, in_specs=in_specs, out_specs=out_specs, check_vma=False
    )
```

```python
import functools

import jax
import jax.numpy as jnp
from jax import lax
from jax.experimental import pallas as pl
from jax.experimental.pallas import tpu as pltpu
from jax.sharding import PartitionSpec as P

HEADS = 16
KV_HEADS = 4
HEAD_DIM = 128
GROUP = HEADS // KV_HEADS
FF = 5632


EPSILON = 1e-05
MOMENTUM = 0.5
AVERAGING = 0.5
STEP_RATE = 0.0003

MESH = pl.DeviceIdType.MESH
MESH_AXES = ("wide", "narrow")
SCORE_SCALE = HEAD_DIM ** (-0.5)
LOG2_E = 1.4426950408889634
MASKED = -1e30


def dot_nt(a, b):
    return lax.dot_general(a, b, (((1,), (1,)), ((), ())), preferred_element_type=jnp.float32)


def dot_tn(a, b):
    return lax.dot_general(a, b, (((0,), (0,)), ((), ())), preferred_element_type=jnp.float32)


UNIT_GROUP = 256
WIDTH_GROUP = 256
LANES = 128


def unit_groups(units):
    return [(low, min(low + UNIT_GROUP, units)) for low in range(0, units, UNIT_GROUP)]


def mlp_kernel(
    cap, counts, live_ref, rows_ref, grad_ref, gateup_first, gateup_last, down_hbm,
    hidden_ref, gateup_grad_ref, back_ref, out_ref, gateup_ref, down_ref, gateup_sems, down_sems,
):
    step = pl.program_id(0)
    width = rows_ref.shape[1]
    units = down_ref.shape[0]
    full, rest = units // UNIT_GROUP, units % UNIT_GROUP
    live = live_ref[step]

    def span(low, size):
        return pl.ds(low if isinstance(low, int) else pl.multiple_of(low, size), size)

    def gateup_part(k, low, size, to=None):
        both = span(2 * low, 2 * size)
        into = both if to is None else span(2 * to, 2 * size)
        first = gateup_first.shape[1]
        held = gateup_first.at[:, both] if 2 * low < first else gateup_last.at[:, span(2 * low - first, 2 * size)]
        return pltpu.make_async_copy(held, gateup_ref.at[:, into], gateup_sems.at[k])

    def down_part(k, low, size):
        one = span(low, size)
        return pltpu.make_async_copy(down_hbm.at[one, :], down_ref.at[one, :], down_sems.at[k])

    @pl.when(step == 0)
    def _():
        for k, (low, high) in enumerate(unit_groups(units)):
            gateup_part(k, low, high - low).start()
            down_part(k, low, high - low).start()

    def run(count):
        def units_step(k, low, size):
            @pl.when(step == 0)
            def _():
                gateup_part(k, 0 if size == UNIT_GROUP else low, size, low).wait()
                down_part(k, low, size).wait()

            both, one = span(2 * low, 2 * size), span(low, size)
            gate_up = jnp.dot(rows_ref[:count, :], gateup_ref[:, both], preferred_element_type=jnp.float32)
            gate, upper = gate_up[:, :size], gate_up[:, size:]
            grad_hidden = dot_nt(grad_ref[:count, :], down_ref[one, :])
            sigmoid = 1.0 / (1.0 + jnp.exp(-gate))
            silu = gate * sigmoid
            hidden_ref[:count, one] = (silu * upper).astype(jnp.bfloat16)
            grad_gate = grad_hidden * upper * (sigmoid + silu * (1.0 - sigmoid))
            grad_upper = grad_hidden * silu
            gateup_grad_ref[:count, both] = jnp.concatenate([grad_gate, grad_upper], axis=1).astype(jnp.bfloat16)

        lax.fori_loop(0, full, lambda k, c: (units_step(k, k * UNIT_GROUP, UNIT_GROUP), c)[1], 0)
        if rest:
            units_step(full, full * UNIT_GROUP, rest)

        def back_step(k, carry):
            at = span(k * WIDTH_GROUP, WIDTH_GROUP)
            back_ref[:count, at] = dot_nt(gateup_grad_ref[:count, :], gateup_ref[at, :]).astype(jnp.bfloat16)
            out = jnp.dot(hidden_ref[:count, :], down_ref[:, at], preferred_element_type=jnp.float32)
            out_ref[:count, at] = out.astype(jnp.bfloat16)
            return carry

        lax.fori_loop(0, width // WIDTH_GROUP, back_step, 0)
        if count < cap:
            for ref in (hidden_ref, gateup_grad_ref, back_ref, out_ref):
                ref[count:, :] = jnp.zeros((cap - count, ref.shape[1]), ref.dtype)

    for low, count in zip((None,) + counts[:-1], counts):
        chosen = live > (-1 if low is None else low)
        if count < cap:
            chosen &= live <= count

        @pl.when(chosen)
        def _(count=count):
            run(count)


def mlp_block(rows, grad, live, gateup_first, gateup_last, down, cap):
    blocks = rows.shape[0] // cap
    width = rows.shape[1]
    units = down.shape[0]
    if units % 128 or cap % 128:
        return mlp_plain(rows, grad, jnp.concatenate([gateup_first, gateup_last], axis=1), down)
    gateup_cols = gateup_first.shape[1] + gateup_last.shape[1]
    counts = (192, 256, 320, 384) if cap == 384 else tuple(range(256, cap, 256)) + (cap,)
    groups = len(unit_groups(units))
    low = jnp.bfloat16
    by_block = lambda cols: pl.BlockSpec((cap, cols), lambda b, live: (b, 0))
    return pl.pallas_call(
        functools.partial(mlp_kernel, cap, counts),
        grid_spec=pltpu.PrefetchScalarGridSpec(
            num_scalar_prefetch=1,
            grid=(blocks,),
            in_specs=[by_block(width), by_block(width)] + [pl.BlockSpec(memory_space=pl.ANY)] * 3,
            out_specs=(by_block(units), by_block(2 * units), by_block(width), by_block(width)),
            scratch_shapes=[
                pltpu.VMEM((width, gateup_cols), low),
                pltpu.VMEM(down.shape, low),
                pltpu.SemaphoreType.DMA((groups,)),
                pltpu.SemaphoreType.DMA((groups,)),
            ],
        ),
        out_shape=(
            jax.ShapeDtypeStruct((blocks * cap, units), low),
            jax.ShapeDtypeStruct((blocks * cap, 2 * units), low),
            jax.ShapeDtypeStruct((blocks * cap, width), low),
            jax.ShapeDtypeStruct((blocks * cap, width), low),
        ),
        compiler_params=pltpu.CompilerParams(vmem_limit_bytes=56 * 1024 * 1024),
        cost_estimate=pl.CostEstimate(
            flops=12 * blocks * cap * width * units,
            bytes_accessed=2 * (width * gateup_cols + down.size) + 12 * blocks * cap * width,
            transcendentals=blocks * cap * units,
        ),
        name="mlp_block",
    )(live, rows, grad, gateup_first, gateup_last, down)


def mlp_plain(rows, grad, gateup, down):
    groups = unit_groups(down.shape[0])
    gate_up = jnp.dot(rows, gateup, preferred_element_type=jnp.float32)
    gate = jnp.concatenate([gate_up[:, 2 * low : low + high] for low, high in groups], axis=1)
    upper = jnp.concatenate([gate_up[:, low + high : 2 * high] for low, high in groups], axis=1)
    grad_hidden = jnp.dot(grad, down.T, preferred_element_type=jnp.float32)
    sigmoid = jax.nn.sigmoid(gate)
    silu = gate * sigmoid
    hidden = (silu * upper).astype(jnp.bfloat16)
    grad_gate = grad_hidden * upper * (sigmoid + silu * (1.0 - sigmoid))
    grad_upper = grad_hidden * silu
    gateup_grad = jnp.concatenate(
        [part[:, low:high] for low, high in groups for part in (grad_gate, grad_upper)], axis=1
    ).astype(jnp.bfloat16)
    back = jnp.dot(gateup_grad, gateup.T, preferred_element_type=jnp.float32).astype(jnp.bfloat16)
    out = jnp.dot(hidden, down, preferred_element_type=jnp.float32).astype(jnp.bfloat16)
    return hidden, gateup_grad, back, out


class Place:
    def __init__(self, n):
        self.n = n
        self.wide = lax.axis_index("wide")
        self.z = lax.axis_index("narrow")
        self.t, self.core = self.wide // 2, self.wide % 2
        self.t_x, self.t_y, self.t_d = self.t ^ 1, self.t ^ 2, self.t ^ 3
        self.by_x = self.device(self.t_x)
        self.by_y = self.device(self.t_y)
        self.by_d = self.device(self.t_d)
        self.sibling = self.device(self.t, core=1 - self.core)
        self.above = self.device(self.t, z=jnp.minimum(self.z + 1, n - 1))
        self.below = self.device(self.t, z=jnp.maximum(self.z - 1, 0))

    def device(self, t, core=None, z=None):
        return (t * 2 + (self.core if core is None else core), self.z if z is None else z)

    def greet(self, others):
        barrier = pltpu.get_barrier_semaphore()
        for other in others:
            pl.semaphore_signal(barrier, inc=1, device_id=other, device_id_type=MESH)

        @pl.when(self.z > 0)
        def _():
            pl.semaphore_signal(barrier, inc=1, device_id=self.below, device_id_type=MESH)

        @pl.when(self.z < self.n - 1)
        def _():
            pl.semaphore_signal(barrier, inc=1, device_id=self.above, device_id_type=MESH)

        inner = (self.z > 0).astype(jnp.int32) + (self.z < self.n - 1).astype(jnp.int32)
        pl.semaphore_wait(barrier, len(others) + inner)


class Copies:
    def __init__(self, send_sems, recv_sems):
        self.send_sems, self.recv_sems = send_sems, recv_sems
        self.count = 0
        self.started = []

    def make(self, src, dst, to):
        k = self.count
        self.count += 1
        return pltpu.make_async_remote_copy(
            src_ref=src, dst_ref=dst, send_sem=self.send_sems.at[k], recv_sem=self.recv_sems.at[k],
            device_id=to, device_id_type=MESH,
        )

    def same(self, ref, to):
        return self.make(ref, ref, to)

    def each(self, moves, when, act):
        def run():
            for m in moves:
                act(m)

        if when is None:
            run()
        else:
            pl.when(when)(run)

    def go(self, moves, when=None):
        self.each(moves, when, lambda m: m.start())
        self.started.append((moves, when))

    def arrive(self, moves, when=None):
        self.each(moves, when, lambda m: m.wait_recv())

    def end(self):
        for moves, when in self.started:
            self.each(moves, when, lambda m: m.wait_send())


class LineGather:
    def __init__(self, place, copies, view, own):
        self.place, self.copies, self.view, self.own = place, copies, view, own
        self.up, self.down = {}, {}

    def send(self, step):
        p, last = self.place, self.place.n - 1
        block = self.view(jnp.maximum(p.z - (step - 1), 0))
        self.up[step] = self.copies.make(self.own if step == 1 else block, block, p.above)
        self.copies.go([self.up[step]], (p.z - (step - 1) >= 0) & (p.z < last))
        block = self.view(jnp.minimum(p.z + (step - 1), last))
        self.down[step] = self.copies.make(self.own if step == 1 else block, block, p.below)
        self.copies.go([self.down[step]], (p.z + (step - 1) <= last) & (p.z > 0))

    def take(self, step):
        p = self.place
        self.copies.arrive([self.up[step]], p.z - step >= 0)
        self.copies.arrive([self.down[step]], p.z + step <= p.n - 1)

    def hand_over(self, step):
        p, last = self.place, self.place.n - 1
        moves = []
        for at, there in ((p.z - step, p.z - step >= 0), (p.z + step, p.z + step <= last)):
            block = self.view(jnp.clip(at, 0, last))
            move = self.copies.same(block, p.sibling)
            self.copies.go([move], there)
            moves.append(([move], there))
        return moves


def gather_kernel(
    n, qkv_ref, out_ref, gateup_ref, down_ref, ext_ref, qkv_all, out_all, ext_all, came, down_all,
    qkv_low, out_low, trade_low, down_low, send_sems, recv_sems, local_sems,
):
    p = Place(n)
    c = Copies(send_sems, recv_sems)
    t, core, z = p.t, p.core, p.z
    low = jnp.bfloat16
    qkv_low[...] = qkv_ref[...].astype(low)
    p.greet([p.by_x, p.by_y, p.by_d, p.sibling])

    half = qkv_ref.shape[1] // 256 * 128
    qa, qb = slice(0, half), slice(half, qkv_ref.shape[1])
    lines = [
        LineGather(p, c, lambda zz, cols=cols: qkv_all.at[t, core, zz, :, cols], qkv_low.at[:, cols])
        for cols in (qa, qb)
    ]
    lines.append(LineGather(p, c, lambda zz: ext_all.at[t, core, zz], ext_ref))
    for line in lines:
        line.send(1)
    local = []

    def place(src, dst):
        move = pltpu.make_async_copy(src, dst, local_sems.at[len(local)])
        move.start()
        local.append(move)

    place(qkv_low, qkv_all.at[t, core, z])
    place(ext_ref, ext_all.at[t, core, z])
    units = trade_low.shape[2] // 2
    for k in range(trade_low.shape[0]):
        for first, last in unit_groups(units):
            for to, start in ((2 * first, k * units), (first + last, gateup_ref.shape[1] // 2 + k * units)):
                trade_low[k, :, to : to + last - first] = gateup_ref[:, start + first : start + last].astype(low)
    place(trade_low.at[t], came.at[t])
    trade = [
        c.make(trade_low.at[k], came.at[t], to) for k, to in ((p.t_x, p.by_x), (p.t_y, p.by_y), (p.t_d, p.by_d))
    ]
    c.go(trade)
    out_low[...] = out_ref[...].astype(low)
    down_low[...] = down_ref[...].astype(low)
    place(out_low, out_all.at[t, core, z])
    place(down_low, down_all.at[core, z])
    line_out = LineGather(p, c, lambda zz: out_all.at[t, core, zz], out_low)
    line_down = LineGather(p, c, lambda zz: down_all.at[core, zz], down_low)
    down_own = c.make(down_low, down_all.at[core, z], p.sibling)
    c.go([down_own])
    handed = [([down_own], None)]
    for step in range(1, n):
        for line in lines:
            line.take(step)
            if step < n - 1:
                line.send(step + 1)
    for move in local:
        move.wait()
    a_y = c.same(qkv_all.at[t, core, :, :, qa], p.by_y)
    b_x = c.same(qkv_all.at[t, core, :, :, qb], p.by_x)
    e_x = c.same(ext_all.at[t, core], p.by_x)
    c.go([a_y, b_x, e_x])
    line_down.send(1)
    line_out.send(1)
    own = [c.same(qkv_all.at[t, core], p.sibling), c.same(ext_all.at[t, core], p.sibling)]
    c.go(own)
    c.arrive([e_x])
    e_y = [c.same(ext_all.at[k, core], p.by_y) for k in (t, p.t_x)]
    c.go(e_y)
    c.arrive([a_y])
    a_x = [c.same(qkv_all.at[k, core, :, :, qa], p.by_x) for k in (t, p.t_y)]
    c.go(a_x)
    c.arrive([b_x])
    b_y = [c.same(qkv_all.at[k, core, :, :, qb], p.by_y) for k in (t, p.t_x)]
    c.go(b_y)
    near = [
        c.same(qkv_all.at[p.t_y, core, :, :, qa], p.sibling),
        c.same(qkv_all.at[p.t_x, core, :, :, qb], p.sibling),
        c.same(ext_all.at[p.t_x, core], p.sibling),
    ]
    c.go(near)
    c.arrive(e_y)
    far = [c.same(ext_all.at[k, core], p.sibling) for k in (p.t_y, p.t_d)]
    c.go(far)
    for step in range(1, n):
        for line in (line_down, line_out):
            line.take(step)
            if step < n - 1:
                line.send(step + 1)
        handed += line_down.hand_over(step)
        if step == max(n - 2, 1):
            c.arrive(a_x)
            c.arrive(b_y)
            last = [c.same(qkv_all.at[k, core, :, :, qa], p.sibling) for k in (p.t_x, p.t_d)]
            last += [c.same(qkv_all.at[k, core, :, :, qb], p.sibling) for k in (p.t_y, p.t_d)]
            c.go(last)
    c.arrive(trade + own + near + far + last)
    for moves, when in handed:
        c.arrive(moves, when)
    c.end()


def gather_first(qkv, out, gateup, down, ext, planes, n):
    any_spec = pl.BlockSpec(memory_space=pl.ANY)
    rows = qkv.shape[0]
    part = gateup.shape[1] // planes
    low = jnp.bfloat16
    copies = 64
    return pl.pallas_call(
        functools.partial(gather_kernel, n),
        out_shape=(
            jax.ShapeDtypeStruct((planes, 2, n, rows, qkv.shape[1]), low),
            jax.ShapeDtypeStruct((planes, 2, n, rows, out.shape[1]), low),
            jax.ShapeDtypeStruct((planes, 2, n) + ext.shape, low),
            jax.ShapeDtypeStruct((planes, rows, part), low),
            jax.ShapeDtypeStruct((2, n) + down.shape, low),
        ),
        in_specs=[pl.BlockSpec(memory_space=pltpu.VMEM)] * 5,
        out_specs=(any_spec,) * 5,
        scratch_shapes=[
            pltpu.VMEM(qkv.shape, low),
            pltpu.VMEM(out.shape, low),
            pltpu.VMEM((planes, rows, part), low),
            pltpu.VMEM(down.shape, low),
            pltpu.SemaphoreType.DMA((copies,)),
            pltpu.SemaphoreType.DMA((copies,)),
            pltpu.SemaphoreType.DMA((8,)),
        ],
        compiler_params=pltpu.CompilerParams(
            collective_id=0, has_side_effects=True, vmem_limit_bytes=32 * 1024 * 1024
        ),
        name="gather_first",
    )(qkv, out, gateup, down, ext)


class PlaneScatter:
    def __init__(self, place, copies, left, right, parts, turned, leaving, came, total, first, second):
        self.p, self.c, self.left, self.right, self.parts = place, copies, left, right, parts
        self.turned, self.leaving, self.came, self.total = turned, leaving, came, total
        self.first, self.second = first, second
        self.moves = {}

    def turn(self):
        rows = self.turned.shape[1]

        def one(k, carry):
            self.turned[k] = self.left[:, pl.ds(pl.multiple_of(k * rows, rows), rows)].T
            return carry

        lax.fori_loop(0, self.turned.shape[0], one, 0)

    def at(self, part):
        low, high, _ = self.parts[part]
        return slice(low, high)

    def begin(self, part):
        p, cols = self.p, self.at(part)
        right = self.right[:, cols]

        def terms(into, core):
            def one(t, carry):
                term = jnp.dot(self.turned[t * 2 + core], right, preferred_element_type=jnp.float32)
                into[t, :, cols] = term.astype(jnp.bfloat16)
                return carry

            lax.fori_loop(0, into.shape[0], one, 0)

        terms(self.leaving, 1 - p.core)
        self.moves[part, 0] = [self.c.make(self.leaving.at[:, :, cols], self.came.at[:, :, cols], p.sibling)]
        self.c.go(self.moves[part, 0])
        terms(self.total, p.core)

    def add(self, t, cols, came):
        both = self.total[t, :, cols].astype(jnp.float32) + came.astype(jnp.float32)
        self.total[t, :, cols] = both.astype(jnp.bfloat16)

    def across_first(self, part):
        p, c, cols = self.p, self.c, self.at(part)
        c.arrive(self.moves[part, 0])

        def one(t, carry):
            self.add(t, cols, self.came[t, :, cols])
            return carry

        lax.fori_loop(0, self.total.shape[0], one, 0)
        near, to = (p.t_x, p.by_x) if self.parts[part][2] else (p.t_y, p.by_y)
        self.moves[part, 1] = [
            c.make(self.total.at[t, :, cols], self.first.at[k, :, cols], to) for k, t in enumerate((near, p.t_d))
        ]
        c.go(self.moves[part, 1])

    def across_second(self, part):
        p, c, cols = self.p, self.c, self.at(part)
        c.arrive(self.moves[part, 1])
        near, to = (p.t_y, p.by_y) if self.parts[part][2] else (p.t_x, p.by_x)
        self.add(near, cols, self.first[1, :, cols])
        self.moves[part, 2] = [c.make(self.total.at[near, :, cols], self.second.at[:, cols], to)]
        c.go(self.moves[part, 2])
        self.add(p.t, cols, self.first[0, :, cols])

    def end(self, part):
        cols = self.at(part)
        self.c.arrive(self.moves[part, 2])
        self.add(self.p.t, cols, self.second[:, cols])


class LineScatter:
    def __init__(self, place, copies, read, cols, up_leaving, up_came, down_leaving, down_came):
        self.p, self.c, self.read, self.cols = place, copies, read, cols
        self.ways = ((up_leaving, up_came, place.above), (down_leaving, down_came, place.below))
        self.rows = up_came.shape[1]
        self.moves = []

    def block(self, d):
        at = pl.ds(pl.multiple_of(jnp.clip(d, 0, self.p.n - 1) * self.rows, self.rows), self.rows)
        return self.read(at, self.cols).astype(jnp.float32)

    def step(self, s):
        p, c, n, cols = self.p, self.c, self.p.n, self.cols
        self.take()
        self.moves = []
        for way, (leaving, came, to) in enumerate(self.ways):
            behind = p.z if way == 0 else n - 1 - p.z
            block = n - s + p.z if way == 0 else p.z - (n - s)
            sends = (behind <= s - 1) & (behind < n - 1)

            @pl.when(sends & (behind == 0) if s > 1 else sends)
            def _():
                leaving[s - 1, :, cols] = self.block(block).astype(jnp.bfloat16)

            if s > 1:
                @pl.when(sends & (behind > 0))
                def _():
                    both = self.block(block) + came[s - 2, :, cols].astype(jnp.float32)
                    leaving[s - 1, :, cols] = both.astype(jnp.bfloat16)

            move = c.make(leaving.at[s - 1, :, cols], came.at[s - 1, :, cols], to)
            c.go([move], sends)
            self.moves.append((move, (behind >= 1) & (behind <= s)))

    def take(self):
        for move, when in self.moves:
            self.c.arrive([move], when)

    def end(self, out_ref):
        p, n, cols = self.p, self.p.n, self.cols
        self.take()
        up_came, down_came = self.ways[0][1], self.ways[1][1]
        own = self.block(p.z)

        @pl.when(p.z == 0)
        def _():
            out_ref[:, cols] = own + down_came[n - 2, :, cols].astype(jnp.float32)

        @pl.when(p.z == n - 1)
        def _():
            out_ref[:, cols] = own + up_came[n - 2, :, cols].astype(jnp.float32)

        @pl.when((p.z > 0) & (p.z < n - 1))
        def _():
            out_ref[:, cols] = own + (
                up_came[n - 2, :, cols].astype(jnp.float32) + down_came[n - 2, :, cols].astype(jnp.float32)
            )


def plane_parts(cols, count):
    edges = [cols // 128 * k // count * 128 for k in range(count + 1)]
    return [(low, high, k % 2 == 0) for k, (low, high) in enumerate(zip(edges[:-1], edges[1:]))]


def plane_scratch(rows, width, cols, planes):
    low = jnp.bfloat16
    line = width // planes // 2
    return [
        pltpu.VMEM((planes * 2, line, rows), low),
        pltpu.VMEM((planes, line, cols), low),
        pltpu.VMEM((planes, line, cols), low),
        pltpu.VMEM((planes, line, cols), low),
        pltpu.VMEM((2, line, cols), low),
        pltpu.VMEM((line, cols), low),
    ]


def qkv_back_kernel(
    n, parts, normed_ref, grad_ref, weights_hbm, pieces_ref, out_sum, sum_ref, back_ref, gateup_ref, out_ref, weights,
    traded, turned, leaving, came, total, first, second, up_leaving, up_came, down_leaving, down_came, out_up_leaving,
    out_up_came, out_down_leaving, out_down_came, send_sems, recv_sems, load_sem,
):
    p = Place(n)
    c = Copies(send_sems, recv_sems)
    held = weights.shape[0]

    def load(k):
        return pltpu.make_async_copy(weights_hbm.at[k * held : (k + 1) * held], weights, load_sem)

    load(0).start()
    p.greet([p.by_x, p.by_y, p.by_d, p.sibling])
    trade = [
        c.make(pieces_ref.at[k], traded.at[p.t], to) for k, to in ((p.t_x, p.by_x), (p.t_y, p.by_y), (p.t_d, p.by_d))
    ]
    c.go(trade)
    traded[p.t] = pieces_ref[p.t]
    out_line = LineScatter(
        p, c, lambda at, cols: out_sum[at, cols], slice(None), out_up_leaving, out_up_came, out_down_leaving, out_down_came
    )
    out_line.step(1)
    scatter = PlaneScatter(p, c, normed_ref, grad_ref, parts, turned, leaving, came, total, first, second)
    every = range(len(parts))
    scatter.turn()
    for k in every:
        scatter.begin(k)
    chunk = 2 * HEAD_DIM

    def back(half):
        load(half).wait()

        def one(k, carry):
            at = pl.ds(pl.multiple_of(k * chunk, chunk), chunk)
            to = pl.ds(pl.multiple_of(half * held + k * chunk, chunk), chunk)
            back_ref[:, to] = dot_nt(grad_ref[...], weights[at, :])
            return carry

        lax.fori_loop(0, held // chunk, one, 0)

    for k in every:
        scatter.across_first(k)
    if n > 2:
        out_line.step(2)
    back(0)
    load(1).start()
    c.arrive(trade)
    units = traded.shape[2] // 2
    for k in range(traded.shape[0]):
        for low, high in unit_groups(units):
            for at, start in ((2 * low, k * units), (low + high, gateup_ref.shape[1] // 2 + k * units)):
                columns = traded[k, :, at : at + high - low]
                gateup_ref[:, start + low : start + high] = columns.astype(jnp.float32)
    for s in range(3, n):
        out_line.step(s)
    for k in every:
        scatter.across_second(k)
    back(1)
    lines = [
        LineScatter(
            p, c, lambda at, cols: total[p.t, at, cols], scatter.at(k), up_leaving, up_came, down_leaving, down_came
        )
        for k in every
    ]
    for k in every:
        scatter.end(k)
        lines[k].step(1)
    for s in range(2, n):
        for line in lines:
            line.step(s)
    out_line.end(out_ref)
    for line in lines:
        line.end(sum_ref)
    c.end()


def qkv_back(normed, grad, weights, pieces, out_sum, planes, n, collective_id):
    rows, width = normed.shape
    cols = grad.shape[1]
    parts = plane_parts(cols, 4)
    in_vmem = pl.BlockSpec(memory_space=pltpu.VMEM)
    low = jnp.bfloat16
    line = pltpu.VMEM((n - 1, width // planes // 2 // n, cols), low)
    out_line = pltpu.VMEM((n - 1, out_sum.shape[0] // n, out_sum.shape[1]), low)
    copies = len(parts) * (4 + 2 * n) + 2 * n + 4
    return pl.pallas_call(
        functools.partial(qkv_back_kernel, n, parts),
        in_specs=[in_vmem, in_vmem, pl.BlockSpec(memory_space=pl.ANY), in_vmem, in_vmem],
        out_specs=(in_vmem,) * 4,
        out_shape=(
            jax.ShapeDtypeStruct((width // planes // 2 // n, cols), jnp.float32),
            jax.ShapeDtypeStruct((rows, width), jnp.float32),
            jax.ShapeDtypeStruct((pieces.shape[1], planes * pieces.shape[2]), jnp.float32),
            jax.ShapeDtypeStruct((out_sum.shape[0] // n, out_sum.shape[1]), jnp.float32),
        ),
        scratch_shapes=[pltpu.VMEM((weights.shape[0] // 2, cols), low), pltpu.VMEM(pieces.shape, low)]
        + plane_scratch(rows, width, cols, planes)
        + [line] * 4
        + [out_line] * 4
        + [pltpu.SemaphoreType.DMA((copies,)), pltpu.SemaphoreType.DMA((copies,)), pltpu.SemaphoreType.DMA],
        compiler_params=pltpu.CompilerParams(
            vmem_limit_bytes=60 * 1024 * 1024, collective_id=collective_id, has_side_effects=True
        ),
        cost_estimate=pl.CostEstimate(
            flops=48 * rows * width * cols, bytes_accessed=2 * weights.size + 8 * rows * width, transcendentals=0
        ),
        name="qkv_back",
    )(normed, grad, weights, pieces, out_sum)


class TokenScatter:
    def __init__(self, place, copies, blocks, near, corner_x, corner_y, came_x, came_y, load_sem):
        self.p, self.c, self.blocks, self.near = place, copies, blocks, near
        self.corner_x, self.corner_y, self.came_x, self.came_y = corner_x, corner_y, came_x, came_y
        self.cap = near.shape[0] // 2
        self.keep = pltpu.make_async_copy(blocks[1], near, load_sem)

    def begin(self):
        p, c, half = self.p, self.c, self.cap // 2
        self.keep.start()
        self.far = [
            c.make(self.blocks[2].at[:half], self.corner_x, p.by_x), c.make(self.blocks[2].at[half:], self.corner_y, p.by_y)
        ]
        c.go(self.far)

    def middle(self):
        p, c, near, cap = self.p, self.c, self.near, self.cap
        self.keep.wait()
        c.arrive(self.far)
        for at, came in ((slice(cap // 2, cap), self.corner_y), (slice(cap, cap + cap // 2), self.corner_x)):
            near[at, :] = (near[at, :].astype(jnp.float32) + came[...].astype(jnp.float32)).astype(jnp.bfloat16)
        self.close = [c.make(near.at[:cap], self.came_x, p.by_x), c.make(near.at[cap:], self.came_y, p.by_y)]
        c.go(self.close)

    def end(self):
        self.c.arrive(self.close)


def mid_back_kernel(
    n, cap, units, *refs,
):
    back, rows_in, gateup_in, hidden_in, grads_in = (refs[k : k + 3] for k in range(0, 15, 3))
    sum_ref, down_ref, gateup_ref = refs[15:18]
    (
        wide_now, both_now, turned, own, near, corner_x, corner_y, came_x, came_y, down_leaving, down_came,
        gateup_leaving, gateup_came, send_sems, recv_sems, load_sems,
    ) = refs[18:]
    p = Place(n)
    c = Copies(send_sems, recv_sems)
    low = jnp.bfloat16
    loaded = [0]

    def load(parts, into, cols=None):
        moves = []
        for at, part in zip((slice(0, cap), slice(cap, 3 * cap), slice(3 * cap, 4 * cap)), parts):
            to = into.at[at] if cols is None else into.at[at, cols]
            moves.append(pltpu.make_async_copy(part, to, load_sems.at[loaded[0]]))
            loaded[0] += 1
            moves[-1].start()
        return moves

    def wait(moves):
        for m in moves:
            m.wait()

    first = load(grads_in, wide_now) + load(hidden_in, both_now, slice(0, units))
    keep = pltpu.make_async_copy(back[0], own, load_sems.at[14])
    keep.start()
    tokens = TokenScatter(p, c, back, near, corner_x, corner_y, came_x, came_y, load_sems.at[15])
    p.greet([p.by_x, p.by_y, p.sibling])
    tokens.begin()

    wait(first)

    def turn(k, carry):
        at = pl.ds(pl.multiple_of(k * LANES, LANES), LANES)
        turned[at, :] = both_now[:, at].T
        return carry

    lax.fori_loop(0, units // LANES, turn, 0)
    part = units // 2
    width = wide_now.shape[1]

    def down_half(core, put):
        def one(k, carry):
            at = pl.ds(pl.multiple_of(k * WIDTH_GROUP, WIDTH_GROUP), WIDTH_GROUP)
            left = turned[pl.ds(pl.multiple_of(core * part, 16), part), :]
            put(at, jnp.dot(left, wide_now[:, at], preferred_element_type=jnp.float32))
            return carry

        lax.fori_loop(0, width // WIDTH_GROUP, one, 0)

    def put_leaving(at, term):
        down_leaving[:, at] = term.astype(low)

    def put_down(at, term):
        down_ref[:, at] = (term + down_came[:, at].astype(jnp.float32)).astype(low)

    down_half(1 - p.core, put_leaving)
    down_move = [c.make(down_leaving, down_came, p.sibling)]
    c.go(down_move)
    tokens.middle()
    c.arrive(down_move)
    down_half(p.core, put_down)

    second = load(rows_in, wide_now) + load(gateup_in, both_now)
    wait(second)
    line = gateup_ref.shape[1]
    cols = 2 * units

    def gateup_part(k, put):
        left = wide_now[:, pl.ds(pl.multiple_of(k * line, line), line)].T

        def one(j, carry):
            at = pl.ds(pl.multiple_of(j * WIDTH_GROUP, WIDTH_GROUP), WIDTH_GROUP)
            put(at, jnp.dot(left, both_now[:, at], preferred_element_type=jnp.float32))
            return carry

        lax.fori_loop(0, cols // WIDTH_GROUP, one, 0)

    moves = []
    planes = gateup_ref.shape[0]
    for t in range(planes):
        slot = t % 2
        if t >= 2:
            moves[t - 2].wait_send()

        def put_slot(at, term, slot=slot):
            gateup_leaving[slot, :, at] = term.astype(low)

        gateup_part(t * 2 + 1 - p.core, put_slot)
        moves.append(c.make(gateup_leaving.at[slot], gateup_came.at[t], p.sibling))
        moves[-1].start()
    for t in range(planes):
        moves[t].wait_recv()

        def put_sum(at, term, t=t):
            gateup_ref[t, :, at] = (term + gateup_came[t, :, at].astype(jnp.float32)).astype(low)

        gateup_part(t * 2 + p.core, put_sum)
    for t in range(max(planes - 2, 0), planes):
        moves[t].wait_send()
    tokens.end()
    keep.wait()
    sum_ref[...] = own[...].astype(jnp.float32) + (
        came_x[...].astype(jnp.float32) + came_y[...].astype(jnp.float32)
    )
    c.end()


def mid_back(back, rows, gateup_grads, hidden, grads, cap, planes, n, collective_id):
    width = rows[0].shape[1]
    units = hidden[0].shape[1]
    line = width // planes // 2
    low = jnp.bfloat16
    any_spec = pl.BlockSpec(memory_space=pl.ANY)
    in_vmem = pl.BlockSpec(memory_space=pltpu.VMEM)
    vmem = lambda *shape: pltpu.VMEM(shape, low)
    return pl.pallas_call(
        functools.partial(mid_back_kernel, n, cap, units),
        in_specs=[any_spec] * 15,
        out_specs=(in_vmem,) * 3,
        out_shape=(
            jax.ShapeDtypeStruct((cap, width), jnp.float32),
            jax.ShapeDtypeStruct((units // 2, width), low),
            jax.ShapeDtypeStruct((planes, line, 2 * units), low),
        ),
        scratch_shapes=[
            vmem(4 * cap, width),
            vmem(4 * cap, 2 * units),
            vmem(units, 4 * cap),
            vmem(cap, width),
            vmem(2 * cap, width),
            vmem(cap // 2, width),
            vmem(cap // 2, width),
            vmem(cap, width),
            vmem(cap, width),
            vmem(units // 2, width),
            vmem(units // 2, width),
            vmem(2, line, 2 * units),
            vmem(planes, line, 2 * units),
            pltpu.SemaphoreType.DMA((12,)),
            pltpu.SemaphoreType.DMA((12,)),
            pltpu.SemaphoreType.DMA((16,)),
        ],
        compiler_params=pltpu.CompilerParams(
            vmem_limit_bytes=61 * 1024 * 1024, collective_id=collective_id, has_side_effects=True
        ),
        cost_estimate=pl.CostEstimate(
            flops=48 * cap * width * units, bytes_accessed=32 * cap * (width + units), transcendentals=0
        ),
        name="mid_back",
    )(*back, *rows, *gateup_grads, *hidden, *grads)


def fill_bias(r, key_code, query_code, query_base, bias):
    rows = bias.shape[0]
    code = key_code[r * rows : (r + 1) * rows, :]
    seen = (code <= query_code[...]) & (code >= query_base[...])
    bias[...] = jnp.where(seen, 0.0, MASKED)


class PlaneGather:
    def __init__(self, place, copies, whole):
        self.p, self.c, self.whole = place, copies, whole
        cols = whole.shape[-1]
        self.a, self.b = slice(0, cols // 2), slice(cols // 2, cols)

    def block(self, t, cols=slice(None)):
        return self.whole.at[t, self.p.core, :, :, cols]

    def begin(self):
        p, c = self.p, self.c
        self.a_y, self.b_x = c.same(self.block(p.t, self.a), p.by_y), c.same(self.block(p.t, self.b), p.by_x)
        self.over = [c.same(self.block(p.t), p.sibling)]
        c.go([self.a_y, self.b_x] + self.over)

    def middle(self):
        p, c = self.p, self.c
        c.arrive([self.a_y, self.b_x])
        self.a_x = [c.same(self.block(k, self.a), p.by_x) for k in (p.t, p.t_y)]
        self.b_y = [c.same(self.block(k, self.b), p.by_y) for k in (p.t, p.t_x)]
        near = [c.same(self.block(p.t_y, self.a), p.sibling), c.same(self.block(p.t_x, self.b), p.sibling)]
        c.go(self.a_x + self.b_y + near)
        self.over += near

    def end(self):
        p, c = self.p, self.c
        c.arrive(self.a_x + self.b_y)
        far = [c.same(self.block(k, self.a), p.sibling) for k in (p.t_x, p.t_d)]
        far += [c.same(self.block(k, self.b), p.sibling) for k in (p.t_y, p.t_d)]
        c.go(far)
        c.arrive(self.over + far)


def attend_kernel(n, with_out, *refs):
    inputs_ref, gain_ref, cosine, sine, weights_hbm, key_code, query_code, query_base = refs[:8]
    refs = refs[8:]
    if with_out:
        (own_grad, _), refs = refs[:2], refs[2:]
    (normed_ref, inverse_ref, q_ref, o_ref, total_ref, kv_all), refs = refs[:6], refs[6:]
    if with_out:
        (out_all, grad_x, grad_y, grad_d), refs = refs[:4], refs[4:]
    weights, peak_now, total_now, mixed_now, bias, send_sems, recv_sems, load_sems = refs
    p = Place(n)
    c = Copies(send_sems, recv_sems)
    z = p.z
    rows, width = q_ref.shape
    values_at = KV_HEADS * HEAD_DIM
    pair = 2 * HEAD_DIM
    slot = lambda r: kv_all.at[r * rows : (r + 1) * rows, :]
    loads = [
        pltpu.make_async_copy(weights_hbm.at[:, cols], weights.at[:, cols], load_sems.at[k])
        for k, cols in enumerate((slice(width, weights.shape[1]), slice(0, width)))
    ]
    for load in loads:
        load.start()
    p.greet([p.by_x, p.by_y, p.sibling] if with_out else [])
    if with_out:
        half = rows // 2
        near = [c.make(own_grad, grad_x, p.by_x), c.make(own_grad, grad_y, p.by_y)]
        out_plane = PlaneGather(p, c, out_all)
        out_plane.begin()
        c.go(near)
    inputs = inputs_ref[...]
    inverse = lax.rsqrt(jnp.mean(inputs * inputs, axis=1, keepdims=True) + EPSILON)
    inverse_ref[...] = inverse
    normed_ref[...] = (inputs * inverse * gain_ref[...]).astype(jnp.bfloat16)

    def project(low, into, to, turned):
        at = pl.ds(pl.multiple_of(low, pair), pair)
        both = jnp.dot(normed_ref[...], weights[:, at], preferred_element_type=jnp.float32)
        for k in range(2):
            head = both[:, k * HEAD_DIM : (k + 1) * HEAD_DIM]
            if turned:
                head = head * cosine[...] + pltpu.roll(head, HEAD_DIM // 2, 1) * sine[...]
            lanes = pl.ds(pl.multiple_of(to + k * HEAD_DIM, HEAD_DIM), HEAD_DIM)
            into[:rows, lanes] = head.astype(jnp.bfloat16)

    def project_all(start, count, into, to, turned):
        def one(k, carry):
            project(start + k * pair, into, to + k * pair, turned)
            return carry

        lax.fori_loop(0, count // pair, one, 0)

    loads[0].wait()
    project_all(width, values_at, kv_all, 0, True)
    project_all(width + values_at, values_at, kv_all, values_at, False)
    copies = [c.make(slot(r), slot(r + 1), p.above) for r in range(n - 1)]
    if copies:
        c.go([copies[0]], z < n - 1)
    for r in range(1, n):
        @pl.when(z < r)
        def _(r=r):
            kv_all[r * rows : (r + 1) * rows, :] = jnp.zeros((rows, kv_all.shape[1]), kv_all.dtype)

    loads[1].wait()
    project_all(0, width, q_ref, 0, True)

    def block(r):
        fill_bias(r, key_code, query_code, query_base, bias)
        at = slice(r * rows, (r + 1) * rows)

        def group(g, carry):
            keys = kv_all[at, pl.ds(pl.multiple_of(g * HEAD_DIM, HEAD_DIM), HEAD_DIM)]
            values = kv_all[at, pl.ds(pl.multiple_of(values_at + g * HEAD_DIM, HEAD_DIM), HEAD_DIM)]
            hidden = bias[...]
            for h in range(GROUP):
                lanes = pl.ds(pl.multiple_of((g * GROUP + h) * HEAD_DIM, HEAD_DIM), HEAD_DIM)
                scores = dot_nt(keys, q_ref[:, lanes]) * (SCORE_SCALE * LOG2_E) + hidden
                peak = jnp.max(scores, axis=0, keepdims=True)
                if r:
                    before = peak_now[g, h : h + 1, :]
                    peak = jnp.maximum(peak, before)
                weights = jnp.exp2(scores - peak)
                total = jnp.sum(weights, axis=0, keepdims=True)
                mixed = dot_tn(values, weights.astype(jnp.bfloat16))
                if r:
                    shrink = jnp.exp2(before - peak)
                    total = total + total_now[g, h : h + 1, :] * shrink
                    mixed = mixed + mixed_now[g, h] * shrink
                peak_now[g, h : h + 1, :] = peak
                total_now[g, h : h + 1, :] = total
                mixed_now[g, h] = mixed
            return carry

        lax.fori_loop(0, KV_HEADS, group, 0)

    block(0)
    for r in range(1, n):
        c.arrive([copies[r - 1]], z >= r)
        if r < n - 1:
            c.go([copies[r]], (z >= r) & (z < n - 1))
        if with_out and r == 1:
            out_plane.middle()
        if with_out and r == max(n - 2, 1):
            c.arrive(near)
            corners = [
                c.make(grad_y.at[:half], grad_d.at[:half], p.by_x),
                c.make(grad_x.at[half:], grad_d.at[half:], p.by_y),
            ]
            c.go(corners)
        if with_out and r == n - 1:
            out_plane.end()

        @pl.when(z >= r)
        def _(r=r):
            block(r)

    def finish(g, carry):
        for h in range(GROUP):
            lanes = pl.ds(pl.multiple_of((g * GROUP + h) * HEAD_DIM, HEAD_DIM), HEAD_DIM)
            total = total_now[g, h : h + 1, :]
            o_ref[:, lanes] = (mixed_now[g, h] / total).T.astype(jnp.bfloat16)
            total_ref[g, h : h + 1, :] = peak_now[g, h : h + 1, :] + jnp.log2(total)
        return carry

    lax.fori_loop(0, KV_HEADS, finish, 0)
    if with_out:
        c.arrive(corners)
    c.end()


def attend(
    inputs, gain, cosine, sine, weights, key_code, query_code, query_base, n, collective_id, down_grad=None, out_all=None
):
    rows, width = inputs.shape
    kv_cols = weights.shape[1] - width
    low = jnp.bfloat16
    in_vmem = pl.BlockSpec(memory_space=pltpu.VMEM)
    any_spec = pl.BlockSpec(memory_space=pl.ANY)
    given = [] if out_all is None else [down_grad, out_all]
    more = [] if out_all is None else [out_all] + [down_grad] * 3
    copies = n + 24
    return pl.pallas_call(
        functools.partial(attend_kernel, n, out_all is not None),
        in_specs=[in_vmem] * 4 + [any_spec] + [in_vmem] * 3 + [any_spec] * len(given),
        out_specs=(in_vmem,) * 6 + (any_spec,) * len(more),
        input_output_aliases={9: 6} if given else {},
        out_shape=(
            jax.ShapeDtypeStruct((rows, width), low),
            jax.ShapeDtypeStruct((rows, 1), jnp.float32),
            jax.ShapeDtypeStruct((rows, width), low),
            jax.ShapeDtypeStruct((rows, width), low),
            jax.ShapeDtypeStruct((KV_HEADS, GROUP, rows), jnp.float32),
            jax.ShapeDtypeStruct((n * rows, kv_cols), low),
        )
        + tuple(jax.ShapeDtypeStruct(o.shape, o.dtype) for o in more),
        scratch_shapes=[
            pltpu.VMEM(weights.shape, low),
            pltpu.VMEM((KV_HEADS, GROUP, rows), jnp.float32),
            pltpu.VMEM((KV_HEADS, GROUP, rows), jnp.float32),
            pltpu.VMEM((KV_HEADS, GROUP, HEAD_DIM, rows), jnp.float32),
            pltpu.VMEM((rows, rows), jnp.float32),
            pltpu.SemaphoreType.DMA((copies,)),
            pltpu.SemaphoreType.DMA((copies,)),
            pltpu.SemaphoreType.DMA((2,)),
        ],
        compiler_params=pltpu.CompilerParams(
            vmem_limit_bytes=52 * 1024 * 1024, collective_id=collective_id, has_side_effects=True
        ),
        cost_estimate=pl.CostEstimate(
            flops=64 * rows * n * rows * width, bytes_accessed=8 * rows * width, transcendentals=HEADS * rows * n * rows
        ),
        name="attend",
    )(inputs, gain, cosine, sine, weights, key_code, query_code, query_base, *given)


def attend_back_kernel(n, parts, *refs):
    q_ref, kv_all, do_ref, total_ref, mixed_ref, key_code, query_code, query_base, cosine, sine = refs[:10]
    refs = refs[10:]
    if parts:
        branch_ref, down_terms, refs = refs[0], refs[1:4], refs[4:]
    grad_ref, refs = refs[0], refs[1:]
    if parts:
        (out_sum, came_x, came_y), refs = refs[:3], refs[3:]
    dq_now, dkv_now, bias, inner_now, leaving, came, send_sems, recv_sems = refs[:8]
    p = Place(n)
    c = Copies(send_sems, recv_sems)
    z = p.z
    rows = q_ref.shape[0]
    values_at = KV_HEADS * HEAD_DIM
    p.greet([p.by_x, p.by_y, p.sibling] if parts else [])
    every = range(len(parts))
    if parts:
        scatter = PlaneScatter(p, c, mixed_ref, branch_ref, parts, *refs[8:14])
        tokens = TokenScatter(p, c, down_terms, *refs[14:17], came_x, came_y, refs[17])
        tokens.begin()
    copies = {r: c.make(leaving.at[r - 1], came.at[r - 1], p.below) for r in range(1, n)}
    dq_now[...] = jnp.zeros_like(dq_now)
    q_cols = HEADS * HEAD_DIM

    def turned_back(head):
        return head * cosine[...] - pltpu.roll(head, HEAD_DIM // 2, 1) * sine[...]

    def put(low, head):
        grad_ref[:, low : low + HEAD_DIM] = head.astype(jnp.bfloat16)

    def block(r):
        fill_bias(r, key_code, query_code, query_base, bias)
        at = slice(r * rows, (r + 1) * rows)

        def group(g, carry):
            key_lanes = pl.ds(pl.multiple_of(g * HEAD_DIM, HEAD_DIM), HEAD_DIM)
            value_lanes = pl.ds(pl.multiple_of(values_at + g * HEAD_DIM, HEAD_DIM), HEAD_DIM)
            keys, values, hidden = kv_all[at, key_lanes], kv_all[at, value_lanes], bias[...]
            dk = dv = None
            for h in range(GROUP):
                lanes = pl.ds(pl.multiple_of((g * GROUP + h) * HEAD_DIM, HEAD_DIM), HEAD_DIM)
                query, grad = q_ref[:, lanes], do_ref[:, lanes]
                scores = dot_nt(keys, query) * (SCORE_SCALE * LOG2_E) + hidden
                weights = jnp.exp2(scores - total_ref[g, h : h + 1, :])
                grad_weights = dot_nt(values, grad)
                grad_scores = (weights * (grad_weights - inner_now[g, h : h + 1, :])).astype(jnp.bfloat16)
                dv_term = jnp.dot(weights.astype(jnp.bfloat16), grad, preferred_element_type=jnp.float32)
                dk_term = jnp.dot(grad_scores, query, preferred_element_type=jnp.float32)
                dv = dv_term if dv is None else dv + dv_term
                dk = dk_term if dk is None else dk + dk_term
                dq_now[g, h] += dot_tn(keys, grad_scores)
            dkv_now[:, key_lanes] = dk * SCORE_SCALE
            dkv_now[:, value_lanes] = dv
            return carry

        lax.fori_loop(0, KV_HEADS, group, 0)

    def inner_of(g, carry):
        for h in range(GROUP):
            lanes = pl.ds(pl.multiple_of((g * GROUP + h) * HEAD_DIM, HEAD_DIM), HEAD_DIM)
            both = do_ref[:, lanes].astype(jnp.float32) * mixed_ref[:, lanes].astype(jnp.float32)
            inner_now[g, h : h + 1, :] = jnp.sum(both.T, axis=0, keepdims=True)
        return carry

    lax.fori_loop(0, KV_HEADS, inner_of, 0)
    for r in range(n - 1, -1, -1):
        @pl.when(z >= r)
        def _(r=r):
            block(r)
            if r < n - 1:
                @pl.when(z < n - 1)
                def _():
                    copies[r + 1].wait_recv()
                    dkv_now[...] += came[r].astype(jnp.float32)
            if r:
                leaving[r - 1] = dkv_now[...].astype(jnp.bfloat16)
                copies[r].start()
            else:
                for g in range(KV_HEADS):
                    put(q_cols + g * HEAD_DIM, turned_back(dkv_now[:, g * HEAD_DIM : (g + 1) * HEAD_DIM]))
                grad_ref[:, q_cols + values_at :] = dkv_now[:, values_at:].astype(jnp.bfloat16)

        if parts and r == n - 1:
            scatter.turn()
            for k in every:
                scatter.begin(k)
        if parts and r == max(n - 2, 0):
            tokens.middle()
            for k in every:
                scatter.across_first(k)
        if parts and r == max(n - 3, 0):
            for k in every:
                scatter.across_second(k)
    if parts:
        for k in every:
            scatter.end(k)
        out_sum[...] = scatter.total[p.t]
        tokens.end()

    def finish(g, carry):
        for h in range(GROUP):
            lanes = pl.ds(pl.multiple_of((g * GROUP + h) * HEAD_DIM, HEAD_DIM), HEAD_DIM)
            grad_ref[:, lanes] = turned_back(dq_now[g, h].T * SCORE_SCALE).astype(jnp.bfloat16)
        return carry

    lax.fori_loop(0, KV_HEADS, finish, 0)
    for r in range(1, n):
        @pl.when(z >= r)
        def _(r=r):
            copies[r].wait_send()
    c.end()


def attend_back(
    query, kv_all, grad, total, mixed, key_code, query_code, query_base, cosine, sine, n, collective_id, branch_grad=None,
    down_terms=(), planes=0,
):
    rows, width = query.shape
    kv_cols = kv_all.shape[1]
    in_vmem = pl.BlockSpec(memory_space=pltpu.VMEM)
    slots = max(n - 1, 1)
    more, parts, shapes, scratch = (), [], (), []
    if branch_grad is not None:
        more, parts = (branch_grad, *down_terms), plane_parts(width, 2)
        came = jax.ShapeDtypeStruct((rows, width), jnp.bfloat16)
        shapes = (jax.ShapeDtypeStruct((width // planes // 2, width), jnp.bfloat16), came, came)
        scratch = plane_scratch(rows, width, width, planes)
        scratch += [pltpu.VMEM((count, width), jnp.bfloat16) for count in (2 * rows, rows // 2, rows // 2)]
        scratch.append(pltpu.SemaphoreType.DMA)
    copies = n + 4 * len(parts) + 4
    any_spec = pl.BlockSpec(memory_space=pl.ANY)
    return pl.pallas_call(
        functools.partial(attend_back_kernel, n, parts),
        in_specs=[in_vmem] * (10 + len(more[:1])) + [any_spec] * len(more[1:]),
        out_specs=(in_vmem,) * (1 + len(shapes[:1])) + (any_spec,) * len(shapes[1:]),
        out_shape=(jax.ShapeDtypeStruct((rows, width + kv_cols), jnp.bfloat16),) + shapes,
        scratch_shapes=[
            pltpu.VMEM((KV_HEADS, GROUP, HEAD_DIM, rows), jnp.float32),
            pltpu.VMEM((rows, kv_cols), jnp.float32),
            pltpu.VMEM((rows, rows), jnp.float32),
            pltpu.VMEM((KV_HEADS, GROUP, rows), jnp.float32),
            pltpu.VMEM((slots, rows, kv_cols), jnp.bfloat16),
            pltpu.VMEM((slots, rows, kv_cols), jnp.bfloat16),
            pltpu.SemaphoreType.DMA((copies,)),
            pltpu.SemaphoreType.DMA((copies,)),
        ]
        + scratch,
        compiler_params=pltpu.CompilerParams(
            vmem_limit_bytes=60 * 1024 * 1024, collective_id=collective_id, has_side_effects=True
        ),
        cost_estimate=pl.CostEstimate(
            flops=72 * rows * n * rows * width, bytes_accessed=16 * rows * width, transcendentals=HEADS * rows * n * rows
        ),
        name="attend_back",
    )(query, kv_all, grad, total, mixed, key_code, query_code, query_base, cosine, sine, *more)


def rotary_tables(positions):
    half_dim = HEAD_DIM // 2
    frequency = jnp.power(10000.0, -2.0 * jnp.arange(half_dim, dtype=jnp.float32) / HEAD_DIM)
    angles = positions[:, None] * frequency[None, :]
    return (jnp.cos(angles), jnp.sin(angles))


def norm_forward(values_in, gain_row):
    inverse = lax.rsqrt(jnp.mean(values_in * values_in, axis=-1, keepdims=True) + EPSILON)
    return (values_in * inverse * gain_row, inverse)


def norm_backward(values_in, inverse, gain_row, incoming):
    scaled_grad = incoming * gain_row
    return inverse * scaled_grad - values_in * inverse * inverse * inverse * jnp.mean(
        scaled_grad * values_in, axis=-1, keepdims=True
    )


def advance_state(weight, moment, average, gradient):
    moment_next = MOMENTUM * moment + gradient
    weight_next = weight - STEP_RATE * (gradient + MOMENTUM * moment_next)
    average_next = AVERAGING * average + (1.0 - AVERAGING) * weight_next
    return (weight_next, moment_next, average_next)


class Links:
    def __init__(self):
        self.wide = lax.axis_size("wide")
        self.n = lax.axis_size("narrow")
        self.planes = self.wide // 2
        self.wide_at = lax.axis_index("wide")
        self.z_at = lax.axis_index("narrow")
        self.t_at = self.wide_at // 2
        self.core_at = self.wide_at % 2
        self.bits = [1 << k for k in range(self.planes.bit_length() - 1)]
        per_chip = 2 * self.n
        self.same_chip = [[t * per_chip + j for j in range(per_chip)] for t in range(self.planes)]
        self.same_plane = [
            [t * per_chip + j for t in range(self.planes)] for j in range(per_chip)
        ]

    def swap(self, values, flip):
        pairs = [(i, i ^ (flip * self.n)) for i in range(self.wide * self.n)]
        return lax.ppermute(values, MESH_AXES, pairs)

    def column_cuts(self, cols):
        lanes = cols // 128
        count = len(self.bits)
        edges = [128 * (lanes * k // count) for k in range(count + 1)]
        orders = [self.bits[k:] + self.bits[:k] for k in range(count)]
        return list(zip(edges[:-1], edges[1:], orders))

    def scatter_core(self, term):
        mine = lax.dynamic_index_in_dim(term, self.core_at, 1, keepdims=False)
        other = lax.dynamic_index_in_dim(term, 1 - self.core_at, 1, keepdims=False)
        got = self.swap(other, 1)
        return (mine.astype(jnp.float32) + got.astype(jnp.float32)).astype(jnp.bfloat16)

    def scatter_rows(self, term):
        rows, cols = term.shape
        term = term.reshape(self.planes, 2, rows // self.wide, cols)
        term = self.scatter_core(term)
        parts = []
        for low, high, order in self.column_cuts(cols):
            part = term[:, :, low:high]
            left = sorted(self.bits, reverse=True)
            part = part.reshape((2,) * len(left) + part.shape[1:])
            for bit in order:
                axis = left.index(bit)
                my_bit = (self.t_at // bit) % 2
                mine = lax.dynamic_index_in_dim(part, my_bit, axis, keepdims=False)
                other = lax.dynamic_index_in_dim(part, 1 - my_bit, axis, keepdims=False)
                got = self.swap(other, 2 * bit)
                part = (mine.astype(jnp.float32) + got.astype(jnp.float32)).astype(jnp.bfloat16)
                left.remove(bit)
            parts.append(part)
        total = jnp.concatenate(parts, axis=1)
        return lax.psum_scatter(total, "narrow", scatter_dimension=0, tiled=True)

    def gather_tokens(self, rows):
        if self.planes != 4:
            every = lax.all_gather(
                rows, MESH_AXES, axis=0, tiled=False, axis_index_groups=self.same_plane
            )
            return [every[k] for k in range(self.planes)]
        half = rows.shape[0] // 2
        by_x = self.swap(rows, 2)
        by_y = self.swap(rows, 4)
        corner = [self.swap(by_y[:half], 2), self.swap(by_x[half:], 4)]
        return [rows, by_x, by_y, jnp.concatenate(corner)]

    def scatter_tokens(self, parts, cap):
        every = jnp.concatenate(parts)
        if self.planes != 4:
            total = lax.psum_scatter(
                every, MESH_AXES, scatter_dimension=0, tiled=True, axis_index_groups=self.same_plane
            )
            return total.astype(jnp.float32)
        total = every[:cap].astype(jnp.float32)
        for k in range(1, 4):
            total += self.swap(every[k * cap : (k + 1) * cap], 2 * k).astype(jnp.float32)
        return total

    def gather_chip(self, pieces):
        every = lax.all_gather(pieces, MESH_AXES, axis=1, tiled=True, axis_index_groups=self.same_chip)
        return every.reshape(-1, every.shape[-1])

    def plane_counts(self, counts, cap):
        if self.planes != 4:
            return jnp.full((self.planes,), cap, jnp.int32)
        at = [((self.t_at ^ d) * 2 + self.core_at) * self.n + self.z_at for d in range(4)]
        return counts[jnp.stack(at)]

    def trade_columns(self, pieces):
        came = jnp.zeros_like(pieces)
        for d in range(self.planes):
            piece = lax.dynamic_index_in_dim(pieces, self.t_at ^ d, 0)
            if d:
                piece = self.swap(piece, 2 * d)
            came = lax.dynamic_update_slice(came, piece, (self.t_at ^ d, 0, 0))
        return came

    def gather_first(self, qkv, out, gateup, down, gains, count):
        rows = qkv.shape[0]
        low = jnp.bfloat16
        if self.planes == 4 and self.n > 1:
            digits = jnp.stack([count // 16, count % 16]).astype(low)
            ext = jnp.concatenate([gains.reshape(1, 2 * rows), jnp.zeros((15, 2 * rows), gains.dtype)])
            ext = lax.dynamic_update_slice(ext, digits[None], (1, 0))
            qkv_all, out_all, ext_all, came, down_all = gather_first(
                qkv, out, gateup, down, ext, self.planes, self.n
            )
            ext_all = ext_all.reshape(self.wide * self.n, 16, 2 * rows)
            gain_full = ext_all[:, 0].reshape(-1, 2, rows).transpose(1, 0, 2).reshape(2, -1)
            digits = ext_all[:, 1, :2].astype(jnp.int32)
            return (
                qkv_all.reshape(self.wide * self.n * rows, -1),
                out_all,
                came,
                down_all.reshape(-1, down.shape[1]),
                gain_full,
                digits[:, 0] * 16 + digits[:, 1],
            )
        return (
            lax.all_gather(qkv.astype(low), MESH_AXES, axis=0, tiled=True),
            lax.all_gather(out.astype(low), MESH_AXES, axis=0, tiled=True),
            self.trade_columns(split_columns(gateup.astype(low), self.planes)),
            lax.all_gather(
                down.astype(low), MESH_AXES, axis=0, tiled=True, axis_index_groups=self.same_chip
            ),
            lax.all_gather(gains, MESH_AXES, axis=1, tiled=True),
            lax.all_gather(count, MESH_AXES),
        )


def dot32(a, b):
    return jnp.dot(a, b, preferred_element_type=jnp.float32)


def dot_low(a, b):
    return jnp.dot(a, b, preferred_element_type=jnp.float32).astype(jnp.bfloat16)


def together(arrays):
    return arrays[0] if len(arrays) == 1 else jnp.concatenate(arrays)


def split_columns(shard, planes):
    units = FF // planes
    found = []
    for t in range(planes):
        for low, high in unit_groups(units):
            for start in (t * units, FF + t * units):
                found.append(shard[:, start + low : start + high])
    return jnp.concatenate(found, axis=1).reshape(shard.shape[0], planes, 2 * units).transpose(1, 0, 2)


def join_columns(pieces):
    planes, _, cols = pieces.shape
    gates, uppers = [], []
    for t in range(planes):
        for low, high in unit_groups(cols // 2):
            gates.append(pieces[t, :, 2 * low : low + high])
            uppers.append(pieces[t, :, low + high : 2 * high])
    return jnp.concatenate(gates + uppers, axis=1)


def pick_live(mask, cap):
    flat = mask.reshape(-1)
    rows = flat.shape[0]
    at = jnp.arange(rows, dtype=jnp.int32)
    rank = jnp.sum(jnp.where(at[None, :] <= at[:, None], flat[None, :], 0), axis=1) - 1
    slot = jnp.arange(cap, dtype=jnp.int32)
    chosen = (rank[None, :] == slot[:, None]) & (flat[None, :] == 1)
    return chosen, slot < jnp.sum(flat)


def layer(links, cap, given):
    (
        tokens,
        active,
        cotangent,
        gain_full,
        counts,
        qkv_low,
        out_all,
        pieces,
        down_low,
    ) = given
    n, planes = links.n, links.planes
    seq_count, span_len, width = tokens.shape
    row_count = seq_count * span_len
    seq_len = n * span_len
    kv_width = KV_HEADS * HEAD_DIM
    ff_part = FF // planes
    shard_rows = pieces.shape[1]
    low = jnp.bfloat16


    first_cols = 2 * UNIT_GROUP * max(ff_part // UNIT_GROUP * 2 // 5, 1)
    gateup_first = links.gather_chip(pieces[:, :, :first_cols])

    def codes_of(block):
        mask = lax.dynamic_slice_in_dim(active, jnp.maximum(block, 0) * span_len, span_len, 1)
        chosen, live = pick_live(mask, cap)
        code = jnp.arange(seq_count, dtype=jnp.int32)[:, None] * seq_len + jnp.arange(span_len, dtype=jnp.int32)
        code = jnp.sum(jnp.where(chosen, code.reshape(1, -1), 0), axis=1) + block * span_len
        return chosen, live & (block >= 0), code

    chosen, live, own_code = codes_of(links.z_at)
    key_codes = []
    for r in range(n):
        _, there, code = codes_of(links.z_at - r)
        key_codes.append(jnp.where(there, code, seq_count * seq_len))
    key_code = jnp.concatenate(key_codes)[:, None]
    query_code = jnp.where(live, own_code, -1)[None]
    query_base = jnp.where(live, own_code // seq_len * seq_len, 0)[None]
    places = jnp.where(live, own_code % seq_len, 0).astype(jnp.float32)
    cosine_table, sine_table = rotary_tables(places)
    picker = chosen.astype(low)
    live_rows = live.astype(jnp.float32)[:, None]

    inputs = dot32(picker, tokens.reshape(row_count, width))
    down_grad = dot_low(picker, cotangent.reshape(row_count, width))
    upstream = down_grad.astype(jnp.float32)

    cosine = jnp.concatenate([cosine_table, cosine_table], axis=1)
    sine = jnp.concatenate([-sine_table, sine_table], axis=1)
    ids = 1 if cap < row_count else 3
    codes = (key_code, query_code, query_base)
    first = (inputs, gain_full[:1], cosine, sine, qkv_low, *codes, n, ids)
    if out_all.ndim == 2:
        out_low = out_all
        normed_low, inverse_one, query_low, attended_low, totals, kv_all = attend(*first)
        down_grad_blocks = links.gather_tokens(down_grad)
    else:
        normed_low, inverse_one, query_low, attended_low, totals, kv_all, out_all, *others = attend(
            *first, down_grad, out_all
        )
        down_grad_blocks = [down_grad, *others]
        out_low = out_all.reshape(width, width)
    pieces_last, attended_low = lax.optimization_barrier((pieces[:, :, first_cols:], attended_low))
    gateup_last = links.gather_chip(pieces_last)
    middle = inputs + live_rows * dot32(attended_low, out_low)
    normed_mid, inverse_two = norm_forward(middle, gain_full[1])
    blocks = links.gather_tokens(normed_mid.astype(low))
    lives = links.plane_counts(counts, cap)

    parts = [[k] for k in range(planes)] if planes != 4 else [[0], [1, 2], [3]]
    hidden_blocks, gateup_grad_blocks, back_parts, down_parts = [], [], [], []
    row_parts, grad_parts = [], []
    for part in parts:
        rows = together([blocks[k] for k in part])
        grads = together([down_grad_blocks[k] for k in part])
        row_parts.append(rows)
        grad_parts.append(grads)
        hidden, gateup_grad, back, down_part = mlp_block(
            rows, grads, lives[jnp.array(part)], gateup_first, gateup_last, down_low, cap
        )
        hidden_blocks.append(hidden)
        gateup_grad_blocks.append(gateup_grad)
        back_parts.append(back)
        down_parts.append(down_part)
    if planes == 4 and n > 1 and cap <= 384:
        grad_normed_mid, down_half, gateup_half = mid_back(
            back_parts, row_parts, gateup_grad_blocks, hidden_blocks, grad_parts, cap, planes, n, ids + 8
        )
    else:
        grad_normed_mid = links.scatter_tokens(back_parts, cap)
        term_down = dot_low(jnp.concatenate(hidden_blocks).T, jnp.concatenate(grad_parts))
        down_half = links.scatter_core(term_down.reshape(1, 2, ff_part // 2, width))[0]
        term_gateup = dot_low(jnp.concatenate(row_parts).T, jnp.concatenate(gateup_grad_blocks))
        gateup_half = links.scatter_core(term_gateup.reshape(planes, 2, n * shard_rows, 2 * ff_part))
    grad_pieces = lax.psum_scatter(gateup_half, "narrow", scatter_dimension=1, tiled=True)

    grad_middle = upstream + norm_backward(middle, inverse_two, gain_full[1], grad_normed_mid)
    branch_grad_low = grad_middle.astype(low)
    grad_attended_low = dot_low(branch_grad_low, out_low.T)
    back = (query_low, kv_all, grad_attended_low, totals, attended_low, *codes, cosine, sine, n, ids + 1)
    if planes == 4 and n > 1:
        grad_projected_low, out_sum, *came = attend_back(*back, branch_grad_low, down_parts, planes)
        down_proj = sum((part.astype(jnp.float32) for part in came), down_parts[0].astype(jnp.float32))
        down_half, grad_pieces, grad_projected_low = lax.optimization_barrier(
            (down_half, grad_pieces, grad_projected_low)
        )
        grad_qkv, grad_normed, grad_gateup, grad_out = qkv_back(
            normed_low, grad_projected_low, qkv_low, grad_pieces, out_sum, planes, n, ids + 4
        )
    else:
        grad_projected_low = attend_back(*back)[0]
        down_proj = links.scatter_tokens(down_parts, cap)
        grad_out = links.scatter_rows(dot_low(attended_low.T, branch_grad_low))
        grad_qkv = links.scatter_rows(dot_low(normed_low.T, grad_projected_low)).astype(jnp.float32)
        grad_normed = dot32(grad_projected_low, qkv_low.T)
        grad_gateup = join_columns(links.trade_columns(grad_pieces)).astype(jnp.float32)
    grad_tokens = (
        grad_middle + norm_backward(inputs, inverse_one, gain_full[0], grad_normed)
    ).astype(low)

    grad_down = lax.psum_scatter(down_half, "narrow", scatter_dimension=0, tiled=True)
    layer_out = (middle + down_proj).astype(low)

    def spread(packed, skipped):
        back = lax.dot_general(
            picker, packed, (((0,), (0,)), ((), ())), preferred_element_type=jnp.float32
        ).astype(low)
        mask = lax.dynamic_slice_in_dim(active, links.z_at * span_len, span_len, 1)
        return jnp.where(mask[:, :, None] == 1, back.reshape(skipped.shape), skipped)

    layer_out, grad_tokens = spread(layer_out, tokens), spread(grad_tokens, cotangent)
    return layer_out, grad_tokens, grad_qkv, grad_out, grad_gateup, grad_down


def on_device(
    tokens,
    active,
    cotangent,
    gain_rows,
    w_qkv,
    w_out,
    w_gateup,
    w_down,
    moment_gains,
    moment_qkv,
    moment_out,
    moment_gateup,
    moment_down,
    average_gains,
    average_qkv,
    average_out,
    average_gateup,
    average_down,
):
    links = Links()
    seq_count, span_len, _ = tokens.shape
    row_count = seq_count * span_len
    low = jnp.bfloat16

    gains_low = gain_rows.astype(low)
    own_mask = lax.dynamic_slice_in_dim(active, links.z_at * span_len, span_len, 1)
    qkv_low, out_all, pieces, down_low, gain_full, counts = links.gather_first(
        w_qkv, w_out, w_gateup, w_down, gains_low, jnp.sum(own_mask)
    )
    gain_full = gain_full.astype(jnp.float32)
    given = (tokens, active, cotangent, gain_full, counts, qkv_low, out_all, pieces, down_low)
    few = -(-3 * row_count // 4 // 128) * 128
    if few < row_count:
        found = lax.cond(
            jnp.max(counts) <= few,
            lambda *g: layer(links, few, g),
            lambda *g: layer(links, row_count, g),
            *given,
        )
    else:
        found = layer(links, row_count, given)
    layer_out, grad_tokens, grad_qkv, grad_out, grad_gateup, grad_down = found
    grad_qkv, grad_out, grad_gateup, grad_down = (
        g.astype(jnp.float32) for g in (grad_qkv, grad_out, grad_gateup, grad_down)
    )

    def gain_grad(shard, gradient, row):
        return jnp.sum(shard.astype(low).astype(jnp.float32) * gradient, axis=1) / gains_low[row].astype(jnp.float32)

    grad_gains = jnp.stack([gain_grad(w_qkv, grad_qkv, 0), gain_grad(w_gateup, grad_gateup, 1)])
    state_gains = advance_state(gain_rows, moment_gains, average_gains, grad_gains)
    state_qkv = advance_state(w_qkv, moment_qkv, average_qkv, grad_qkv)
    state_out = advance_state(w_out, moment_out, average_out, grad_out)
    state_gateup = advance_state(w_gateup, moment_gateup, average_gateup, grad_gateup)
    state_down = advance_state(w_down, moment_down, average_down, grad_down)
    return (
        layer_out,
        grad_tokens,
        grad_gains,
        grad_qkv,
        grad_out,
        grad_gateup,
        grad_down,
        state_gains[0],
        state_qkv[0],
        state_out[0],
        state_gateup[0],
        state_down[0],
        state_gains[1],
        state_qkv[1],
        state_out[1],
        state_gateup[1],
        state_down[1],
        state_gains[2],
        state_qkv[2],
        state_out[2],
        state_gateup[2],
        state_down[2],
    )


def solution(mesh):
    in_specs = (
        P("wide", "narrow", None),
        P("wide", None),
        P("wide", "narrow", None),
        P(None, ("wide", "narrow")),
        P(("wide", "narrow"), None),
        P(("wide", "narrow"), None),
        P(("wide", "narrow"), None),
        P(("wide", "narrow"), None),
        P(None, ("wide", "narrow")),
        P(("wide", "narrow"), None),
        P(("wide", "narrow"), None),
        P(("wide", "narrow"), None),
        P(("wide", "narrow"), None),
        P(None, ("wide", "narrow")),
        P(("wide", "narrow"), None),
        P(("wide", "narrow"), None),
        P(("wide", "narrow"), None),
        P(("wide", "narrow"), None),
    )
    out_specs = (
        P("wide", "narrow", None),
        P("wide", "narrow", None),
        P(None, ("wide", "narrow")),
        P(("wide", "narrow"), None),
        P(("wide", "narrow"), None),
        P(("wide", "narrow"), None),
        P(("wide", "narrow"), None),
        P(None, ("wide", "narrow")),
        P(("wide", "narrow"), None),
        P(("wide", "narrow"), None),
        P(("wide", "narrow"), None),
        P(("wide", "narrow"), None),
        P(None, ("wide", "narrow")),
        P(("wide", "narrow"), None),
        P(("wide", "narrow"), None),
        P(("wide", "narrow"), None),
        P(("wide", "narrow"), None),
        P(None, ("wide", "narrow")),
        P(("wide", "narrow"), None),
        P(("wide", "narrow"), None),
        P(("wide", "narrow"), None),
        P(("wide", "narrow"), None),
    )
    return jax.shard_map(
        on_device, mesh=mesh, in_specs=in_specs, out_specs=out_specs, check_vma=False
    )
```

```python
import functools

import jax
import jax.numpy as jnp
from jax import lax
from jax.experimental import pallas as pl
from jax.experimental.pallas import tpu as pltpu
from jax.sharding import PartitionSpec as P

HEADS = 16
KV_HEADS = 4
HEAD_DIM = 128
GROUP = HEADS // KV_HEADS
FF = 5632


EPSILON = 1e-05
MOMENTUM = 0.5
AVERAGING = 0.5
STEP_RATE = 0.0003

MESH = pl.DeviceIdType.MESH
MESH_AXES = ("wide", "narrow")
SCORE_SCALE = HEAD_DIM ** (-0.5)
LOG2_E = 1.4426950408889634
MASKED = -1e30


def dot_nt(a, b):
    return lax.dot_general(a, b, (((1,), (1,)), ((), ())), preferred_element_type=jnp.float32)


def dot_tn(a, b):
    return lax.dot_general(a, b, (((0,), (0,)), ((), ())), preferred_element_type=jnp.float32)


UNIT_GROUP = 256
WIDTH_GROUP = 256
LANES = 128


def unit_groups(units):
    return [(low, min(low + UNIT_GROUP, units)) for low in range(0, units, UNIT_GROUP)]


def first_columns(units):
    return 2 * UNIT_GROUP * max(units // UNIT_GROUP * 2 // 5, 1)


def mlp_kernel(
    cap, counts, live_ref, rows_ref, grad_ref, gateup_first, gateup_last, down_hbm,
    hidden_ref, gateup_grad_ref, back_ref, out_ref, gateup_ref, down_ref, gateup_sems, down_sems,
):
    step = pl.program_id(0)
    width = rows_ref.shape[1]
    units = down_ref.shape[0]
    full, rest = units // UNIT_GROUP, units % UNIT_GROUP
    live = live_ref[step]

    def span(low, size):
        return pl.ds(low if isinstance(low, int) else pl.multiple_of(low, size), size)

    def gateup_part(k, low, size, to=None):
        both = span(2 * low, 2 * size)
        into = both if to is None else span(2 * to, 2 * size)
        first = gateup_first.shape[1]
        held = gateup_first.at[:, both] if 2 * low < first else gateup_last.at[:, span(2 * low - first, 2 * size)]
        return pltpu.make_async_copy(held, gateup_ref.at[:, into], gateup_sems.at[k])

    def down_part(k, low, size):
        one = span(low, size)
        return pltpu.make_async_copy(down_hbm.at[one, :], down_ref.at[one, :], down_sems.at[k])

    @pl.when(step == 0)
    def _():
        for k, (low, high) in enumerate(unit_groups(units)):
            gateup_part(k, low, high - low).start()
            down_part(k, low, high - low).start()

    def run(count):
        def units_step(k, low, size):
            @pl.when(step == 0)
            def _():
                gateup_part(k, 0 if size == UNIT_GROUP else low, size, low).wait()
                down_part(k, low, size).wait()

            both, one = span(2 * low, 2 * size), span(low, size)
            gate_up = jnp.dot(rows_ref[:count, :], gateup_ref[:, both], preferred_element_type=jnp.float32)
            gate, upper = gate_up[:, :size], gate_up[:, size:]
            grad_hidden = dot_nt(grad_ref[:count, :], down_ref[one, :])
            sigmoid = 1.0 / (1.0 + jnp.exp(-gate))
            silu = gate * sigmoid
            hidden_ref[:count, one] = (silu * upper).astype(jnp.bfloat16)
            grad_gate = grad_hidden * upper * (sigmoid + silu * (1.0 - sigmoid))
            grad_upper = grad_hidden * silu
            gateup_grad_ref[:count, both] = jnp.concatenate([grad_gate, grad_upper], axis=1).astype(jnp.bfloat16)

        lax.fori_loop(0, full, lambda k, c: (units_step(k, k * UNIT_GROUP, UNIT_GROUP), c)[1], 0)
        if rest:
            units_step(full, full * UNIT_GROUP, rest)

        def back_step(k, carry):
            at = span(k * WIDTH_GROUP, WIDTH_GROUP)
            back_ref[:count, at] = dot_nt(gateup_grad_ref[:count, :], gateup_ref[at, :]).astype(jnp.bfloat16)
            out = jnp.dot(hidden_ref[:count, :], down_ref[:, at], preferred_element_type=jnp.float32)
            out_ref[:count, at] = out.astype(jnp.bfloat16)
            return carry

        lax.fori_loop(0, width // WIDTH_GROUP, back_step, 0)
        if count < cap:
            for ref in (hidden_ref, gateup_grad_ref, back_ref, out_ref):
                ref[count:, :] = jnp.zeros((cap - count, ref.shape[1]), ref.dtype)

    for low, count in zip((None,) + counts[:-1], counts):
        chosen = live > (-1 if low is None else low)
        if count < cap:
            chosen &= live <= count

        @pl.when(chosen)
        def _(count=count):
            run(count)


def mlp_block(rows, grad, live, gateup_first, gateup_last, down, cap):
    blocks = rows.shape[0] // cap
    width = rows.shape[1]
    units = down.shape[0]
    if units % 128 or cap % 128:
        return mlp_plain(rows, grad, jnp.concatenate([gateup_first, gateup_last], axis=1), down)
    gateup_cols = gateup_first.shape[1] + gateup_last.shape[1]
    counts = (192, 256, 320, 384) if cap == 384 else tuple(range(256, cap, 256)) + (cap,)
    groups = len(unit_groups(units))
    low = jnp.bfloat16
    by_block = lambda cols: pl.BlockSpec((cap, cols), lambda b, live: (b, 0))
    return pl.pallas_call(
        functools.partial(mlp_kernel, cap, counts),
        grid_spec=pltpu.PrefetchScalarGridSpec(
            num_scalar_prefetch=1,
            grid=(blocks,),
            in_specs=[by_block(width), by_block(width)] + [pl.BlockSpec(memory_space=pl.ANY)] * 3,
            out_specs=(by_block(units), by_block(2 * units), by_block(width), by_block(width)),
            scratch_shapes=[
                pltpu.VMEM((width, gateup_cols), low),
                pltpu.VMEM(down.shape, low),
                pltpu.SemaphoreType.DMA((groups,)),
                pltpu.SemaphoreType.DMA((groups,)),
            ],
        ),
        out_shape=(
            jax.ShapeDtypeStruct((blocks * cap, units), low),
            jax.ShapeDtypeStruct((blocks * cap, 2 * units), low),
            jax.ShapeDtypeStruct((blocks * cap, width), low),
            jax.ShapeDtypeStruct((blocks * cap, width), low),
        ),
        compiler_params=pltpu.CompilerParams(vmem_limit_bytes=56 * 1024 * 1024),
        cost_estimate=pl.CostEstimate(
            flops=12 * blocks * cap * width * units,
            bytes_accessed=2 * (width * gateup_cols + down.size) + 12 * blocks * cap * width,
            transcendentals=blocks * cap * units,
        ),
        name="mlp_block",
    )(live, rows, grad, gateup_first, gateup_last, down)


def mlp_plain(rows, grad, gateup, down):
    groups = unit_groups(down.shape[0])
    gate_up = jnp.dot(rows, gateup, preferred_element_type=jnp.float32)
    gate = jnp.concatenate([gate_up[:, 2 * low : low + high] for low, high in groups], axis=1)
    upper = jnp.concatenate([gate_up[:, low + high : 2 * high] for low, high in groups], axis=1)
    grad_hidden = jnp.dot(grad, down.T, preferred_element_type=jnp.float32)
    sigmoid = jax.nn.sigmoid(gate)
    silu = gate * sigmoid
    hidden = (silu * upper).astype(jnp.bfloat16)
    grad_gate = grad_hidden * upper * (sigmoid + silu * (1.0 - sigmoid))
    grad_upper = grad_hidden * silu
    gateup_grad = jnp.concatenate(
        [part[:, low:high] for low, high in groups for part in (grad_gate, grad_upper)], axis=1
    ).astype(jnp.bfloat16)
    back = jnp.dot(gateup_grad, gateup.T, preferred_element_type=jnp.float32).astype(jnp.bfloat16)
    out = jnp.dot(hidden, down, preferred_element_type=jnp.float32).astype(jnp.bfloat16)
    return hidden, gateup_grad, back, out


class Place:
    def __init__(self, n):
        self.n = n
        self.wide = lax.axis_index("wide")
        self.z = lax.axis_index("narrow")
        self.t, self.core = self.wide // 2, self.wide % 2
        self.t_x, self.t_y, self.t_d = self.t ^ 1, self.t ^ 2, self.t ^ 3
        self.by_x = self.device(self.t_x)
        self.by_y = self.device(self.t_y)
        self.by_d = self.device(self.t_d)
        self.sibling = self.device(self.t, core=1 - self.core)
        self.above = self.device(self.t, z=jnp.minimum(self.z + 1, n - 1))
        self.below = self.device(self.t, z=jnp.maximum(self.z - 1, 0))

    def device(self, t, core=None, z=None):
        return (t * 2 + (self.core if core is None else core), self.z if z is None else z)

    def greet(self, others):
        barrier = pltpu.get_barrier_semaphore()
        for other in others:
            pl.semaphore_signal(barrier, inc=1, device_id=other, device_id_type=MESH)

        @pl.when(self.z > 0)
        def _():
            pl.semaphore_signal(barrier, inc=1, device_id=self.below, device_id_type=MESH)

        @pl.when(self.z < self.n - 1)
        def _():
            pl.semaphore_signal(barrier, inc=1, device_id=self.above, device_id_type=MESH)

        inner = (self.z > 0).astype(jnp.int32) + (self.z < self.n - 1).astype(jnp.int32)
        pl.semaphore_wait(barrier, len(others) + inner)


class Copies:
    def __init__(self, send_sems, recv_sems):
        self.send_sems, self.recv_sems = send_sems, recv_sems
        self.count = 0
        self.started = []

    def make(self, src, dst, to):
        k = self.count
        self.count += 1
        return pltpu.make_async_remote_copy(
            src_ref=src, dst_ref=dst, send_sem=self.send_sems.at[k], recv_sem=self.recv_sems.at[k],
            device_id=to, device_id_type=MESH,
        )

    def same(self, ref, to):
        return self.make(ref, ref, to)

    def each(self, moves, when, act):
        def run():
            for m in moves:
                act(m)

        if when is None:
            run()
        else:
            pl.when(when)(run)

    def go(self, moves, when=None):
        self.each(moves, when, lambda m: m.start())
        self.started.append((moves, when))

    def arrive(self, moves, when=None):
        self.each(moves, when, lambda m: m.wait_recv())

    def end(self):
        for moves, when in self.started:
            self.each(moves, when, lambda m: m.wait_send())


class LineGather:
    def __init__(self, place, copies, view, own):
        self.place, self.copies, self.view, self.own = place, copies, view, own
        self.up, self.down = {}, {}

    def send(self, step):
        p, last = self.place, self.place.n - 1
        block = self.view(jnp.maximum(p.z - (step - 1), 0))
        self.up[step] = self.copies.make(self.own if step == 1 else block, block, p.above)
        self.copies.go([self.up[step]], (p.z - (step - 1) >= 0) & (p.z < last))
        block = self.view(jnp.minimum(p.z + (step - 1), last))
        self.down[step] = self.copies.make(self.own if step == 1 else block, block, p.below)
        self.copies.go([self.down[step]], (p.z + (step - 1) <= last) & (p.z > 0))

    def take(self, step):
        p = self.place
        self.copies.arrive([self.up[step]], p.z - step >= 0)
        self.copies.arrive([self.down[step]], p.z + step <= p.n - 1)

    def hand_over(self, step):
        p, last = self.place, self.place.n - 1
        moves = []
        for at, there in ((p.z - step, p.z - step >= 0), (p.z + step, p.z + step <= last)):
            block = self.view(jnp.clip(at, 0, last))
            move = self.copies.same(block, p.sibling)
            self.copies.go([move], there)
            moves.append(([move], there))
        return moves


def gather_kernel(
    n, qkv_ref, out_ref, gateup_ref, down_ref, ext_ref, qkv_all, out_all, ext_all, came_first, came_last,
    down_all, qkv_low, out_low, trade_low, down_low, send_sems, recv_sems, local_sems,
):
    p = Place(n)
    c = Copies(send_sems, recv_sems)
    t, core, z = p.t, p.core, p.z
    low = jnp.bfloat16
    qkv_low[...] = qkv_ref[...].astype(low)
    p.greet([p.by_x, p.by_y, p.by_d, p.sibling])

    half = qkv_ref.shape[1] // 256 * 128
    qa, qb = slice(0, half), slice(half, qkv_ref.shape[1])
    lines = [
        LineGather(p, c, lambda zz, cols=cols: qkv_all.at[t, core, zz, :, cols], qkv_low.at[:, cols])
        for cols in (qa, qb)
    ]
    lines.append(LineGather(p, c, lambda zz: ext_all.at[t, core, zz], ext_ref))
    for line in lines:
        line.send(1)
    local = []

    def place(src, dst):
        move = pltpu.make_async_copy(src, dst, local_sems.at[len(local)])
        move.start()
        local.append(move)

    place(qkv_low, qkv_all.at[t, core, z])
    place(ext_ref, ext_all.at[t, core, z])
    units = trade_low.shape[2] // 2
    for k in range(trade_low.shape[0]):
        for first, last in unit_groups(units):
            for to, start in ((2 * first, k * units), (first + last, gateup_ref.shape[1] // 2 + k * units)):
                trade_low[k, :, to : to + last - first] = gateup_ref[:, start + first : start + last].astype(low)
    cut = came_first.shape[2]
    halves = ((slice(0, cut), came_first), (slice(cut, 2 * units), came_last))
    for cols, came in halves:
        place(trade_low.at[t, :, cols], came.at[t])
    trade = [
        c.make(trade_low.at[k, :, cols], came.at[t], to)
        for cols, came in halves
        for k, to in ((p.t_x, p.by_x), (p.t_y, p.by_y), (p.t_d, p.by_d))
    ]
    c.go(trade)
    out_low[...] = out_ref[...].astype(low)
    down_low[...] = down_ref[...].astype(low)
    place(out_low, out_all.at[t, core, z])
    place(down_low, down_all.at[core, z])
    line_out = LineGather(p, c, lambda zz: out_all.at[t, core, zz], out_low)
    line_down = LineGather(p, c, lambda zz: down_all.at[core, zz], down_low)
    down_own = c.make(down_low, down_all.at[core, z], p.sibling)
    c.go([down_own])
    handed = [([down_own], None)]
    for step in range(1, n):
        for line in lines:
            line.take(step)
            if step < n - 1:
                line.send(step + 1)
    for move in local:
        move.wait()
    a_y = c.same(qkv_all.at[t, core, :, :, qa], p.by_y)
    b_x = c.same(qkv_all.at[t, core, :, :, qb], p.by_x)
    e_x = c.same(ext_all.at[t, core], p.by_x)
    c.go([a_y, b_x, e_x])
    line_down.send(1)
    line_out.send(1)
    own = [c.same(qkv_all.at[t, core], p.sibling), c.same(ext_all.at[t, core], p.sibling)]
    c.go(own)
    c.arrive([e_x])
    e_y = [c.same(ext_all.at[k, core], p.by_y) for k in (t, p.t_x)]
    c.go(e_y)
    c.arrive([a_y])
    a_x = [c.same(qkv_all.at[k, core, :, :, qa], p.by_x) for k in (t, p.t_y)]
    c.go(a_x)
    c.arrive([b_x])
    b_y = [c.same(qkv_all.at[k, core, :, :, qb], p.by_y) for k in (t, p.t_x)]
    c.go(b_y)
    near = [
        c.same(qkv_all.at[p.t_y, core, :, :, qa], p.sibling),
        c.same(qkv_all.at[p.t_x, core, :, :, qb], p.sibling),
        c.same(ext_all.at[p.t_x, core], p.sibling),
    ]
    c.go(near)
    c.arrive(e_y)
    far = [c.same(ext_all.at[k, core], p.sibling) for k in (p.t_y, p.t_d)]
    c.go(far)
    for step in range(1, n):
        for line in (line_down, line_out):
            line.take(step)
            if step < n - 1:
                line.send(step + 1)
        handed += line_down.hand_over(step)
        if step == max(n - 2, 1):
            c.arrive(a_x)
            c.arrive(b_y)
            last = [c.same(qkv_all.at[k, core, :, :, qa], p.sibling) for k in (p.t_x, p.t_d)]
            last += [c.same(qkv_all.at[k, core, :, :, qb], p.sibling) for k in (p.t_y, p.t_d)]
            c.go(last)
    c.arrive(trade + own + near + far + last)
    for moves, when in handed:
        c.arrive(moves, when)
    c.end()


def gather_first(qkv, out, gateup, down, ext, planes, n):
    any_spec = pl.BlockSpec(memory_space=pl.ANY)
    rows = qkv.shape[0]
    part = gateup.shape[1] // planes
    low = jnp.bfloat16
    copies = 72
    cut = first_columns(part // 2)
    return pl.pallas_call(
        functools.partial(gather_kernel, n),
        out_shape=(
            jax.ShapeDtypeStruct((planes, 2, n, rows, qkv.shape[1]), low),
            jax.ShapeDtypeStruct((planes, 2, n, rows, out.shape[1]), low),
            jax.ShapeDtypeStruct((planes, 2, n) + ext.shape, low),
            jax.ShapeDtypeStruct((planes, rows, cut), low),
            jax.ShapeDtypeStruct((planes, rows, part - cut), low),
            jax.ShapeDtypeStruct((2, n) + down.shape, low),
        ),
        in_specs=[pl.BlockSpec(memory_space=pltpu.VMEM)] * 5,
        out_specs=(any_spec,) * 6,
        scratch_shapes=[
            pltpu.VMEM(qkv.shape, low),
            pltpu.VMEM(out.shape, low),
            pltpu.VMEM((planes, rows, part), low),
            pltpu.VMEM(down.shape, low),
            pltpu.SemaphoreType.DMA((copies,)),
            pltpu.SemaphoreType.DMA((copies,)),
            pltpu.SemaphoreType.DMA((8,)),
        ],
        compiler_params=pltpu.CompilerParams(
            collective_id=0, has_side_effects=True, vmem_limit_bytes=32 * 1024 * 1024
        ),
        name="gather_first",
    )(qkv, out, gateup, down, ext)


class PlaneScatter:
    def __init__(self, place, copies, left, right, parts, turned, leaving, came, total, first, second):
        self.p, self.c, self.left, self.right, self.parts = place, copies, left, right, parts
        self.turned, self.leaving, self.came, self.total = turned, leaving, came, total
        self.first, self.second = first, second
        self.moves = {}

    def turn(self):
        rows = self.turned.shape[1]

        def one(k, carry):
            self.turned[k] = self.left[:, pl.ds(pl.multiple_of(k * rows, rows), rows)].T
            return carry

        lax.fori_loop(0, self.turned.shape[0], one, 0)

    def at(self, part):
        low, high, _ = self.parts[part]
        return slice(low, high)

    def begin(self, part):
        p, cols = self.p, self.at(part)
        right = self.right[:, cols]

        def terms(into, core):
            def one(t, carry):
                term = jnp.dot(self.turned[t * 2 + core], right, preferred_element_type=jnp.float32)
                into[t, :, cols] = term.astype(jnp.bfloat16)
                return carry

            lax.fori_loop(0, into.shape[0], one, 0)

        terms(self.leaving, 1 - p.core)
        self.moves[part, 0] = [self.c.make(self.leaving.at[:, :, cols], self.came.at[:, :, cols], p.sibling)]
        self.c.go(self.moves[part, 0])
        terms(self.total, p.core)

    def add(self, t, cols, came):
        both = self.total[t, :, cols].astype(jnp.float32) + came.astype(jnp.float32)
        self.total[t, :, cols] = both.astype(jnp.bfloat16)

    def across_first(self, part):
        p, c, cols = self.p, self.c, self.at(part)
        c.arrive(self.moves[part, 0])

        def one(t, carry):
            self.add(t, cols, self.came[t, :, cols])
            return carry

        lax.fori_loop(0, self.total.shape[0], one, 0)
        near, to = (p.t_x, p.by_x) if self.parts[part][2] else (p.t_y, p.by_y)
        self.moves[part, 1] = [
            c.make(self.total.at[t, :, cols], self.first.at[k, :, cols], to) for k, t in enumerate((near, p.t_d))
        ]
        c.go(self.moves[part, 1])

    def across_second(self, part):
        p, c, cols = self.p, self.c, self.at(part)
        c.arrive(self.moves[part, 1])
        near, to = (p.t_y, p.by_y) if self.parts[part][2] else (p.t_x, p.by_x)
        self.add(near, cols, self.first[1, :, cols])
        self.moves[part, 2] = [c.make(self.total.at[near, :, cols], self.second.at[:, cols], to)]
        c.go(self.moves[part, 2])
        self.add(p.t, cols, self.first[0, :, cols])

    def end(self, part):
        cols = self.at(part)
        self.c.arrive(self.moves[part, 2])
        self.add(self.p.t, cols, self.second[:, cols])


class LineScatter:
    def __init__(self, place, copies, read, cols, up_leaving, up_came, down_leaving, down_came):
        self.p, self.c, self.read, self.cols = place, copies, read, cols
        self.ways = ((up_leaving, up_came, place.above), (down_leaving, down_came, place.below))
        self.rows = up_came.shape[1]
        self.moves = []

    def block(self, d):
        at = pl.ds(pl.multiple_of(jnp.clip(d, 0, self.p.n - 1) * self.rows, self.rows), self.rows)
        return self.read(at, self.cols).astype(jnp.float32)

    def step(self, s):
        p, c, n, cols = self.p, self.c, self.p.n, self.cols
        self.take()
        self.moves = []
        for way, (leaving, came, to) in enumerate(self.ways):
            behind = p.z if way == 0 else n - 1 - p.z
            block = n - s + p.z if way == 0 else p.z - (n - s)
            sends = (behind <= s - 1) & (behind < n - 1)

            @pl.when(sends & (behind == 0) if s > 1 else sends)
            def _():
                leaving[s - 1, :, cols] = self.block(block).astype(jnp.bfloat16)

            if s > 1:
                @pl.when(sends & (behind > 0))
                def _():
                    both = self.block(block) + came[s - 2, :, cols].astype(jnp.float32)
                    leaving[s - 1, :, cols] = both.astype(jnp.bfloat16)

            move = c.make(leaving.at[s - 1, :, cols], came.at[s - 1, :, cols], to)
            c.go([move], sends)
            self.moves.append((move, (behind >= 1) & (behind <= s)))

    def take(self):
        for move, when in self.moves:
            self.c.arrive([move], when)

    def end(self, out_ref):
        p, n, cols = self.p, self.p.n, self.cols
        self.take()
        up_came, down_came = self.ways[0][1], self.ways[1][1]
        own = self.block(p.z)

        @pl.when(p.z == 0)
        def _():
            out_ref[:, cols] = own + down_came[n - 2, :, cols].astype(jnp.float32)

        @pl.when(p.z == n - 1)
        def _():
            out_ref[:, cols] = own + up_came[n - 2, :, cols].astype(jnp.float32)

        @pl.when((p.z > 0) & (p.z < n - 1))
        def _():
            out_ref[:, cols] = own + (
                up_came[n - 2, :, cols].astype(jnp.float32) + down_came[n - 2, :, cols].astype(jnp.float32)
            )


def plane_parts(cols, count):
    edges = [cols // 128 * k // count * 128 for k in range(count + 1)]
    return [(low, high, k % 2 == 0) for k, (low, high) in enumerate(zip(edges[:-1], edges[1:]))]


def plane_scratch(rows, width, cols, planes):
    low = jnp.bfloat16
    line = width // planes // 2
    return [
        pltpu.VMEM((planes * 2, line, rows), low),
        pltpu.VMEM((planes, line, cols), low),
        pltpu.VMEM((planes, line, cols), low),
        pltpu.VMEM((planes, line, cols), low),
        pltpu.VMEM((2, line, cols), low),
        pltpu.VMEM((line, cols), low),
    ]


def qkv_back_kernel(
    n, parts, normed_ref, grad_ref, weights_hbm, pieces_ref, out_sum, sum_ref, back_ref, gateup_ref, out_ref, weights,
    traded, turned, leaving, came, total, first, second, up_leaving, up_came, down_leaving, down_came, out_up_leaving,
    out_up_came, out_down_leaving, out_down_came, send_sems, recv_sems, load_sem,
):
    p = Place(n)
    c = Copies(send_sems, recv_sems)
    held = weights.shape[0]

    def load(k):
        return pltpu.make_async_copy(weights_hbm.at[k * held : (k + 1) * held], weights, load_sem)

    load(0).start()
    p.greet([p.by_x, p.by_y, p.by_d, p.sibling])
    trade = [
        c.make(pieces_ref.at[k], traded.at[p.t], to) for k, to in ((p.t_x, p.by_x), (p.t_y, p.by_y), (p.t_d, p.by_d))
    ]
    c.go(trade)
    traded[p.t] = pieces_ref[p.t]
    out_line = LineScatter(
        p, c, lambda at, cols: out_sum[at, cols], slice(None), out_up_leaving, out_up_came, out_down_leaving, out_down_came
    )
    out_line.step(1)
    scatter = PlaneScatter(p, c, normed_ref, grad_ref, parts, turned, leaving, came, total, first, second)
    every = range(len(parts))
    scatter.turn()
    for k in every:
        scatter.begin(k)
    chunk = 2 * HEAD_DIM

    def back(half):
        load(half).wait()

        def one(k, carry):
            at = pl.ds(pl.multiple_of(k * chunk, chunk), chunk)
            to = pl.ds(pl.multiple_of(half * held + k * chunk, chunk), chunk)
            back_ref[:, to] = dot_nt(grad_ref[...], weights[at, :])
            return carry

        lax.fori_loop(0, held // chunk, one, 0)

    for k in every:
        scatter.across_first(k)
    if n > 2:
        out_line.step(2)
    back(0)
    load(1).start()
    c.arrive(trade)
    units = traded.shape[2] // 2
    for k in range(traded.shape[0]):
        for low, high in unit_groups(units):
            for at, start in ((2 * low, k * units), (low + high, gateup_ref.shape[1] // 2 + k * units)):
                columns = traded[k, :, at : at + high - low]
                gateup_ref[:, start + low : start + high] = columns.astype(jnp.float32)
    for s in range(3, n):
        out_line.step(s)
    for k in every:
        scatter.across_second(k)
    back(1)
    lines = [
        LineScatter(
            p, c, lambda at, cols: total[p.t, at, cols], scatter.at(k), up_leaving, up_came, down_leaving, down_came
        )
        for k in every
    ]
    for k in every:
        scatter.end(k)
        lines[k].step(1)
    for s in range(2, n):
        for line in lines:
            line.step(s)
    out_line.end(out_ref)
    for line in lines:
        line.end(sum_ref)
    c.end()


def qkv_back(normed, grad, weights, pieces, out_sum, planes, n, collective_id):
    rows, width = normed.shape
    cols = grad.shape[1]
    parts = plane_parts(cols, 4)
    in_vmem = pl.BlockSpec(memory_space=pltpu.VMEM)
    low = jnp.bfloat16
    line = pltpu.VMEM((n - 1, width // planes // 2 // n, cols), low)
    out_line = pltpu.VMEM((n - 1, out_sum.shape[0] // n, out_sum.shape[1]), low)
    copies = len(parts) * (4 + 2 * n) + 2 * n + 4
    return pl.pallas_call(
        functools.partial(qkv_back_kernel, n, parts),
        in_specs=[in_vmem, in_vmem, pl.BlockSpec(memory_space=pl.ANY), in_vmem, in_vmem],
        out_specs=(in_vmem,) * 4,
        out_shape=(
            jax.ShapeDtypeStruct((width // planes // 2 // n, cols), jnp.float32),
            jax.ShapeDtypeStruct((rows, width), jnp.float32),
            jax.ShapeDtypeStruct((pieces.shape[1], planes * pieces.shape[2]), jnp.float32),
            jax.ShapeDtypeStruct((out_sum.shape[0] // n, out_sum.shape[1]), jnp.float32),
        ),
        scratch_shapes=[pltpu.VMEM((weights.shape[0] // 2, cols), low), pltpu.VMEM(pieces.shape, low)]
        + plane_scratch(rows, width, cols, planes)
        + [line] * 4
        + [out_line] * 4
        + [pltpu.SemaphoreType.DMA((copies,)), pltpu.SemaphoreType.DMA((copies,)), pltpu.SemaphoreType.DMA],
        compiler_params=pltpu.CompilerParams(
            vmem_limit_bytes=60 * 1024 * 1024, collective_id=collective_id, has_side_effects=True
        ),
        cost_estimate=pl.CostEstimate(
            flops=48 * rows * width * cols, bytes_accessed=2 * weights.size + 8 * rows * width, transcendentals=0
        ),
        name="qkv_back",
    )(normed, grad, weights, pieces, out_sum)


class TokenScatter:
    def __init__(self, place, copies, blocks, near, corner_x, corner_y, came_x, came_y, load_sem):
        self.p, self.c, self.blocks, self.near = place, copies, blocks, near
        self.corner_x, self.corner_y, self.came_x, self.came_y = corner_x, corner_y, came_x, came_y
        self.cap = near.shape[0] // 2
        self.keep = pltpu.make_async_copy(blocks[1], near, load_sem)

    def begin(self):
        p, c, half = self.p, self.c, self.cap // 2
        self.keep.start()
        self.far = [
            c.make(self.blocks[2].at[:half], self.corner_x, p.by_x), c.make(self.blocks[2].at[half:], self.corner_y, p.by_y)
        ]
        c.go(self.far)

    def middle(self):
        p, c, near, cap = self.p, self.c, self.near, self.cap
        self.keep.wait()
        c.arrive(self.far)
        for at, came in ((slice(cap // 2, cap), self.corner_y), (slice(cap, cap + cap // 2), self.corner_x)):
            near[at, :] = (near[at, :].astype(jnp.float32) + came[...].astype(jnp.float32)).astype(jnp.bfloat16)
        self.close = [c.make(near.at[:cap], self.came_x, p.by_x), c.make(near.at[cap:], self.came_y, p.by_y)]
        c.go(self.close)

    def end(self):
        self.c.arrive(self.close)


def mid_back_kernel(
    n, cap, units, *refs,
):
    back, rows_in, gateup_in, hidden_in, grads_in = (refs[k : k + 3] for k in range(0, 15, 3))
    sum_ref, down_ref, gateup_ref = refs[15:18]
    (
        wide_now, both_now, turned, own, near, corner_x, corner_y, came_x, came_y, down_leaving, down_came,
        gateup_leaving, gateup_came, send_sems, recv_sems, load_sems,
    ) = refs[18:]
    p = Place(n)
    c = Copies(send_sems, recv_sems)
    low = jnp.bfloat16
    loaded = [0]

    def load(parts, into, cols=None):
        moves = []
        for at, part in zip((slice(0, cap), slice(cap, 3 * cap), slice(3 * cap, 4 * cap)), parts):
            to = into.at[at] if cols is None else into.at[at, cols]
            moves.append(pltpu.make_async_copy(part, to, load_sems.at[loaded[0]]))
            loaded[0] += 1
            moves[-1].start()
        return moves

    def wait(moves):
        for m in moves:
            m.wait()

    first = load(grads_in, wide_now) + load(hidden_in, both_now, slice(0, units))
    keep = pltpu.make_async_copy(back[0], own, load_sems.at[14])
    keep.start()
    tokens = TokenScatter(p, c, back, near, corner_x, corner_y, came_x, came_y, load_sems.at[15])
    p.greet([p.by_x, p.by_y, p.sibling])
    tokens.begin()

    wait(first)

    def turn(k, carry):
        at = pl.ds(pl.multiple_of(k * LANES, LANES), LANES)
        turned[at, :] = both_now[:, at].T
        return carry

    lax.fori_loop(0, units // LANES, turn, 0)
    part = units // 2
    width = wide_now.shape[1]

    def down_half(core, put):
        def one(k, carry):
            at = pl.ds(pl.multiple_of(k * WIDTH_GROUP, WIDTH_GROUP), WIDTH_GROUP)
            left = turned[pl.ds(pl.multiple_of(core * part, 16), part), :]
            put(at, jnp.dot(left, wide_now[:, at], preferred_element_type=jnp.float32))
            return carry

        lax.fori_loop(0, width // WIDTH_GROUP, one, 0)

    def put_leaving(at, term):
        down_leaving[:, at] = term.astype(low)

    def put_down(at, term):
        down_ref[:, at] = (term + down_came[:, at].astype(jnp.float32)).astype(low)

    down_half(1 - p.core, put_leaving)
    down_move = [c.make(down_leaving, down_came, p.sibling)]
    c.go(down_move)
    tokens.middle()
    c.arrive(down_move)
    down_half(p.core, put_down)

    second = load(rows_in, wide_now) + load(gateup_in, both_now)
    wait(second)
    line = gateup_ref.shape[1]
    cols = 2 * units

    def gateup_part(k, put):
        left = wide_now[:, pl.ds(pl.multiple_of(k * line, line), line)].T

        def one(j, carry):
            at = pl.ds(pl.multiple_of(j * WIDTH_GROUP, WIDTH_GROUP), WIDTH_GROUP)
            put(at, jnp.dot(left, both_now[:, at], preferred_element_type=jnp.float32))
            return carry

        lax.fori_loop(0, cols // WIDTH_GROUP, one, 0)

    moves = []
    planes = gateup_ref.shape[0]
    for t in range(planes):
        slot = t % 2
        if t >= 2:
            moves[t - 2].wait_send()

        def put_slot(at, term, slot=slot):
            gateup_leaving[slot, :, at] = term.astype(low)

        gateup_part(t * 2 + 1 - p.core, put_slot)
        moves.append(c.make(gateup_leaving.at[slot], gateup_came.at[t], p.sibling))
        moves[-1].start()
    for t in range(planes):
        moves[t].wait_recv()

        def put_sum(at, term, t=t):
            gateup_ref[t, :, at] = (term + gateup_came[t, :, at].astype(jnp.float32)).astype(low)

        gateup_part(t * 2 + p.core, put_sum)
    for t in range(max(planes - 2, 0), planes):
        moves[t].wait_send()
    tokens.end()
    keep.wait()
    sum_ref[...] = own[...].astype(jnp.float32) + (
        came_x[...].astype(jnp.float32) + came_y[...].astype(jnp.float32)
    )
    c.end()


def mid_back(back, rows, gateup_grads, hidden, grads, cap, planes, n, collective_id):
    width = rows[0].shape[1]
    units = hidden[0].shape[1]
    line = width // planes // 2
    low = jnp.bfloat16
    any_spec = pl.BlockSpec(memory_space=pl.ANY)
    in_vmem = pl.BlockSpec(memory_space=pltpu.VMEM)
    vmem = lambda *shape: pltpu.VMEM(shape, low)
    return pl.pallas_call(
        functools.partial(mid_back_kernel, n, cap, units),
        in_specs=[any_spec] * 15,
        out_specs=(in_vmem,) * 3,
        out_shape=(
            jax.ShapeDtypeStruct((cap, width), jnp.float32),
            jax.ShapeDtypeStruct((units // 2, width), low),
            jax.ShapeDtypeStruct((planes, line, 2 * units), low),
        ),
        scratch_shapes=[
            vmem(4 * cap, width),
            vmem(4 * cap, 2 * units),
            vmem(units, 4 * cap),
            vmem(cap, width),
            vmem(2 * cap, width),
            vmem(cap // 2, width),
            vmem(cap // 2, width),
            vmem(cap, width),
            vmem(cap, width),
            vmem(units // 2, width),
            vmem(units // 2, width),
            vmem(2, line, 2 * units),
            vmem(planes, line, 2 * units),
            pltpu.SemaphoreType.DMA((12,)),
            pltpu.SemaphoreType.DMA((12,)),
            pltpu.SemaphoreType.DMA((16,)),
        ],
        compiler_params=pltpu.CompilerParams(
            vmem_limit_bytes=61 * 1024 * 1024, collective_id=collective_id, has_side_effects=True
        ),
        cost_estimate=pl.CostEstimate(
            flops=48 * cap * width * units, bytes_accessed=32 * cap * (width + units), transcendentals=0
        ),
        name="mid_back",
    )(*back, *rows, *gateup_grads, *hidden, *grads)


def fill_bias(r, key_code, query_code, query_base, bias):
    rows = bias.shape[0]
    code = key_code[r * rows : (r + 1) * rows, :]
    seen = (code <= query_code[...]) & (code >= query_base[...])
    bias[...] = jnp.where(seen, 0.0, MASKED)


class PlaneGather:
    def __init__(self, place, copies, whole):
        self.p, self.c, self.whole = place, copies, whole
        cols = whole.shape[-1]
        self.a, self.b = slice(0, cols // 2), slice(cols // 2, cols)

    def block(self, t, cols=slice(None)):
        return self.whole.at[t, self.p.core, :, :, cols]

    def begin(self):
        p, c = self.p, self.c
        self.a_y, self.b_x = c.same(self.block(p.t, self.a), p.by_y), c.same(self.block(p.t, self.b), p.by_x)
        self.over = [c.same(self.block(p.t), p.sibling)]
        c.go([self.a_y, self.b_x] + self.over)

    def middle(self):
        p, c = self.p, self.c
        c.arrive([self.a_y, self.b_x])
        self.a_x = [c.same(self.block(k, self.a), p.by_x) for k in (p.t, p.t_y)]
        self.b_y = [c.same(self.block(k, self.b), p.by_y) for k in (p.t, p.t_x)]
        near = [c.same(self.block(p.t_y, self.a), p.sibling), c.same(self.block(p.t_x, self.b), p.sibling)]
        c.go(self.a_x + self.b_y + near)
        self.over += near

    def end(self):
        p, c = self.p, self.c
        c.arrive(self.a_x + self.b_y)
        far = [c.same(self.block(k, self.a), p.sibling) for k in (p.t_x, p.t_d)]
        far += [c.same(self.block(k, self.b), p.sibling) for k in (p.t_y, p.t_d)]
        c.go(far)
        c.arrive(self.over + far)


def attend_kernel(n, with_out, *refs):
    inputs_ref, gain_ref, cosine, sine, weights_hbm, key_code, query_code, query_base = refs[:8]
    refs = refs[8:]
    if with_out:
        (own_grad, _), refs = refs[:2], refs[2:]
    (normed_ref, inverse_ref, q_ref, o_ref, total_ref, kv_all), refs = refs[:6], refs[6:]
    if with_out:
        (out_all, grad_x, grad_y, grad_d), refs = refs[:4], refs[4:]
    weights, peak_now, total_now, mixed_now, bias, send_sems, recv_sems, load_sems = refs
    p = Place(n)
    c = Copies(send_sems, recv_sems)
    z = p.z
    rows, width = q_ref.shape
    values_at = KV_HEADS * HEAD_DIM
    pair = 2 * HEAD_DIM
    slot = lambda r: kv_all.at[r * rows : (r + 1) * rows, :]
    loads = [
        pltpu.make_async_copy(weights_hbm.at[:, cols], weights.at[:, cols], load_sems.at[k])
        for k, cols in enumerate((slice(width, weights.shape[1]), slice(0, width)))
    ]
    for load in loads:
        load.start()
    p.greet([p.by_x, p.by_y, p.sibling] if with_out else [])
    if with_out:
        half = rows // 2
        near = [c.make(own_grad, grad_x, p.by_x), c.make(own_grad, grad_y, p.by_y)]
        out_plane = PlaneGather(p, c, out_all)
        out_plane.begin()
        c.go(near)
    inputs = inputs_ref[...]
    inverse = lax.rsqrt(jnp.mean(inputs * inputs, axis=1, keepdims=True) + EPSILON)
    inverse_ref[...] = inverse
    normed_ref[...] = (inputs * inverse * gain_ref[...]).astype(jnp.bfloat16)

    def project(low, into, to, turned):
        at = pl.ds(pl.multiple_of(low, pair), pair)
        both = jnp.dot(normed_ref[...], weights[:, at], preferred_element_type=jnp.float32)
        for k in range(2):
            head = both[:, k * HEAD_DIM : (k + 1) * HEAD_DIM]
            if turned:
                head = head * cosine[...] + pltpu.roll(head, HEAD_DIM // 2, 1) * sine[...]
            lanes = pl.ds(pl.multiple_of(to + k * HEAD_DIM, HEAD_DIM), HEAD_DIM)
            into[:rows, lanes] = head.astype(jnp.bfloat16)

    def project_all(start, count, into, to, turned):
        def one(k, carry):
            project(start + k * pair, into, to + k * pair, turned)
            return carry

        lax.fori_loop(0, count // pair, one, 0)

    loads[0].wait()
    project_all(width, values_at, kv_all, 0, True)
    project_all(width + values_at, values_at, kv_all, values_at, False)
    copies = [c.make(slot(r), slot(r + 1), p.above) for r in range(n - 1)]
    if copies:
        c.go([copies[0]], z < n - 1)
    for r in range(1, n):
        @pl.when(z < r)
        def _(r=r):
            kv_all[r * rows : (r + 1) * rows, :] = jnp.zeros((rows, kv_all.shape[1]), kv_all.dtype)

    loads[1].wait()
    project_all(0, width, q_ref, 0, True)

    def block(r):
        fill_bias(r, key_code, query_code, query_base, bias)
        at = slice(r * rows, (r + 1) * rows)

        def group(g, carry):
            keys = kv_all[at, pl.ds(pl.multiple_of(g * HEAD_DIM, HEAD_DIM), HEAD_DIM)]
            values = kv_all[at, pl.ds(pl.multiple_of(values_at + g * HEAD_DIM, HEAD_DIM), HEAD_DIM)]
            hidden = bias[...]
            for h in range(GROUP):
                lanes = pl.ds(pl.multiple_of((g * GROUP + h) * HEAD_DIM, HEAD_DIM), HEAD_DIM)
                scores = dot_nt(keys, q_ref[:, lanes]) * (SCORE_SCALE * LOG2_E) + hidden
                peak = jnp.max(scores, axis=0, keepdims=True)
                if r:
                    before = peak_now[g, h : h + 1, :]
                    peak = jnp.maximum(peak, before)
                weights = jnp.exp2(scores - peak)
                total = jnp.sum(weights, axis=0, keepdims=True)
                mixed = dot_tn(values, weights.astype(jnp.bfloat16))
                if r:
                    shrink = jnp.exp2(before - peak)
                    total = total + total_now[g, h : h + 1, :] * shrink
                    mixed = mixed + mixed_now[g, h] * shrink
                peak_now[g, h : h + 1, :] = peak
                total_now[g, h : h + 1, :] = total
                mixed_now[g, h] = mixed
            return carry

        lax.fori_loop(0, KV_HEADS, group, 0)

    block(0)
    for r in range(1, n):
        c.arrive([copies[r - 1]], z >= r)
        if r < n - 1:
            c.go([copies[r]], (z >= r) & (z < n - 1))
        if with_out and r == 1:
            out_plane.middle()
        if with_out and r == max(n - 2, 1):
            c.arrive(near)
            corners = [
                c.make(grad_y.at[:half], grad_d.at[:half], p.by_x),
                c.make(grad_x.at[half:], grad_d.at[half:], p.by_y),
            ]
            c.go(corners)
        if with_out and r == n - 1:
            out_plane.end()

        @pl.when(z >= r)
        def _(r=r):
            block(r)

    def finish(g, carry):
        for h in range(GROUP):
            lanes = pl.ds(pl.multiple_of((g * GROUP + h) * HEAD_DIM, HEAD_DIM), HEAD_DIM)
            total = total_now[g, h : h + 1, :]
            o_ref[:, lanes] = (mixed_now[g, h] / total).T.astype(jnp.bfloat16)
            total_ref[g, h : h + 1, :] = peak_now[g, h : h + 1, :] + jnp.log2(total)
        return carry

    lax.fori_loop(0, KV_HEADS, finish, 0)
    if with_out:
        c.arrive(corners)
    c.end()


def attend(
    inputs, gain, cosine, sine, weights, key_code, query_code, query_base, n, collective_id, down_grad=None, out_all=None
):
    rows, width = inputs.shape
    kv_cols = weights.shape[1] - width
    low = jnp.bfloat16
    in_vmem = pl.BlockSpec(memory_space=pltpu.VMEM)
    any_spec = pl.BlockSpec(memory_space=pl.ANY)
    given = [] if out_all is None else [down_grad, out_all]
    more = [] if out_all is None else [out_all] + [down_grad] * 3
    copies = n + 24
    return pl.pallas_call(
        functools.partial(attend_kernel, n, out_all is not None),
        in_specs=[in_vmem] * 4 + [any_spec] + [in_vmem] * 3 + [any_spec] * len(given),
        out_specs=(in_vmem,) * 6 + (any_spec,) * len(more),
        input_output_aliases={9: 6} if given else {},
        out_shape=(
            jax.ShapeDtypeStruct((rows, width), low),
            jax.ShapeDtypeStruct((rows, 1), jnp.float32),
            jax.ShapeDtypeStruct((rows, width), low),
            jax.ShapeDtypeStruct((rows, width), low),
            jax.ShapeDtypeStruct((KV_HEADS, GROUP, rows), jnp.float32),
            jax.ShapeDtypeStruct((n * rows, kv_cols), low),
        )
        + tuple(jax.ShapeDtypeStruct(o.shape, o.dtype) for o in more),
        scratch_shapes=[
            pltpu.VMEM(weights.shape, low),
            pltpu.VMEM((KV_HEADS, GROUP, rows), jnp.float32),
            pltpu.VMEM((KV_HEADS, GROUP, rows), jnp.float32),
            pltpu.VMEM((KV_HEADS, GROUP, HEAD_DIM, rows), jnp.float32),
            pltpu.VMEM((rows, rows), jnp.float32),
            pltpu.SemaphoreType.DMA((copies,)),
            pltpu.SemaphoreType.DMA((copies,)),
            pltpu.SemaphoreType.DMA((2,)),
        ],
        compiler_params=pltpu.CompilerParams(
            vmem_limit_bytes=52 * 1024 * 1024, collective_id=collective_id, has_side_effects=True
        ),
        cost_estimate=pl.CostEstimate(
            flops=64 * rows * n * rows * width, bytes_accessed=8 * rows * width, transcendentals=HEADS * rows * n * rows
        ),
        name="attend",
    )(inputs, gain, cosine, sine, weights, key_code, query_code, query_base, *given)


def attend_back_kernel(n, parts, *refs):
    q_ref, kv_all, do_ref, total_ref, mixed_ref, key_code, query_code, query_base, cosine, sine = refs[:10]
    refs = refs[10:]
    if parts:
        branch_ref, down_terms, refs = refs[0], refs[1:4], refs[4:]
    grad_ref, refs = refs[0], refs[1:]
    if parts:
        (out_sum, came_x, came_y), refs = refs[:3], refs[3:]
    dq_now, dkv_now, bias, inner_now, leaving, came, send_sems, recv_sems = refs[:8]
    p = Place(n)
    c = Copies(send_sems, recv_sems)
    z = p.z
    rows = q_ref.shape[0]
    values_at = KV_HEADS * HEAD_DIM
    p.greet([p.by_x, p.by_y, p.sibling] if parts else [])
    every = range(len(parts))
    if parts:
        scatter = PlaneScatter(p, c, mixed_ref, branch_ref, parts, *refs[8:14])
        tokens = TokenScatter(p, c, down_terms, *refs[14:17], came_x, came_y, refs[17])
        tokens.begin()
    copies = {r: c.make(leaving.at[r - 1], came.at[r - 1], p.below) for r in range(1, n)}
    dq_now[...] = jnp.zeros_like(dq_now)
    q_cols = HEADS * HEAD_DIM

    def turned_back(head):
        return head * cosine[...] - pltpu.roll(head, HEAD_DIM // 2, 1) * sine[...]

    def put(low, head):
        grad_ref[:, low : low + HEAD_DIM] = head.astype(jnp.bfloat16)

    def block(r):
        fill_bias(r, key_code, query_code, query_base, bias)
        at = slice(r * rows, (r + 1) * rows)

        def group(g, carry):
            key_lanes = pl.ds(pl.multiple_of(g * HEAD_DIM, HEAD_DIM), HEAD_DIM)
            value_lanes = pl.ds(pl.multiple_of(values_at + g * HEAD_DIM, HEAD_DIM), HEAD_DIM)
            keys, values, hidden = kv_all[at, key_lanes], kv_all[at, value_lanes], bias[...]
            dk = dv = None
            for h in range(GROUP):
                lanes = pl.ds(pl.multiple_of((g * GROUP + h) * HEAD_DIM, HEAD_DIM), HEAD_DIM)
                query, grad = q_ref[:, lanes], do_ref[:, lanes]
                scores = dot_nt(keys, query) * (SCORE_SCALE * LOG2_E) + hidden
                weights = jnp.exp2(scores - total_ref[g, h : h + 1, :])
                grad_weights = dot_nt(values, grad)
                grad_scores = (weights * (grad_weights - inner_now[g, h : h + 1, :])).astype(jnp.bfloat16)
                dv_term = jnp.dot(weights.astype(jnp.bfloat16), grad, preferred_element_type=jnp.float32)
                dk_term = jnp.dot(grad_scores, query, preferred_element_type=jnp.float32)
                dv = dv_term if dv is None else dv + dv_term
                dk = dk_term if dk is None else dk + dk_term
                dq_now[g, h] += dot_tn(keys, grad_scores)
            dkv_now[:, key_lanes] = dk * SCORE_SCALE
            dkv_now[:, value_lanes] = dv
            return carry

        lax.fori_loop(0, KV_HEADS, group, 0)

    def inner_of(g, carry):
        for h in range(GROUP):
            lanes = pl.ds(pl.multiple_of((g * GROUP + h) * HEAD_DIM, HEAD_DIM), HEAD_DIM)
            both = do_ref[:, lanes].astype(jnp.float32) * mixed_ref[:, lanes].astype(jnp.float32)
            inner_now[g, h : h + 1, :] = jnp.sum(both.T, axis=0, keepdims=True)
        return carry

    lax.fori_loop(0, KV_HEADS, inner_of, 0)
    for r in range(n - 1, -1, -1):
        @pl.when(z >= r)
        def _(r=r):
            block(r)
            if r < n - 1:
                @pl.when(z < n - 1)
                def _():
                    copies[r + 1].wait_recv()
                    dkv_now[...] += came[r].astype(jnp.float32)
            if r:
                leaving[r - 1] = dkv_now[...].astype(jnp.bfloat16)
                copies[r].start()
            else:
                for g in range(KV_HEADS):
                    put(q_cols + g * HEAD_DIM, turned_back(dkv_now[:, g * HEAD_DIM : (g + 1) * HEAD_DIM]))
                grad_ref[:, q_cols + values_at :] = dkv_now[:, values_at:].astype(jnp.bfloat16)

        if parts and r == n - 1:
            scatter.turn()
            for k in every:
                scatter.begin(k)
        if parts and r == max(n - 2, 0):
            tokens.middle()
            for k in every:
                scatter.across_first(k)
        if parts and r == max(n - 3, 0):
            for k in every:
                scatter.across_second(k)
    if parts:
        for k in every:
            scatter.end(k)
        out_sum[...] = scatter.total[p.t]
        tokens.end()

    def finish(g, carry):
        for h in range(GROUP):
            lanes = pl.ds(pl.multiple_of((g * GROUP + h) * HEAD_DIM, HEAD_DIM), HEAD_DIM)
            grad_ref[:, lanes] = turned_back(dq_now[g, h].T * SCORE_SCALE).astype(jnp.bfloat16)
        return carry

    lax.fori_loop(0, KV_HEADS, finish, 0)
    for r in range(1, n):
        @pl.when(z >= r)
        def _(r=r):
            copies[r].wait_send()
    c.end()


def attend_back(
    query, kv_all, grad, total, mixed, key_code, query_code, query_base, cosine, sine, n, collective_id, branch_grad=None,
    down_terms=(), planes=0,
):
    rows, width = query.shape
    kv_cols = kv_all.shape[1]
    in_vmem = pl.BlockSpec(memory_space=pltpu.VMEM)
    slots = max(n - 1, 1)
    more, parts, shapes, scratch = (), [], (), []
    if branch_grad is not None:
        more, parts = (branch_grad, *down_terms), plane_parts(width, 2)
        came = jax.ShapeDtypeStruct((rows, width), jnp.bfloat16)
        shapes = (jax.ShapeDtypeStruct((width // planes // 2, width), jnp.bfloat16), came, came)
        scratch = plane_scratch(rows, width, width, planes)
        scratch += [pltpu.VMEM((count, width), jnp.bfloat16) for count in (2 * rows, rows // 2, rows // 2)]
        scratch.append(pltpu.SemaphoreType.DMA)
    copies = n + 4 * len(parts) + 4
    any_spec = pl.BlockSpec(memory_space=pl.ANY)
    return pl.pallas_call(
        functools.partial(attend_back_kernel, n, parts),
        in_specs=[in_vmem] * (10 + len(more[:1])) + [any_spec] * len(more[1:]),
        out_specs=(in_vmem,) * (1 + len(shapes[:1])) + (any_spec,) * len(shapes[1:]),
        out_shape=(jax.ShapeDtypeStruct((rows, width + kv_cols), jnp.bfloat16),) + shapes,
        scratch_shapes=[
            pltpu.VMEM((KV_HEADS, GROUP, HEAD_DIM, rows), jnp.float32),
            pltpu.VMEM((rows, kv_cols), jnp.float32),
            pltpu.VMEM((rows, rows), jnp.float32),
            pltpu.VMEM((KV_HEADS, GROUP, rows), jnp.float32),
            pltpu.VMEM((slots, rows, kv_cols), jnp.bfloat16),
            pltpu.VMEM((slots, rows, kv_cols), jnp.bfloat16),
            pltpu.SemaphoreType.DMA((copies,)),
            pltpu.SemaphoreType.DMA((copies,)),
        ]
        + scratch,
        compiler_params=pltpu.CompilerParams(
            vmem_limit_bytes=60 * 1024 * 1024, collective_id=collective_id, has_side_effects=True
        ),
        cost_estimate=pl.CostEstimate(
            flops=72 * rows * n * rows * width, bytes_accessed=16 * rows * width, transcendentals=HEADS * rows * n * rows
        ),
        name="attend_back",
    )(query, kv_all, grad, total, mixed, key_code, query_code, query_base, cosine, sine, *more)


def rotary_tables(positions):
    half_dim = HEAD_DIM // 2
    frequency = jnp.power(10000.0, -2.0 * jnp.arange(half_dim, dtype=jnp.float32) / HEAD_DIM)
    angles = positions[:, None] * frequency[None, :]
    return (jnp.cos(angles), jnp.sin(angles))


def norm_forward(values_in, gain_row):
    inverse = lax.rsqrt(jnp.mean(values_in * values_in, axis=-1, keepdims=True) + EPSILON)
    return (values_in * inverse * gain_row, inverse)


def norm_backward(values_in, inverse, gain_row, incoming):
    scaled_grad = incoming * gain_row
    return inverse * scaled_grad - values_in * inverse * inverse * inverse * jnp.mean(
        scaled_grad * values_in, axis=-1, keepdims=True
    )


def advance_state(weight, moment, average, gradient):
    moment_next = MOMENTUM * moment + gradient
    weight_next = weight - STEP_RATE * (gradient + MOMENTUM * moment_next)
    average_next = AVERAGING * average + (1.0 - AVERAGING) * weight_next
    return (weight_next, moment_next, average_next)


class Links:
    def __init__(self):
        self.wide = lax.axis_size("wide")
        self.n = lax.axis_size("narrow")
        self.planes = self.wide // 2
        self.wide_at = lax.axis_index("wide")
        self.z_at = lax.axis_index("narrow")
        self.t_at = self.wide_at // 2
        self.core_at = self.wide_at % 2
        self.bits = [1 << k for k in range(self.planes.bit_length() - 1)]
        per_chip = 2 * self.n
        self.same_chip = [[t * per_chip + j for j in range(per_chip)] for t in range(self.planes)]
        self.same_plane = [
            [t * per_chip + j for t in range(self.planes)] for j in range(per_chip)
        ]

    def swap(self, values, flip):
        pairs = [(i, i ^ (flip * self.n)) for i in range(self.wide * self.n)]
        return lax.ppermute(values, MESH_AXES, pairs)

    def column_cuts(self, cols):
        lanes = cols // 128
        count = len(self.bits)
        edges = [128 * (lanes * k // count) for k in range(count + 1)]
        orders = [self.bits[k:] + self.bits[:k] for k in range(count)]
        return list(zip(edges[:-1], edges[1:], orders))

    def scatter_core(self, term):
        mine = lax.dynamic_index_in_dim(term, self.core_at, 1, keepdims=False)
        other = lax.dynamic_index_in_dim(term, 1 - self.core_at, 1, keepdims=False)
        got = self.swap(other, 1)
        return (mine.astype(jnp.float32) + got.astype(jnp.float32)).astype(jnp.bfloat16)

    def scatter_rows(self, term):
        rows, cols = term.shape
        term = term.reshape(self.planes, 2, rows // self.wide, cols)
        term = self.scatter_core(term)
        parts = []
        for low, high, order in self.column_cuts(cols):
            part = term[:, :, low:high]
            left = sorted(self.bits, reverse=True)
            part = part.reshape((2,) * len(left) + part.shape[1:])
            for bit in order:
                axis = left.index(bit)
                my_bit = (self.t_at // bit) % 2
                mine = lax.dynamic_index_in_dim(part, my_bit, axis, keepdims=False)
                other = lax.dynamic_index_in_dim(part, 1 - my_bit, axis, keepdims=False)
                got = self.swap(other, 2 * bit)
                part = (mine.astype(jnp.float32) + got.astype(jnp.float32)).astype(jnp.bfloat16)
                left.remove(bit)
            parts.append(part)
        total = jnp.concatenate(parts, axis=1)
        return lax.psum_scatter(total, "narrow", scatter_dimension=0, tiled=True)

    def gather_tokens(self, rows):
        if self.planes != 4:
            every = lax.all_gather(
                rows, MESH_AXES, axis=0, tiled=False, axis_index_groups=self.same_plane
            )
            return [every[k] for k in range(self.planes)]
        half = rows.shape[0] // 2
        by_x = self.swap(rows, 2)
        by_y = self.swap(rows, 4)
        corner = [self.swap(by_y[:half], 2), self.swap(by_x[half:], 4)]
        return [rows, by_x, by_y, jnp.concatenate(corner)]

    def scatter_tokens(self, parts, cap):
        every = jnp.concatenate(parts)
        if self.planes != 4:
            total = lax.psum_scatter(
                every, MESH_AXES, scatter_dimension=0, tiled=True, axis_index_groups=self.same_plane
            )
            return total.astype(jnp.float32)
        total = every[:cap].astype(jnp.float32)
        for k in range(1, 4):
            total += self.swap(every[k * cap : (k + 1) * cap], 2 * k).astype(jnp.float32)
        return total

    def gather_chip(self, pieces):
        every = lax.all_gather(pieces, MESH_AXES, axis=1, tiled=True, axis_index_groups=self.same_chip)
        return every.reshape(-1, every.shape[-1])

    def plane_counts(self, counts, cap):
        if self.planes != 4:
            return jnp.full((self.planes,), cap, jnp.int32)
        at = [((self.t_at ^ d) * 2 + self.core_at) * self.n + self.z_at for d in range(4)]
        return counts[jnp.stack(at)]

    def trade_columns(self, pieces):
        came = jnp.zeros_like(pieces)
        for d in range(self.planes):
            piece = lax.dynamic_index_in_dim(pieces, self.t_at ^ d, 0)
            if d:
                piece = self.swap(piece, 2 * d)
            came = lax.dynamic_update_slice(came, piece, (self.t_at ^ d, 0, 0))
        return came

    def gather_first(self, qkv, out, gateup, down, gains, count):
        rows = qkv.shape[0]
        low = jnp.bfloat16
        if self.planes == 4 and self.n > 1:
            digits = jnp.stack([count // 16, count % 16]).astype(low)
            ext = jnp.concatenate([gains.reshape(1, 2 * rows), jnp.zeros((15, 2 * rows), gains.dtype)])
            ext = lax.dynamic_update_slice(ext, digits[None], (1, 0))
            qkv_all, out_all, ext_all, *came, down_all = gather_first(
                qkv, out, gateup, down, ext, self.planes, self.n
            )
            ext_all = ext_all.reshape(self.wide * self.n, 16, 2 * rows)
            gain_full = ext_all[:, 0].reshape(-1, 2, rows).transpose(1, 0, 2).reshape(2, -1)
            digits = ext_all[:, 1, :2].astype(jnp.int32)
            return (
                qkv_all.reshape(self.wide * self.n * rows, -1),
                out_all,
                came,
                down_all.reshape(-1, down.shape[1]),
                gain_full,
                digits[:, 0] * 16 + digits[:, 1],
            )
        came = self.trade_columns(split_columns(gateup.astype(low), self.planes))
        cut = first_columns(came.shape[2] // 2)
        return (
            lax.all_gather(qkv.astype(low), MESH_AXES, axis=0, tiled=True),
            lax.all_gather(out.astype(low), MESH_AXES, axis=0, tiled=True),
            (came[:, :, :cut], came[:, :, cut:]),
            lax.all_gather(
                down.astype(low), MESH_AXES, axis=0, tiled=True, axis_index_groups=self.same_chip
            ),
            lax.all_gather(gains, MESH_AXES, axis=1, tiled=True),
            lax.all_gather(count, MESH_AXES),
        )


def dot32(a, b):
    return jnp.dot(a, b, preferred_element_type=jnp.float32)


def dot_low(a, b):
    return jnp.dot(a, b, preferred_element_type=jnp.float32).astype(jnp.bfloat16)


def together(arrays):
    return arrays[0] if len(arrays) == 1 else jnp.concatenate(arrays)


def split_columns(shard, planes):
    units = FF // planes
    found = []
    for t in range(planes):
        for low, high in unit_groups(units):
            for start in (t * units, FF + t * units):
                found.append(shard[:, start + low : start + high])
    return jnp.concatenate(found, axis=1).reshape(shard.shape[0], planes, 2 * units).transpose(1, 0, 2)


def join_columns(pieces):
    planes, _, cols = pieces.shape
    gates, uppers = [], []
    for t in range(planes):
        for low, high in unit_groups(cols // 2):
            gates.append(pieces[t, :, 2 * low : low + high])
            uppers.append(pieces[t, :, low + high : 2 * high])
    return jnp.concatenate(gates + uppers, axis=1)


def pick_live(mask, cap):
    flat = mask.reshape(-1)
    rows = flat.shape[0]
    at = jnp.arange(rows, dtype=jnp.int32)
    rank = jnp.sum(jnp.where(at[None, :] <= at[:, None], flat[None, :], 0), axis=1) - 1
    slot = jnp.arange(cap, dtype=jnp.int32)
    chosen = (rank[None, :] == slot[:, None]) & (flat[None, :] == 1)
    return chosen, slot < jnp.sum(flat)


def layer(links, cap, given):
    (
        tokens,
        active,
        cotangent,
        gain_full,
        counts,
        qkv_low,
        out_all,
        pieces,
        down_low,
    ) = given
    n, planes = links.n, links.planes
    seq_count, span_len, width = tokens.shape
    row_count = seq_count * span_len
    seq_len = n * span_len
    kv_width = KV_HEADS * HEAD_DIM
    ff_part = FF // planes
    shard_rows = pieces[0].shape[1]
    low = jnp.bfloat16


    gateup_first = links.gather_chip(pieces[0])

    def codes_of(block):
        mask = lax.dynamic_slice_in_dim(active, jnp.maximum(block, 0) * span_len, span_len, 1)
        chosen, live = pick_live(mask, cap)
        code = jnp.arange(seq_count, dtype=jnp.int32)[:, None] * seq_len + jnp.arange(span_len, dtype=jnp.int32)
        code = jnp.sum(jnp.where(chosen, code.reshape(1, -1), 0), axis=1) + block * span_len
        return chosen, live & (block >= 0), code

    chosen, live, own_code = codes_of(links.z_at)
    key_codes = []
    for r in range(n):
        _, there, code = codes_of(links.z_at - r)
        key_codes.append(jnp.where(there, code, seq_count * seq_len))
    key_code = jnp.concatenate(key_codes)[:, None]
    query_code = jnp.where(live, own_code, -1)[None]
    query_base = jnp.where(live, own_code // seq_len * seq_len, 0)[None]
    places = jnp.where(live, own_code % seq_len, 0).astype(jnp.float32)
    cosine_table, sine_table = rotary_tables(places)
    picker = chosen.astype(low)
    live_rows = live.astype(jnp.float32)[:, None]

    inputs = dot32(picker, tokens.reshape(row_count, width))
    down_grad = dot_low(picker, cotangent.reshape(row_count, width))
    upstream = down_grad.astype(jnp.float32)

    cosine = jnp.concatenate([cosine_table, cosine_table], axis=1)
    sine = jnp.concatenate([-sine_table, sine_table], axis=1)
    ids = 1 if cap < row_count else 3
    codes = (key_code, query_code, query_base)
    first = (inputs, gain_full[:1], cosine, sine, qkv_low, *codes, n, ids)
    if out_all.ndim == 2:
        out_low = out_all
        normed_low, inverse_one, query_low, attended_low, totals, kv_all = attend(*first)
        down_grad_blocks = links.gather_tokens(down_grad)
    else:
        normed_low, inverse_one, query_low, attended_low, totals, kv_all, out_all, *others = attend(
            *first, down_grad, out_all
        )
        down_grad_blocks = [down_grad, *others]
        out_low = out_all.reshape(width, width)
    pieces_last, attended_low = lax.optimization_barrier((pieces[1], attended_low))
    gateup_last = links.gather_chip(pieces_last)
    middle = inputs + live_rows * dot32(attended_low, out_low)
    normed_mid, inverse_two = norm_forward(middle, gain_full[1])
    blocks = links.gather_tokens(normed_mid.astype(low))
    lives = links.plane_counts(counts, cap)

    parts = [[k] for k in range(planes)] if planes != 4 else [[0], [1, 2], [3]]
    hidden_blocks, gateup_grad_blocks, back_parts, down_parts = [], [], [], []
    row_parts, grad_parts = [], []
    for part in parts:
        rows = together([blocks[k] for k in part])
        grads = together([down_grad_blocks[k] for k in part])
        row_parts.append(rows)
        grad_parts.append(grads)
        hidden, gateup_grad, back, down_part = mlp_block(
            rows, grads, lives[jnp.array(part)], gateup_first, gateup_last, down_low, cap
        )
        hidden_blocks.append(hidden)
        gateup_grad_blocks.append(gateup_grad)
        back_parts.append(back)
        down_parts.append(down_part)
    if planes == 4 and n > 1 and cap <= 384:
        grad_normed_mid, down_half, gateup_half = mid_back(
            back_parts, row_parts, gateup_grad_blocks, hidden_blocks, grad_parts, cap, planes, n, ids + 8
        )
    else:
        grad_normed_mid = links.scatter_tokens(back_parts, cap)
        term_down = dot_low(jnp.concatenate(hidden_blocks).T, jnp.concatenate(grad_parts))
        down_half = links.scatter_core(term_down.reshape(1, 2, ff_part // 2, width))[0]
        term_gateup = dot_low(jnp.concatenate(row_parts).T, jnp.concatenate(gateup_grad_blocks))
        gateup_half = links.scatter_core(term_gateup.reshape(planes, 2, n * shard_rows, 2 * ff_part))
    grad_pieces = lax.psum_scatter(gateup_half, "narrow", scatter_dimension=1, tiled=True)

    grad_middle = upstream + norm_backward(middle, inverse_two, gain_full[1], grad_normed_mid)
    branch_grad_low = grad_middle.astype(low)
    grad_attended_low = dot_low(branch_grad_low, out_low.T)
    back = (query_low, kv_all, grad_attended_low, totals, attended_low, *codes, cosine, sine, n, ids + 1)
    if planes == 4 and n > 1:
        grad_projected_low, out_sum, *came = attend_back(*back, branch_grad_low, down_parts, planes)
        down_proj = sum((part.astype(jnp.float32) for part in came), down_parts[0].astype(jnp.float32))
        down_half, grad_pieces, grad_projected_low = lax.optimization_barrier(
            (down_half, grad_pieces, grad_projected_low)
        )
        grad_qkv, grad_normed, grad_gateup, grad_out = qkv_back(
            normed_low, grad_projected_low, qkv_low, grad_pieces, out_sum, planes, n, ids + 4
        )
    else:
        grad_projected_low = attend_back(*back)[0]
        down_proj = links.scatter_tokens(down_parts, cap)
        grad_out = links.scatter_rows(dot_low(attended_low.T, branch_grad_low))
        grad_qkv = links.scatter_rows(dot_low(normed_low.T, grad_projected_low)).astype(jnp.float32)
        grad_normed = dot32(grad_projected_low, qkv_low.T)
        grad_gateup = join_columns(links.trade_columns(grad_pieces)).astype(jnp.float32)
    grad_tokens = (
        grad_middle + norm_backward(inputs, inverse_one, gain_full[0], grad_normed)
    ).astype(low)

    grad_down = lax.psum_scatter(down_half, "narrow", scatter_dimension=0, tiled=True)
    layer_out = (middle + down_proj).astype(low)

    def spread(packed, skipped):
        back = lax.dot_general(
            picker, packed, (((0,), (0,)), ((), ())), preferred_element_type=jnp.float32
        ).astype(low)
        mask = lax.dynamic_slice_in_dim(active, links.z_at * span_len, span_len, 1)
        return jnp.where(mask[:, :, None] == 1, back.reshape(skipped.shape), skipped)

    layer_out, grad_tokens = spread(layer_out, tokens), spread(grad_tokens, cotangent)
    return layer_out, grad_tokens, grad_qkv, grad_out, grad_gateup, grad_down


def on_device(
    tokens,
    active,
    cotangent,
    gain_rows,
    w_qkv,
    w_out,
    w_gateup,
    w_down,
    moment_gains,
    moment_qkv,
    moment_out,
    moment_gateup,
    moment_down,
    average_gains,
    average_qkv,
    average_out,
    average_gateup,
    average_down,
):
    links = Links()
    seq_count, span_len, _ = tokens.shape
    row_count = seq_count * span_len
    low = jnp.bfloat16

    gains_low = gain_rows.astype(low)
    own_mask = lax.dynamic_slice_in_dim(active, links.z_at * span_len, span_len, 1)
    qkv_low, out_all, pieces, down_low, gain_full, counts = links.gather_first(
        w_qkv, w_out, w_gateup, w_down, gains_low, jnp.sum(own_mask)
    )
    gain_full = gain_full.astype(jnp.float32)
    given = (tokens, active, cotangent, gain_full, counts, qkv_low, out_all, pieces, down_low)
    few = -(-3 * row_count // 4 // 128) * 128
    if few < row_count:
        found = lax.cond(
            jnp.max(counts) <= few,
            lambda *g: layer(links, few, g),
            lambda *g: layer(links, row_count, g),
            *given,
        )
    else:
        found = layer(links, row_count, given)
    layer_out, grad_tokens, grad_qkv, grad_out, grad_gateup, grad_down = found
    grad_qkv, grad_out, grad_gateup, grad_down = (
        g.astype(jnp.float32) for g in (grad_qkv, grad_out, grad_gateup, grad_down)
    )

    def gain_grad(shard, gradient, row):
        return jnp.sum(shard.astype(low).astype(jnp.float32) * gradient, axis=1) / gains_low[row].astype(jnp.float32)

    grad_gains = jnp.stack([gain_grad(w_qkv, grad_qkv, 0), gain_grad(w_gateup, grad_gateup, 1)])
    state_gains = advance_state(gain_rows, moment_gains, average_gains, grad_gains)
    state_qkv = advance_state(w_qkv, moment_qkv, average_qkv, grad_qkv)
    state_out = advance_state(w_out, moment_out, average_out, grad_out)
    state_gateup = advance_state(w_gateup, moment_gateup, average_gateup, grad_gateup)
    state_down = advance_state(w_down, moment_down, average_down, grad_down)
    return (
        layer_out,
        grad_tokens,
        grad_gains,
        grad_qkv,
        grad_out,
        grad_gateup,
        grad_down,
        state_gains[0],
        state_qkv[0],
        state_out[0],
        state_gateup[0],
        state_down[0],
        state_gains[1],
        state_qkv[1],
        state_out[1],
        state_gateup[1],
        state_down[1],
        state_gains[2],
        state_qkv[2],
        state_out[2],
        state_gateup[2],
        state_down[2],
    )


def solution(mesh):
    in_specs = (
        P("wide", "narrow", None),
        P("wide", None),
        P("wide", "narrow", None),
        P(None, ("wide", "narrow")),
        P(("wide", "narrow"), None),
        P(("wide", "narrow"), None),
        P(("wide", "narrow"), None),
        P(("wide", "narrow"), None),
        P(None, ("wide", "narrow")),
        P(("wide", "narrow"), None),
        P(("wide", "narrow"), None),
        P(("wide", "narrow"), None),
        P(("wide", "narrow"), None),
        P(None, ("wide", "narrow")),
        P(("wide", "narrow"), None),
        P(("wide", "narrow"), None),
        P(("wide", "narrow"), None),
        P(("wide", "narrow"), None),
    )
    out_specs = (
        P("wide", "narrow", None),
        P("wide", "narrow", None),
        P(None, ("wide", "narrow")),
        P(("wide", "narrow"), None),
        P(("wide", "narrow"), None),
        P(("wide", "narrow"), None),
        P(("wide", "narrow"), None),
        P(None, ("wide", "narrow")),
        P(("wide", "narrow"), None),
        P(("wide", "narrow"), None),
        P(("wide", "narrow"), None),
        P(("wide", "narrow"), None),
        P(None, ("wide", "narrow")),
        P(("wide", "narrow"), None),
        P(("wide", "narrow"), None),
        P(("wide", "narrow"), None),
        P(("wide", "narrow"), None),
        P(None, ("wide", "narrow")),
        P(("wide", "narrow"), None),
        P(("wide", "narrow"), None),
        P(("wide", "narrow"), None),
        P(("wide", "narrow"), None),
    )
    return jax.shard_map(
        on_device, mesh=mesh, in_specs=in_specs, out_specs=out_specs, check_vma=False
    )
```
